32 devices in a mesh: row: 8 (over y, x, core), col: 4 (over z).
Axes of the slice: x: 2, y: 2, z: 4, core: 2. Of those that a mesh axis runs over, the one named last changes fastest.
Arguments:
- saved_factor: float32 [4096, 4096], P('row', 'col'), may hold values from -1 to 3, as said below
- cotangent: float32 [4096, 4096], P('row', 'col'), may hold values from -6 to 6
Outputs:
- adjoint: float32 [4096, 4096], P('row', 'col')
The draws below stay inside these ranges and needn't reach their ends.
Inputs may be any that keep to these rules, and one draw needn't show every extreme that they name: `saved_factor`: entry (i, j) is zero where j > i + 4096 - 3 * 512, and 1 or more where j = i + 4096 - 3 * 512.
All inputs are finite; a program needn't handle non-finite values.
Results may differ from the reference program's by a relative error of at most 0.0001.
Values sent between devices are 32-bit elements; how exact they have to be, the bound alone decides.
No kernel may reach another device: no remote copies, remote signals or barrier semaphores. Data moves between devices by JAX's collectives and lax.ppermute only.
A program may use at most 128 MiB of HBM per device.

```python
import math
import jax
import jax.numpy as jnp
from jax import lax

NB = 512
NP = 3
ORDER = 4096


def draw_saved_factor(key, part):
    first_key = jax.random.fold_in(key, 11)
    second_key = jax.random.fold_in(key, 23)
    spread = jax.random.normal(first_key, (ORDER, ORDER), jnp.float32)
    diagonal = jax.random.uniform(second_key, (ORDER,), jnp.float32, 1.0, 2.0)
    gap = ORDER - NP * NB
    row_pos = jnp.arange(ORDER, dtype=jnp.int32)[:, None]
    col_pos = jnp.arange(ORDER, dtype=jnp.int32)[None, :]
    lower_part = jnp.where(col_pos < row_pos + gap, spread, 0.0) * (0.3 / math.sqrt(NB))
    on_diag = jnp.where(col_pos == row_pos + gap, diagonal[:, None], 0.0)
    return (lower_part + on_diag).astype(jnp.float32)


def block_levels(own_key, shape, cuts, smallest, top_value):
    def one(position, blocks):
        draws = jax.random.uniform(jax.random.fold_in(jax.random.fold_in(own_key, 6), position), (blocks,), jnp.float32, smallest / len(cuts), top_value / len(cuts))
        return jnp.repeat(jnp.exp(draws), shape[position] // blocks).reshape((-1,) + (1,) * (len(shape) - position - 1))

    gain = one(*cuts[0])
    for cut in cuts[1:]:
        gain = gain * one(*cut)
    return gain


def noise(key, shape, scale, bound, pieces=(), kind=jnp.bfloat16):
    values = scale * jax.random.normal(key, shape, jnp.float32)
    if pieces:
        values = values * block_levels(key, shape, pieces, -0.22, 0.18)
    return jnp.clip(values, -bound, bound).astype(kind)


def setup_inputs(seed: int = 0) -> dict:
    keys = jax.random.split(jax.random.key(seed), 3)
    return {
        "saved_factor": draw_saved_factor(jax.random.fold_in(keys[2], 71), 0),
        "cotangent": noise(keys[1], (ORDER, ORDER), 1.0, 6.0, ((0, 8), (1, 4)), jnp.float32),
    }


precise = lax.Precision.HIGHEST

def matmul(left_side, right_side):
    return jnp.dot(left_side.astype(jnp.float32), right_side.astype(jnp.float32), precision=precise, preferred_element_type=jnp.float32)

def inner_rows(left_side, right_side):
    return lax.dot_general(left_side.astype(jnp.float32), right_side.astype(jnp.float32), (((0,), (0,)), ((), ())), precision=precise, preferred_element_type=jnp.float32)

def lower_half(matrix):
    return jnp.tril(matrix) - 0.5 * jnp.diag(jnp.diag(matrix))

def reference(saved_factor, cotangent):
    full_order = saved_factor.shape[0]
    identity = jnp.eye(NB, dtype=saved_factor.dtype)
    running = cotangent
    for number in range(NP):
        row_start = (NP - 1 - number) * NB
        row_end = row_start + NB
        col_start = full_order - (number + 1) * NB
        col_end = col_start + NB
        diag_factor = saved_factor[row_start:row_end, col_start:col_end]
        inverse = lax.linalg.triangular_solve(diag_factor, identity, left_side=True, lower=True)
        solved = matmul(running[row_end:, col_start:col_end], inverse)
        running = running.at[row_end:, col_start:col_end].set(solved)
        running = running.at[row_end:, :col_start].add(-matmul(solved, saved_factor[row_start:row_end, :col_start]))
        diag_grad = jnp.tril(running[row_start:row_end, col_start:col_end]) - jnp.tril(inner_rows(solved, saved_factor[row_end:, col_start:col_end]))
        diag_adj = lower_half(matmul(matmul(inverse.T, lower_half(matmul(diag_factor.T, diag_grad))), inverse))
        running = running.at[row_start:row_end, col_start:col_end].set(diag_adj)
        symmetric = diag_adj + diag_adj.T
        running = running.at[row_start:row_end, :col_start].add(-(inner_rows(solved, saved_factor[row_end:, :col_start]) + matmul(symmetric, saved_factor[row_start:row_end, :col_start])))
    return running
```

```python
import functools

import jax
import jax.numpy as jnp
from jax import lax
from jax.experimental import pallas as pl
from jax.experimental.pallas import tpu as pltpu
from jax.sharding import PartitionSpec as P

NB = 512
NP = 3
HALF = NB // 2
BASE = 16
TILE = 128

fine = lax.Precision.HIGHEST
good = lax.Precision.HIGH


def mm(left, right, precision=good):
    return jnp.dot(left, right, precision=precision, preferred_element_type=jnp.float32)


def mm_t(left, right, precision=good):
    return lax.dot_general(
        left, right, (((0,), (0,)), ((), ())), precision=precision, preferred_element_type=jnp.float32
    )


def lower_half(matrix):
    return jnp.tril(matrix) - 0.5 * jnp.diag(jnp.diag(matrix))


def fine_dot(left, right):
    return jnp.dot(left, right, precision=fine, preferred_element_type=jnp.float32)


def inverse_kernel(d_ref, x_ref, tiles, base):
    for t in range(NB // TILE):
        span = pl.ds(t * TILE, TILE)
        tiles[span, :] = d_ref[span, span]
    blocks = NB // BASE
    lane = lax.broadcasted_iota(jnp.int32, (blocks, TILE), 1)
    first = lax.rem(lax.broadcasted_iota(jnp.int32, (blocks, TILE), 0), TILE // BASE) * BASE
    place = lane - first
    solved = []
    for i in range(BASE):
        row = tiles[pl.ds(i, blocks, stride=BASE), :]
        acc = jnp.where(place == i, 1.0, 0.0)
        for k in range(i):
            factor = jnp.sum(jnp.where(place == k, row, 0.0), axis=1, keepdims=True)
            acc = acc - factor * solved[k]
        pivot = jnp.sum(jnp.where(place == i, row, 0.0), axis=1, keepdims=True)
        solved.append(acc / pivot)
        base[pl.ds(i, blocks, stride=BASE), :] = solved[i]
    rows = lax.broadcasted_iota(jnp.int32, (HALF, HALF), 0)
    cols = lax.broadcasted_iota(jnp.int32, (HALF, HALF), 1)
    empty = jnp.zeros((TILE, TILE), jnp.float32)
    corners = []
    for t in range(2):
        top = jnp.concatenate([base[pl.ds(t * HALF, TILE), :], empty], axis=1)
        bottom = jnp.concatenate([empty, base[pl.ds(t * HALF + TILE, TILE), :]], axis=1)
        corners.append(jnp.concatenate([top, bottom], axis=0))
    size = BASE
    while size < HALF:
        below = (rows // (2 * size) == cols // (2 * size)) & (rows // size != cols // size) & (rows > cols)
        for t in range(2):
            span = pl.ds(t * HALF, HALF)
            part = jnp.where(below, d_ref[span, span], 0.0)
            corners[t] = corners[t] - fine_dot(fine_dot(corners[t], part), corners[t])
        size *= 2
    top, bottom = pl.ds(0, HALF), pl.ds(HALF, HALF)
    x_ref[top, top] = corners[0]
    x_ref[top, bottom] = jnp.zeros((HALF, HALF), jnp.float32)
    x_ref[bottom, top] = -fine_dot(fine_dot(corners[1], d_ref[bottom, top]), corners[0])
    x_ref[bottom, bottom] = corners[1]


def invert(matrix):
    return pl.pallas_call(
        inverse_kernel,
        out_shape=jax.ShapeDtypeStruct((NB, NB), jnp.float32),
        in_specs=[pl.BlockSpec(memory_space=pltpu.VMEM)],
        out_specs=pl.BlockSpec(memory_space=pltpu.VMEM),
        scratch_shapes=[pltpu.VMEM((NB, TILE), jnp.float32), pltpu.VMEM((NB, TILE), jnp.float32)],
        compiler_params=pltpu.CompilerParams(vmem_limit_bytes=32 * 1024 * 1024),
        cost_estimate=pl.CostEstimate(flops=20 * 2 * HALF**3 * 6, bytes_accessed=2 * 4 * NB * NB, transcendentals=0),
        name="invert",
    )(matrix)


class Grid:
    def __init__(self):
        self.row_count = lax.axis_size("row")
        self.col_count = lax.axis_size("col")
        self.row = lax.axis_index("row")
        self.col = lax.axis_index("col")
        self.odd = self.row % 2 == 1
        self.paired = self.row_count == 8

    def send(self, value, pairs):
        count = self.col_count
        flat = [(a[0] * count + a[1], b[0] * count + b[1]) for a, b in pairs]
        return lax.ppermute(value, ("row", "col"), flat)

    def within(self, value, moves, planes):
        return self.send(value, [((a, c), (b, c)) for c in planes for a, b in moves])

    def down(self, value, rows, planes):
        return self.send(value, [((r, c), (r, c - 1)) for c in planes for r in rows])

    def is_row(self, *rows):
        return functools.reduce(jnp.logical_or, [self.row == r for r in rows])


def spread(grid, carry, root):
    planes = range(grid.col_count)
    if not grid.paired:
        bit = 1
        while bit < grid.row_count:
            carry = carry + grid.within(carry, [(root ^ m, root ^ m ^ bit) for m in range(bit)], planes)
            bit *= 2
        return carry
    base = root & ~1
    for moves in (((0, 4), (1, 3)), ((4, 6), (3, 7), (1, 5), (0, 2))):
        carry = carry + grid.within(carry, [(a ^ base, b ^ base) for a, b in moves], planes)
    other = grid.within(carry, [(r, r ^ 1) for r in range(grid.row_count)], planes)
    upper = jnp.where(grid.odd, other, carry)
    lower = jnp.where(grid.odd, carry, other)
    return jnp.concatenate([upper, lower], axis=0)


def gather_sum(grid, part, roots):
    if not roots:
        return jnp.zeros_like(part)
    chosen = functools.reduce(
        jnp.logical_or, [(grid.col == c) & (grid.row == root) for c, root in roots.items()]
    )

    def pairs(moves):
        return [((a ^ (root & ~1), c), (b ^ (root & ~1), c)) for c, root in roots.items() for a, b in moves]

    if not grid.paired:
        bit = grid.row_count // 2
        while bit:
            part = part + grid.send(
                part,
                [((root ^ m ^ bit, c), (root ^ m, c)) for c, root in roots.items() for m in range(bit)],
            )
            bit //= 2
        return jnp.where(chosen, part, 0.0)
    half = part.shape[0] // 2
    upper, lower = part[:half], part[half:]
    swapped = grid.send(
        jnp.where(grid.odd, upper, lower),
        [((r, c), (r ^ 1, c)) for c in roots for r in range(grid.row_count)],
    )
    carry = jnp.where(grid.odd, lower, upper) + swapped
    carry = carry + grid.send(carry, pairs(((6, 4), (7, 3), (5, 1), (2, 0))))
    carry = carry + grid.send(carry, pairs(((4, 0), (3, 1))))
    other = grid.send(carry, [((root ^ 1, c), (root, c)) for c, root in roots.items()])
    carry = jnp.where(chosen, carry, 0.0)
    return jnp.concatenate(
        [jnp.where(grid.odd, other, carry), jnp.where(grid.odd, carry, other)], axis=0
    )


def adjoint_of(diag_factor, diag_cot, inverse):
    inner = lower_half(mm_t(diag_factor, jnp.tril(diag_cot)))
    return lower_half(mm(mm_t(inverse, inner), inverse))


def shards(saved_factor, cotangent):
    grid = Grid()
    row, col = grid.row, grid.col
    last, near = grid.col_count - 1, grid.col_count - 2
    planes = list(range(grid.col_count))
    solved_rows = range(NP, grid.row_count)
    below = row >= NP

    if grid.paired:
        mine = jnp.where(grid.odd, saved_factor[HALF:], saved_factor[:HALF])
        given = jnp.where(grid.odd, saved_factor[:HALF], saved_factor[HALF:])
        mate = grid.within(given, [(r, r ^ 1) for r in range(NP)], planes)
        seeds = [
            jnp.where(row == root, mine, jnp.where(row == root ^ 1, mate, 0.0)) for root in (2, 1, 0)
        ]
    else:
        seeds = [jnp.where(row == root, saved_factor, 0.0) for root in (2, 1, 0)]
    strip0_right = spread(grid, seeds[0][:, NB:], 2)
    strip0_left = spread(grid, seeds[0][:, :NB], 2)
    strip1_left = spread(grid, seeds[1][:, :NB], 1)
    strip1_right = spread(grid, seeds[1][:, NB:], 1)
    strip2 = spread(grid, seeds[2], 0)
    strip2_right = strip2[:, NB:]

    first_inverse = invert(strip0_right)
    second_diag = jnp.where(col == last, strip1_left, strip2_right)
    second_inverse = invert(second_diag)

    solved0 = mm(cotangent[:, NB:], first_inverse)
    solved1 = mm(cotangent[:, :NB] - mm(solved0, strip0_left), second_inverse)
    starts = {1: solved0, 2: solved1}

    steps = last + NP
    held = {}
    running = cotangent
    came = None
    state = {}
    for step in range(1, steps + 1):
        if step in starts:
            now = jnp.where(below & (col == last), starts[step], 0.0)
            if came is not None:
                now = now + came
        elif step == 4:
            solved2 = mm(
                cotangent[:, NB:] - mm(held[2], strip0_right) - mm(held[3], strip1_right),
                second_inverse,
            )
            now = jnp.where(below & (col == near), solved2, 0.0)
            if came is not None:
                now = now + came
        else:
            now = came
        held[step] = now
        which = {c: step - 1 - (last - c) for c in planes}
        roots = {
            c: 2 - k for c, k in which.items() if 0 <= k < NP and not (c == last and k == 2)
        }
        onward = [c for c in roots if c > 0]
        came = grid.down(now, solved_rows, onward) if onward else jnp.zeros_like(now)
        running = running - gather_sum(grid, mm_t(now, saved_factor), roots)
        if step == 1:
            adj0 = adjoint_of(strip0_right, running[:, NB:], first_inverse)
            sym0 = adj0 + adj0.T
            cross = mm(running[:, :NB] - mm(sym0, strip0_left), second_inverse)
            crossed = grid.send(cross, [((2, last), (1, last))])
        if step == 2:
            adj1 = adjoint_of(
                second_diag, running[:, :NB] - mm_t(crossed, strip0_left), second_inverse
            )
            sym1 = adj1 + adj1.T

    blocks = []
    for k in range(NP):
        block = held[k + 1]
        for hop in range(1, grid.col_count):
            if k + 1 + hop in held:
                block = jnp.where(col == last - hop, held[k + 1 + hop], block)
        blocks.append(block)

    hop0 = grid.send(sym0, [((2, last), (2, near))])
    hop1 = grid.send(cross, [((2, last), (2, near))])
    hop2 = grid.send(crossed, [((1, last), (1, near))])
    hop3 = grid.send(sym1, [((1, last), (1, near))])
    left0 = hop0 + hop2.T
    left1 = hop1 + hop3
    cross2 = mm(
        running[:, NB:] - mm(left0, strip0_right) - mm(left1, strip1_right), second_inverse
    )
    from2 = grid.send(cross2, [((2, near), (0, near))])
    from1 = grid.send(cross2, [((1, near), (0, near))])
    adj2 = adjoint_of(
        strip2_right,
        running[:, NB:] - mm_t(from2, strip0_right) - mm_t(from1, strip1_right),
        second_inverse,
    )
    sym2 = adj2 + adj2.T
    if near > 0:
        pair = jnp.stack([hop0 + hop2, hop1 + hop3])
        total = pair
        late = jnp.where(row == 0, from2, cross2)
        late_total = late
        square = sym2
        square_total = sym2
        for c in range(near, 0, -1):
            pair = grid.down(pair, (1, 2), [c])
            total = total + pair
            late = grid.down(late, (0, 1, 2), [c])
            late_total = jnp.where(col == near, late_total, 0.0) + late if c == near else late_total + late
            square = grid.down(square, (0,), [c])
            square_total = (
                jnp.where(col == near, square_total, 0.0) + square if c == near else square_total + square
            )
        mate = grid.within(late_total, [(1, 0)], range(near))
        other = jnp.where(col == near, from1, mate)
    else:
        total = jnp.stack([hop0 + hop2, hop1 + hop3])
        late_total = jnp.where(row == 0, from2, cross2)
        square_total = sym2
        other = from1
    blocks[0] = jnp.where(
        below, blocks[0], jnp.where(row == 2, total[0], jnp.where(row == 1, total[0], late_total).T)
    )
    blocks[1] = jnp.where(below, blocks[1], jnp.where(row == 0, other.T, total[1]))
    blocks[2] = jnp.where(below, blocks[2], jnp.where(row == 0, square_total, late_total))

    result = running
    strips = (
        jnp.concatenate([strip0_left, strip0_right], axis=1),
        jnp.concatenate([strip1_left, strip1_right], axis=1),
        strip2,
    )
    for block, strip in zip(blocks, strips):
        result = result - mm(block, strip)

    right = jnp.where(
        col == last,
        jnp.where(below, held[1], jnp.where(row == 2, adj0, cotangent[:, NB:])),
        jnp.where(
            col == near,
            jnp.where(row == 0, adj2, blocks[2]),
            result[:, NB:],
        ),
    )
    left = jnp.where(
        col == last,
        jnp.where(
            below,
            held[2],
            jnp.where(row == 2, cross, jnp.where(row == 1, adj1, cotangent[:, :NB])),
        ),
        result[:, :NB],
    )
    return jnp.concatenate([left, right], axis=1)


def solution(mesh):
    placed = (P("row", "col"), P("row", "col"))
    return jax.shard_map(
        shards, mesh=mesh, in_specs=placed, out_specs=P("row", "col"), check_vma=False
    )
```

```python
import functools

import jax
import jax.numpy as jnp
from jax import lax
from jax.experimental import pallas as pl
from jax.experimental.pallas import tpu as pltpu
from jax.sharding import PartitionSpec as P

NB = 512
NP = 3
HALF = NB // 2
BASE = 16
TILE = 128

fine = lax.Precision.HIGHEST
good = lax.Precision.HIGH


def mm(left, right, precision=good):
    return jnp.dot(left, right, precision=precision, preferred_element_type=jnp.float32)


def mm_t(left, right, precision=good):
    return lax.dot_general(
        left, right, (((0,), (0,)), ((), ())), precision=precision, preferred_element_type=jnp.float32
    )


def lower_half(matrix):
    return jnp.tril(matrix) - 0.5 * jnp.diag(jnp.diag(matrix))


def fine_dot(left, right):
    return jnp.dot(left, right, precision=fine, preferred_element_type=jnp.float32)


def inverse_kernel(d_ref, x_ref, tiles, base):
    for t in range(NB // TILE):
        span = pl.ds(t * TILE, TILE)
        tiles[span, :] = d_ref[span, span]
    blocks = NB // BASE
    lane = lax.broadcasted_iota(jnp.int32, (blocks, TILE), 1)
    first = lax.rem(lax.broadcasted_iota(jnp.int32, (blocks, TILE), 0), TILE // BASE) * BASE
    place = lane - first
    solved = []
    for i in range(BASE):
        row = tiles[pl.ds(i, blocks, stride=BASE), :]
        acc = jnp.where(place == i, 1.0, 0.0)
        for k in range(i):
            factor = jnp.sum(jnp.where(place == k, row, 0.0), axis=1, keepdims=True)
            acc = acc - factor * solved[k]
        pivot = jnp.sum(jnp.where(place == i, row, 0.0), axis=1, keepdims=True)
        solved.append(acc / pivot)
        base[pl.ds(i, blocks, stride=BASE), :] = solved[i]
    rows = lax.broadcasted_iota(jnp.int32, (HALF, HALF), 0)
    cols = lax.broadcasted_iota(jnp.int32, (HALF, HALF), 1)
    empty = jnp.zeros((TILE, TILE), jnp.float32)
    corners = []
    for t in range(2):
        top = jnp.concatenate([base[pl.ds(t * HALF, TILE), :], empty], axis=1)
        bottom = jnp.concatenate([empty, base[pl.ds(t * HALF + TILE, TILE), :]], axis=1)
        corners.append(jnp.concatenate([top, bottom], axis=0))
    size = BASE
    while size < HALF:
        below = (rows // (2 * size) == cols // (2 * size)) & (rows // size != cols // size) & (rows > cols)
        for t in range(2):
            span = pl.ds(t * HALF, HALF)
            part = jnp.where(below, d_ref[span, span], 0.0)
            corners[t] = corners[t] - fine_dot(fine_dot(corners[t], part), corners[t])
        size *= 2
    top, bottom = pl.ds(0, HALF), pl.ds(HALF, HALF)
    x_ref[top, top] = corners[0]
    x_ref[top, bottom] = jnp.zeros((HALF, HALF), jnp.float32)
    x_ref[bottom, top] = -fine_dot(fine_dot(corners[1], d_ref[bottom, top]), corners[0])
    x_ref[bottom, bottom] = corners[1]


def invert(matrix):
    return pl.pallas_call(
        inverse_kernel,
        out_shape=jax.ShapeDtypeStruct((NB, NB), jnp.float32),
        in_specs=[pl.BlockSpec(memory_space=pltpu.VMEM)],
        out_specs=pl.BlockSpec(memory_space=pltpu.VMEM),
        scratch_shapes=[pltpu.VMEM((NB, TILE), jnp.float32), pltpu.VMEM((NB, TILE), jnp.float32)],
        compiler_params=pltpu.CompilerParams(vmem_limit_bytes=32 * 1024 * 1024),
        cost_estimate=pl.CostEstimate(flops=20 * 2 * HALF**3 * 6, bytes_accessed=2 * 4 * NB * NB, transcendentals=0),
        name="invert",
    )(matrix)


class Grid:
    def __init__(self):
        self.row_count = lax.axis_size("row")
        self.col_count = lax.axis_size("col")
        self.row = lax.axis_index("row")
        self.col = lax.axis_index("col")
        self.odd = self.row % 2 == 1
        self.paired = self.row_count == 8

    def send(self, value, pairs):
        count = self.col_count
        flat = [(a[0] * count + a[1], b[0] * count + b[1]) for a, b in pairs]
        return lax.ppermute(value, ("row", "col"), flat)

    def within(self, value, moves, planes):
        return self.send(value, [((a, c), (b, c)) for c in planes for a, b in moves])

    def down(self, value, rows, planes):
        return self.send(value, [((r, c), (r, c - 1)) for c in planes for r in rows])

    def is_row(self, *rows):
        return functools.reduce(jnp.logical_or, [self.row == r for r in rows])


def spread(grid, carry, root):
    planes = range(grid.col_count)
    if not grid.paired:
        bit = 1
        while bit < grid.row_count:
            carry = carry + grid.within(carry, [(root ^ m, root ^ m ^ bit) for m in range(bit)], planes)
            bit *= 2
        return carry
    base = root & ~1
    for moves in (((0, 4), (1, 3)), ((4, 6), (3, 7), (1, 5), (0, 2))):
        carry = carry + grid.within(carry, [(a ^ base, b ^ base) for a, b in moves], planes)
    other = grid.within(carry, [(r, r ^ 1) for r in range(grid.row_count)], planes)
    upper = jnp.where(grid.odd, other, carry)
    lower = jnp.where(grid.odd, carry, other)
    return jnp.concatenate([upper, lower], axis=0)


def gather_sum(grid, part, roots):
    if not roots:
        return jnp.zeros_like(part)
    chosen = functools.reduce(
        jnp.logical_or, [(grid.col == c) & (grid.row == root) for c, root in roots.items()]
    )

    def pairs(moves):
        return [((a ^ (root & ~1), c), (b ^ (root & ~1), c)) for c, root in roots.items() for a, b in moves]

    if not grid.paired:
        bit = grid.row_count // 2
        while bit:
            part = part + grid.send(
                part,
                [((root ^ m ^ bit, c), (root ^ m, c)) for c, root in roots.items() for m in range(bit)],
            )
            bit //= 2
        return jnp.where(chosen, part, 0.0)
    half = part.shape[0] // 2
    upper, lower = part[:half], part[half:]
    swapped = grid.send(
        jnp.where(grid.odd, upper, lower),
        [((r, c), (r ^ 1, c)) for c in roots for r in range(grid.row_count)],
    )
    carry = jnp.where(grid.odd, lower, upper) + swapped
    carry = carry + grid.send(carry, pairs(((6, 4), (7, 3), (5, 1), (2, 0))))
    carry = carry + grid.send(carry, pairs(((4, 0), (3, 1))))
    other = grid.send(carry, [((root ^ 1, c), (root, c)) for c, root in roots.items()])
    carry = jnp.where(chosen, carry, 0.0)
    return jnp.concatenate(
        [jnp.where(grid.odd, other, carry), jnp.where(grid.odd, carry, other)], axis=0
    )


def adjoint_of(diag_factor, diag_cot, inverse):
    inner = lower_half(mm_t(diag_factor, jnp.tril(diag_cot)))
    return lower_half(mm(mm_t(inverse, inner), inverse))


def general(grid, saved_factor, cotangent):
    row, col = grid.row, grid.col
    last, near = grid.col_count - 1, grid.col_count - 2
    planes = list(range(grid.col_count))
    solved_rows = range(NP, grid.row_count)
    below = row >= NP

    if grid.paired:
        mine = jnp.where(grid.odd, saved_factor[HALF:], saved_factor[:HALF])
        given = jnp.where(grid.odd, saved_factor[:HALF], saved_factor[HALF:])
        mate = grid.within(given, [(r, r ^ 1) for r in range(NP)], planes)
        seeds = [
            jnp.where(row == root, mine, jnp.where(row == root ^ 1, mate, 0.0)) for root in (2, 1, 0)
        ]
    else:
        seeds = [jnp.where(row == root, saved_factor, 0.0) for root in (2, 1, 0)]
    strip0_right = spread(grid, seeds[0][:, NB:], 2)
    strip0_left = spread(grid, seeds[0][:, :NB], 2)
    strip1_left = spread(grid, seeds[1][:, :NB], 1)
    strip1_right = spread(grid, seeds[1][:, NB:], 1)
    strip2 = spread(grid, seeds[2], 0)
    strip2_right = strip2[:, NB:]

    first_inverse = invert(strip0_right)
    second_diag = jnp.where(col == last, strip1_left, strip2_right)
    second_inverse = invert(second_diag)

    solved0 = mm(cotangent[:, NB:], first_inverse)
    solved1 = mm(cotangent[:, :NB] - mm(solved0, strip0_left), second_inverse)
    starts = {1: solved0, 2: solved1}

    steps = last + NP
    held = {}
    running = cotangent
    came = None
    state = {}
    for step in range(1, steps + 1):
        if step in starts:
            now = jnp.where(below & (col == last), starts[step], 0.0)
            if came is not None:
                now = now + came
        elif step == 4:
            solved2 = mm(
                cotangent[:, NB:] - mm(held[2], strip0_right) - mm(held[3], strip1_right),
                second_inverse,
            )
            now = jnp.where(below & (col == near), solved2, 0.0)
            if came is not None:
                now = now + came
        else:
            now = came
        held[step] = now
        which = {c: step - 1 - (last - c) for c in planes}
        roots = {
            c: 2 - k for c, k in which.items() if 0 <= k < NP and not (c == last and k == 2)
        }
        onward = [c for c in roots if c > 0]
        came = grid.down(now, solved_rows, onward) if onward else jnp.zeros_like(now)
        running = running - gather_sum(grid, mm_t(now, saved_factor), roots)
        if step == 1:
            adj0 = adjoint_of(strip0_right, running[:, NB:], first_inverse)
            sym0 = adj0 + adj0.T
            cross = mm(running[:, :NB] - mm(sym0, strip0_left), second_inverse)
            crossed = grid.send(cross, [((2, last), (1, last))])
        if step == 2:
            adj1 = adjoint_of(
                second_diag, running[:, :NB] - mm_t(crossed, strip0_left), second_inverse
            )
            sym1 = adj1 + adj1.T

    blocks = []
    for k in range(NP):
        block = held[k + 1]
        for hop in range(1, grid.col_count):
            if k + 1 + hop in held:
                block = jnp.where(col == last - hop, held[k + 1 + hop], block)
        blocks.append(block)

    hop0 = grid.send(sym0, [((2, last), (2, near))])
    hop1 = grid.send(cross, [((2, last), (2, near))])
    hop2 = grid.send(crossed, [((1, last), (1, near))])
    hop3 = grid.send(sym1, [((1, last), (1, near))])
    left0 = hop0 + hop2.T
    left1 = hop1 + hop3
    cross2 = mm(
        running[:, NB:] - mm(left0, strip0_right) - mm(left1, strip1_right), second_inverse
    )
    from2 = grid.send(cross2, [((2, near), (0, near))])
    from1 = grid.send(cross2, [((1, near), (0, near))])
    adj2 = adjoint_of(
        strip2_right,
        running[:, NB:] - mm_t(from2, strip0_right) - mm_t(from1, strip1_right),
        second_inverse,
    )
    sym2 = adj2 + adj2.T
    if near > 0:
        pair = jnp.stack([hop0 + hop2, hop1 + hop3])
        total = pair
        late = jnp.where(row == 0, from2, cross2)
        late_total = late
        square = sym2
        square_total = sym2
        for c in range(near, 0, -1):
            pair = grid.down(pair, (1, 2), [c])
            total = total + pair
            late = grid.down(late, (0, 1, 2), [c])
            late_total = jnp.where(col == near, late_total, 0.0) + late if c == near else late_total + late
            square = grid.down(square, (0,), [c])
            square_total = (
                jnp.where(col == near, square_total, 0.0) + square if c == near else square_total + square
            )
        mate = grid.within(late_total, [(1, 0)], range(near))
        other = jnp.where(col == near, from1, mate)
    else:
        total = jnp.stack([hop0 + hop2, hop1 + hop3])
        late_total = jnp.where(row == 0, from2, cross2)
        square_total = sym2
        other = from1
    blocks[0] = jnp.where(
        below, blocks[0], jnp.where(row == 2, total[0], jnp.where(row == 1, total[0], late_total).T)
    )
    blocks[1] = jnp.where(below, blocks[1], jnp.where(row == 0, other.T, total[1]))
    blocks[2] = jnp.where(below, blocks[2], jnp.where(row == 0, square_total, late_total))

    result = running
    strips = (
        jnp.concatenate([strip0_left, strip0_right], axis=1),
        jnp.concatenate([strip1_left, strip1_right], axis=1),
        strip2,
    )
    for block, strip in zip(blocks, strips):
        result = result - mm(block, strip)

    right = jnp.where(
        col == last,
        jnp.where(below, held[1], jnp.where(row == 2, adj0, cotangent[:, NB:])),
        jnp.where(
            col == near,
            jnp.where(row == 0, adj2, blocks[2]),
            result[:, NB:],
        ),
    )
    left = jnp.where(
        col == last,
        jnp.where(
            below,
            held[2],
            jnp.where(row == 2, cross, jnp.where(row == 1, adj1, cotangent[:, :NB])),
        ),
        result[:, :NB],
    )
    return jnp.concatenate([left, right], axis=1)


def split(value):
    high = value.astype(jnp.bfloat16)
    return high, (value - high.astype(jnp.float32)).astype(jnp.bfloat16)


def dot3(left, right):
    (lh, ll), (rh, rl) = left, right
    dot = functools.partial(jnp.dot, preferred_element_type=jnp.float32)
    return dot(lh, rh) + (dot(lh, rl) + dot(ll, rh))


def dots(left, right):
    return dot3(split(left), split(right))


SQUARE = (NB, NB)
FLAT = (HALF, NB)


def gated(kernel, bit, clear, ins, outs):
    def body(flags, *refs):
        given, results = refs[:ins], refs[ins : ins + outs]
        here = refs[ins + outs : 2 * ins + outs]
        staged = refs[2 * ins + outs : 2 * ins + 2 * outs] if not clear else results
        extra = refs[2 * ins + (1 if clear else 2) * outs : -1]
        sems = refs[-1]

        @pl.when(flags[bit] == 1)
        def _():
            copies = [pltpu.make_async_copy(a, b, sems.at[k]) for k, (a, b) in enumerate(zip(given, here))]
            for copy in copies:
                copy.start()
            for copy in copies:
                copy.wait()
            kernel(flags, *here, *staged, *extra)
            if not clear:
                copies = [
                    pltpu.make_async_copy(a, b, sems.at[k]) for k, (a, b) in enumerate(zip(staged, results))
                ]
                for copy in copies:
                    copy.start()
                for copy in copies:
                    copy.wait()

        if clear:

            @pl.when(flags[bit] == 0)
            def _():
                for out in results:
                    out[...] = jnp.zeros_like(out)

    return body


def on_chip(kernel, outs, flags, ins, scratch=(), name=None, bit=None, clear=False):
    lazy = bit is not None
    work = [pltpu.VMEM(s, jnp.float32) for s in scratch]
    if lazy:
        kernel = gated(kernel, bit, clear, len(ins), len(outs))
        staged = [] if clear else [pltpu.VMEM(s, jnp.float32) for s in outs]
        work = [pltpu.VMEM(x.shape, jnp.float32) for x in ins] + staged + work
        work += [pltpu.SemaphoreType.DMA((max(len(ins), len(outs)),))]
    inside = pl.ANY if lazy else pltpu.VMEM
    outside = pl.ANY if lazy and not clear else pltpu.VMEM
    result = pl.pallas_call(
        kernel,
        out_shape=[jax.ShapeDtypeStruct(s, jnp.float32) for s in outs],
        in_specs=[pl.BlockSpec(memory_space=pltpu.SMEM)]
        + [pl.BlockSpec(memory_space=inside)] * len(ins),
        out_specs=[pl.BlockSpec(memory_space=outside)] * len(outs),
        scratch_shapes=work,
        compiler_params=pltpu.CompilerParams(vmem_limit_bytes=48 * 1024 * 1024),
        cost_estimate=pl.CostEstimate(flops=0, bytes_accessed=0, transcendentals=0),
        name=name,
    )(flags, *ins)
    return result[0] if len(outs) == 1 else result


ODD, SIDE, TOP, NEXT, ROW, COL, PICK, HEAD, CROSS, FOOT, LOW, LOWEST, MID, LAST, TOP_ALL, NEXT_ALL, UPTO, NEAR, HEAD1, HIGH_ALL = range(20)
UPPER, LOWER = pl.ds(0, HALF), pl.ds(HALF, HALF)
LEFT, RIGHT = pl.ds(0, NB), pl.ds(NB, NB)


def assemble_kernel(flags, own, own_mate, got, got_mate, zero, one):
    here = pl.multiple_of(flags[ODD] * HALF, HALF)
    there = pl.multiple_of((1 - flags[ODD]) * HALF, HALF)

    @pl.when(flags[SIDE] == 1)
    def _():
        zero[pl.ds(here, HALF), :] = own[...]
        zero[pl.ds(there, HALF), :] = own_mate[...]
        one[pl.ds(here, HALF), :] = got[...]
        one[pl.ds(there, HALF), :] = got_mate[...]

    @pl.when(flags[SIDE] == 0)
    def _():
        one[pl.ds(here, HALF), :] = own[...]
        one[pl.ds(there, HALF), :] = own_mate[...]
        zero[pl.ds(here, HALF), :] = got[...]
        zero[pl.ds(there, HALF), :] = got_mate[...]


def pick_kernel(flags, factor, mate, early, later, third, fourth):
    for root, source, span in ((2, factor, UPPER), (3, mate, LOWER)):

        @pl.when(flags[ROW] == root)
        def _(source=source, span=span):
            early[...] = source[span, RIGHT]
            later[...] = source[span, LEFT]

    for root, one, two, span in ((0, mate, factor, UPPER), (1, factor, mate, LOWER)):

        @pl.when(flags[ROW] == root)
        def _(one=one, two=two, span=span):
            later[...] = one[span, RIGHT]
            third[...] = one[span, LEFT]
            fourth[...] = two[span, LEFT]

        @pl.when((flags[ROW] == root) & (flags[COL] == 3))
        def _(one=one, span=span):
            early[...] = one[span, LEFT]

        @pl.when((flags[ROW] == root) & (flags[COL] < 3))
        def _(two=two, span=span):
            early[...] = two[span, RIGHT]


def join_kernel(flags, own, mate, *outs):
    here = pl.multiple_of(flags[ODD] * HALF, HALF)
    there = pl.multiple_of((1 - flags[ODD]) * HALF, HALF)
    for k, out in enumerate(outs):
        span = pl.ds(k * NB, NB)
        out[pl.ds(here, HALF), :] = own[:, span]
        out[pl.ds(there, HALF), :] = mate[:, span]


def first_kernel(flags, cotangent, inverse, out):
    out[...] = dots(cotangent[:, RIGHT], inverse[...])


def second_kernel(flags, cotangent, inverse, block0, strip, out):
    value = cotangent[:, LEFT] - dots(block0[...], strip[...])
    out[...] = dots(value, inverse[...])


def third_kernel(flags, cotangent, inverse, block0, strip0, block1, strip1, out):
    value = cotangent[:, RIGHT] - dots(block0[...], strip0[...])
    value = value - dots(block1[...], strip1[...])
    out[...] = dots(value, inverse[...])


def share_kernel(flags, now, factor, keep, give, turned):
    turned[...] = now[...].T
    here = pl.multiple_of(flags[ODD] * HALF, HALF)
    there = pl.multiple_of((1 - flags[ODD]) * HALF, HALF)
    parts = split(factor[...])
    keep[...] = dot3(split(turned[pl.ds(here, HALF), :]), parts)
    give[...] = dot3(split(turned[pl.ds(there, HALF), :]), parts)


def tri(matrix, scale):
    rows = lax.broadcasted_iota(jnp.int32, matrix.shape, 0)
    cols = lax.broadcasted_iota(jnp.int32, matrix.shape, 1)
    return jnp.where(rows > cols, matrix, jnp.where(rows == cols, scale * matrix, 0.0))


def adjoint_in(diag_factor, diag_cot, inverse, adj, sym, hold):
    hold[...] = tri(dots(diag_factor[...].T, tri(diag_cot, 1.0)), 0.5)
    hold[...] = dots(inverse[...].T, hold[...])
    value = tri(dots(hold[...], inverse[...]), 0.5)
    adj[...] = value
    sym[...] = value + value.T


def adjoint0_kernel(
    flags, total, mate, cotangent, diag_factor, strip, inverse, next_inverse, adj, sym, cross, turned, hold
):
    hold[UPPER, :] = cotangent[UPPER, RIGHT] - total[:, RIGHT]
    hold[LOWER, :] = cotangent[LOWER, RIGHT] - mate[:, RIGHT]
    adjoint_in(diag_factor, hold[...], inverse, adj, sym, hold)
    hold[UPPER, :] = cotangent[UPPER, LEFT] - total[:, LEFT]
    hold[LOWER, :] = cotangent[LOWER, LEFT] - mate[:, LEFT]
    hold[...] = hold[...] - dots(sym[...], strip[...])
    value = dots(hold[...], next_inverse[...])
    cross[...] = value
    turned[...] = value.T


def adjoint1_kernel(flags, total, mate, cotangent, turned, strip, diag_factor, inverse, adj, sym, hold):
    hold[UPPER, :] = cotangent[UPPER, LEFT] - mate[:, LEFT]
    hold[LOWER, :] = cotangent[LOWER, LEFT] - total[:, LEFT]
    hold[...] = hold[...] - dots(turned[...], strip[...])
    adjoint_in(diag_factor, hold[...], inverse, adj, sym, hold)


def adjoint2_kernel(flags, upper, lower, from2, from1, strip0, strip1, diag_factor, inverse, adj, sym, hold):
    hold[UPPER, :] = upper[:, RIGHT]
    hold[LOWER, :] = lower[:, RIGHT]
    hold[...] = hold[...] - dots(from2[...].T, strip0[...])
    hold[...] = hold[...] - dots(from1[...].T, strip1[...])
    adjoint_in(diag_factor, hold[...], inverse, adj, sym, hold)


def cross_kernel(flags, upper, lower, inverse, left0, strip0, left1, strip1, out, hold):
    hold[UPPER, :] = upper[:, RIGHT]
    hold[LOWER, :] = lower[:, RIGHT]
    value = hold[...] - dots(left0[...], strip0[...])
    value = value - dots(left1[...], strip1[...])
    out[...] = dots(value, inverse[...])


FINAL = (
    "now1", "now2", "now3", "now4", "now5", "now6", "own0", "own1", "late", "own0_b", "own1_b",
    "late_b", "own0_c", "own1_c", "late_c", "from2", "from1", "sym2", "over2", "over1",
    "sym_b", "sym_c", "adj0", "cross", "adj1", "adj2", "cotangent",
)


def final_kernel(flags, upper, lower, left0, left1, left2, right0, right1, right2, *refs):
    given = dict(zip(FINAL, refs[: len(FINAL)]))
    out, block, high, low, sems, out_sem = refs[len(FINAL) :]
    step = pl.program_id(0)
    row, col = flags[ROW], flags[COL]
    blocks = {
        "solved": (("now4", "now5", "now6"), ("now3", "now4", "now5"), ("now2", "now3", "now4")),
        "strip": (("own0_c", "own1_c", "late_c"), ("own0_b", "own1_b", "late_b"), ("own0", "own1", "late")),
        "foot": (("over2", "over1", "sym_c"), ("over2", "over1", "sym_b"), ("from2", "from1", "sym2")),
    }
    kinds = {"solved": row >= NP, "strip": (row == 1) | (row == 2), "foot": row == 0}

    def fetch(kind, plane):
        copies = [
            pltpu.make_async_copy(given[name], block.at[k], sems.at[k])
            for k, name in enumerate(blocks[kind][plane])
        ]
        for copy in copies:
            copy.start()
        for copy in copies:
            copy.wait()
        for k in range(NP):
            span = pl.ds(k * NB, NB)
            value = block[k].T if kind == "foot" and k < 2 else block[k]
            high[:, span], low[:, span] = split(value)

    @pl.when(step == 0)
    def _():
        for kind, holds in kinds.items():
            for plane in range(3):

                @pl.when(holds & (col == plane))
                def _(kind=kind, plane=plane):
                    fetch(kind, plane)

    def updated(strips):
        parts = [split(strip[...]) for strip in strips]
        for span, base in ((UPPER, upper), (LOWER, lower)):
            value = base[...]
            for k, part in enumerate(parts):
                left = (high[span, pl.ds(k * NB, NB)], low[span, pl.ds(k * NB, NB)])
                value = value - dot3(left, part)
            out[span, :] = value

    def moved(name, offset):
        column = pl.multiple_of(lax.rem(step, 2) * HALF + offset, HALF)
        copy = pltpu.make_async_copy(given[name].at[:, pl.ds(column, HALF)], out, out_sem)
        copy.start()
        copy.wait()

    def take(holds, name, offset=0):
        @pl.when(holds)
        def _():
            moved(name, offset)

    @pl.when((step < 2) & (col == 3))
    def _():
        take(row >= NP, "now2")
        take(row == 2, "cross")
        take(row == 1, "adj1")
        take(row == 0, "cotangent")

    @pl.when((step >= 2) & (col == 3))
    def _():
        take(row >= NP, "now1")
        take(row == 2, "adj0")
        take(row < 2, "cotangent", NB)

    @pl.when((step >= 2) & (col == 2))
    def _():
        take(row >= NP, "now4")
        take(row == 0, "adj2")
        take((row == 1) | (row == 2), "late")

    @pl.when((step < 2) & (col < 3))
    def _():
        updated((left0, left1, left2))

    @pl.when((step >= 2) & (col < 2))
    def _():
        updated((right0, right1, right2))


def final(flags, running, lefts, rights, given):
    left_spec = pl.BlockSpec((NB, HALF), lambda j: (0, jnp.minimum(j, 1)))
    right_spec = pl.BlockSpec((NB, HALF), lambda j: (0, jnp.maximum(j - 2, 0)))
    wide = pl.BlockSpec((HALF, HALF), lambda j: (0, j))
    return pl.pallas_call(
        final_kernel,
        grid=(4,),
        out_shape=jax.ShapeDtypeStruct((NB, 2 * NB), jnp.float32),
        in_specs=[pl.BlockSpec(memory_space=pltpu.SMEM)]
        + [wide] * 2
        + [left_spec] * 3
        + [right_spec] * 3
        + [pl.BlockSpec(memory_space=pl.ANY)] * len(FINAL),
        out_specs=pl.BlockSpec((NB, HALF), lambda j: (0, j)),
        scratch_shapes=[pltpu.VMEM((NP, NB, NB), jnp.float32)]
        + [pltpu.VMEM((NB, NP * NB), jnp.bfloat16)] * 2
        + [pltpu.SemaphoreType.DMA((NP,)), pltpu.SemaphoreType.DMA],
        compiler_params=pltpu.CompilerParams(vmem_limit_bytes=48 * 1024 * 1024),
        cost_estimate=pl.CostEstimate(flops=0, bytes_accessed=0, transcendentals=0),
        name="final",
    )(flags, *running, *lefts, *rights, *[given[name] for name in FINAL])


FIRST = ('E1', 'S1', 'S4', 'S5', 'S6')
PLAN = {
    "inverse1": "I1",
    "solved1": "J1",
    "now2": "J6",
    "sum2_0": "J1",
    "cross": "J2",
    "crossed": "J2",
    "now3": "",
    "own3": "J2",
    "strip1_left": "J2",
    "own4": "I2",
    "strip2_left": "J3",
    "solved2": "J2",
    "sum3_0": "J2",
    "sym1": "J3",
    "now4": "B3",
    "sum4_0": "J3",
    "own0": "KL",
    "own1": "",
    "late": "J4",
    "sum5_0": "J4",
    "now5": "",
    "own0_b": "J3",
    "own0_c": "I4",
    "from2": "B4",
    "from1": "",
    "own1_b": "B3",
    "own1_c": "J4",
    "late_b": "J6",
    "late_c": "J6",
    "running4": "I4",
    "sym2": "I2",
    "sum6_0": "J5",
    "now6": "",
    "over2": "I1",
    "over1": "K6",
    "sym_b": "B4",
    "sym_c": "",
}


def placed(grid, saved_factor, cotangent):
    row, col = grid.row, grid.col
    planes = range(4)
    below = row >= NP
    side = (row // 2) % 2 == 1
    parts = [grid.odd, side, below & (col == 3), below & (col == 2), row, col, col == 1]
    parts += [(row == 2) & (col == 3), ((row == 1) | (row == 2)) & (col == 2), (row == 0) & (col == 2)]
    parts += [below & (col <= 2), below & (col <= 1), below & ((col == 1) | (col == 2)), below & (col == 0)]
    parts += [col == 3, col == 2, below & (col >= 2), row < 4, (row == 1) & (col == 3), col >= 2]
    flags = jnp.stack([jnp.asarray(p).astype(jnp.int32) for p in parts])

    def core(value):
        return grid.within(value, [(r, r ^ 1) for r in range(8)], planes)

    def down(value, *sources, cut=False):
        if not cut:
            return grid.down(value, range(NP, 8), sources)
        upper, lower = value[:HALF], value[HALF:]
        upper = grid.down(upper, range(NP, 8), sources)
        upper, lower = fence(upper, lower)
        lower = grid.down(lower, range(NP, 8), sources)
        return jnp.concatenate([upper, lower], axis=0)

    def own_from(value, source, target):
        return grid.send(value, [((r, source), (r, target)) for r in (1, 2)])

    def moves(roots, pairs):
        return [((a ^ (root & ~1), c), (b ^ (root & ~1), c)) for c, root in roots.items() for a, b in pairs]

    def inward(value, roots):
        pairs = moves(roots, ((6, 4), (7, 3), (5, 1)))
        pairs += [((2, c), (0, c)) for c, root in roots.items() if root < 2]
        return value + grid.send(value, pairs)

    def home(value, roots):
        return value + grid.send(value, moves(roots, ((4, 0), (3, 1))))

    def settle(running, total, roots):
        upper, lower = running
        mate = core(total)
        chosen = functools.reduce(
            jnp.logical_or, [(col == c) & (row == root) for c, root in roots.items()]
        )
        upper = upper - jnp.where(chosen, jnp.where(grid.odd, mate, total), 0.0)
        lower = lower - jnp.where(chosen, jnp.where(grid.odd, total, mate), 0.0)
        return upper, lower

    def share(now, bit, point):
        keep, give = on_chip(
            share_kernel, [(HALF, 2 * NB)] * 2, flags, (now, saved_factor), [SQUARE], "share", bit, True
        )
        if point in FIRST:
            now, keep, give = fence(now, keep, give)
        return now, keep + core(give)

    def inverted(matrix, bit):
        def kernel(flags, *refs):
            inverse_kernel(*refs)

        return on_chip(kernel, [SQUARE], flags, (matrix,), [(NB, TILE)] * 2, "invert", bit)

    def solve(kernel, bit, *ins):
        return on_chip(kernel, [SQUARE], flags, ins, (), "solve", bit, True)

    def fence(*values):
        return lax.optimization_barrier(values)

    factor = saved_factor

    mate = core(factor)
    early, later, third, fourth = on_chip(
        pick_kernel, [FLAT] * 4, flags, (factor, mate), name="pick", bit=NEAR
    )
    near = row < 4

    def away(mine):
        return grid.within(mine, [(r, r ^ 4) for r in range(4)], planes)

    def both(own):
        got = grid.within(own, [(r, r ^ 2) for r in range(8)], planes)
        return on_chip(
            assemble_kernel, [SQUARE] * 2, flags, (own, core(own), got, core(got)), name="assemble"
        )

    got_early = away(early)
    own_early = jnp.where(near, early, got_early)
    later, own_early = fence(later, own_early)
    got_later = away(later)
    strip0_right, diag1 = both(own_early)
    own_later = jnp.where(near, later, got_later)
    strip0_left, strip1_right = both(own_later)

    ready = {}

    def due(point, *values):
        wanted = [ready[name] for name, at in PLAN.items() if at == point and name in ready]
        if not wanted:
            return values if len(values) > 1 else values[0]
        tied = fence(*values, *wanted)[: len(values)]
        return tied if len(values) > 1 else tied[0]

    inverse0 = inverted(strip0_right, TOP_ALL)
    now1 = solve(first_kernel, TOP, cotangent, inverse0)

    def spread_out(last):
        return jnp.where(near, last, grid.within(last, [(0, 4), (1, 5)], range(3)))

    def spread_on(own):
        got = grid.within(own, [(0, 2), (1, 3), (4, 6), (5, 7)], range(3))
        own = jnp.where(side, got, own)
        return on_chip(join_kernel, [SQUARE], flags, (own, core(own)), name="join")

    def others():
        own3 = spread_out(due("A3", third))
        ready["own3"] = own3
        strip1_left = spread_on(due("B3", own3))
        ready["strip1_left"] = strip1_left
        own4 = spread_out(due("A4", fourth))
        ready["own4"] = own4
        strip2_left = spread_on(due("B4", own4))
        ready["strip2_left"] = strip2_left
        return strip1_left, strip2_left

    if "E0" in FIRST:
        strip1_left, strip2_left = others()

    sums1, sums2, sums3 = {3: 2}, {3: 1, 2: 2}, {2: 1, 1: 2}
    sums4, sums5 = {2: 0, 1: 1, 0: 2}, {1: 0, 0: 1}
    to_foot = [((2, c), (0, c)) for c in range(3)]
    to_foot_core = [((1, c), (0, c)) for c in range(3)]
    now1_on, sum1 = share(now1, TOP, "S1")
    came1 = down(due("H1", now1_on), 3, cut="C1" in FIRST)
    inverse1 = inverted(diag1, HIGH_ALL)
    ready["inverse1"] = inverse1
    solved1 = solve(second_kernel, TOP, cotangent, inverse1, now1, strip0_left)
    ready["solved1"] = solved1
    sum1 = inward(due("I1", sum1), sums1)
    ready["sum1"] = sum1
    now2 = due("N2", solved1 + came1)
    ready["now2"] = now2

    if "E1" in FIRST:
        strip1_left, strip2_left = others()

    now2_on, sum2 = share(now2, UPTO, "S2")
    ready["sum2_0"] = sum2
    came2 = down(due("H2", now2_on), 3, 2, cut="C2" in FIRST)
    sum1 = home(due("J1", sum1), sums1)
    mate1 = core(sum1)
    adj0, sym0, cross, turned = on_chip(
        adjoint0_kernel,
        [SQUARE] * 4,
        flags,
        (sum1, mate1, cotangent, strip0_right, strip0_left, inverse0, inverse1),
        [SQUARE],
        "adjoint",
        HEAD,
    )
    ready["cross"] = cross
    crossed = grid.send(turned, [((2, 3), (1, 3))])
    ready["crossed"] = crossed
    block0 = jnp.where(row == 1, crossed, sym0)
    own0 = own_from(block0, 3, 2)
    ready["own0"] = own0
    block0 = due("KA", block0)
    own0_b, own0_c = own_from(block0, 3, 1), own_from(block0, 3, 0)
    sum2 = inward(due("I2", sum2), sums2)
    ready["sum2"] = sum2
    now3 = due("N3", came2)
    ready["now3"] = now3
    solved2 = solve(third_kernel, NEXT, cotangent, inverse1, now2, strip0_right, now3, strip1_right)
    ready["solved2"] = solved2

    if "E2" in FIRST:
        strip1_left, strip2_left = others()

    now3_on, sum3 = share(now3, MID, "S3")
    ready["sum3_0"] = sum3
    came3 = down(due("H3", now3_on), 2, 1, cut="C3" in FIRST)
    sum2 = home(due("J2", sum2), sums2)
    mate2 = core(sum2)
    adj1, sym1 = on_chip(
        adjoint1_kernel,
        [SQUARE] * 2,
        flags,
        (sum2, mate2, cotangent, crossed, strip0_left, diag1, inverse1),
        [SQUARE],
        "adjoint",
        HEAD1,
    )
    ready["sym1"] = sym1
    block1 = jnp.where(row == 1, sym1, cross)
    own1 = own_from(block1, 3, 2)
    ready["own1"] = own1
    block1 = due("KB", block1)
    own1_b, own1_c = own_from(block1, 3, 1), own_from(block1, 3, 0)
    ready.update(own0_b=own0_b, own0_c=own0_c, own1_b=own1_b, own1_c=own1_c)
    chosen = (row == 2) & (col == 2)
    running = (
        cotangent[:HALF] - jnp.where(chosen, sum2, 0.0),
        cotangent[HALF:] - jnp.where(chosen, mate2, 0.0),
    )
    sum3 = inward(due("I3", sum3), sums3)
    ready["sum3"] = sum3
    now4 = due("N4", solved2 + came3)
    ready["now4"] = now4

    if "E3" in FIRST:
        strip1_left, strip2_left = others()

    now4_on, sum4 = share(now4, LOW, "S4")
    ready["sum4_0"] = sum4
    came4 = down(due("H4", now4_on), 2, 1, cut="C4" in FIRST)
    sum3 = home(due("J3", sum3), sums3)
    running = settle(running, sum3, sums3)
    late = on_chip(
        cross_kernel,
        [SQUARE],
        flags,
        (*running, inverse1, own0, strip0_right, own1, strip1_right),
        [SQUARE],
        "solve",
        CROSS,
        True,
    )
    ready["late"] = late
    from2, from1 = grid.send(late, to_foot), grid.send(late, to_foot_core)
    ready["from2"], ready["from1"] = from2, from1
    late_on = due("KL", late)
    late_b, late_c = own_from(late_on, 2, 1), own_from(late_on, 2, 0)
    ready["late_b"], ready["late_c"] = late_b, late_c
    sum4 = inward(due("I4", sum4), sums4)
    ready["sum4"] = sum4
    now5 = due("N5", came4)
    ready["now5"] = now5

    now5_on, sum5 = share(now5, LOWEST, "S5")
    ready["sum5_0"] = sum5
    came5 = down(due("H5", now5_on), 1, cut="C5" in FIRST)
    sum4 = home(due("J4", sum4), sums4)
    running = settle(running, sum4, sums4)
    ready["running4"] = running[0]
    adj2, sym2 = on_chip(
        adjoint2_kernel,
        [SQUARE] * 2,
        flags,
        (*running, from2, from1, strip0_right, strip1_right, diag1, inverse1),
        [SQUARE],
        "adjoint",
        FOOT,
    )
    ready["sym2"] = sym2
    sym_b = grid.send(sym2, [((0, 2), (0, 1))])
    sym_c = grid.send(sym2, [((0, 2), (0, 0))])
    late_low = due("KO", late_b + late_c)
    over2, over1 = grid.send(late_low, to_foot), grid.send(late_low, to_foot_core)
    ready.update(sym_b=sym_b, sym_c=sym_c, over2=over2, over1=over1)
    sum5 = inward(due("I5", sum5), sums5)
    ready["sum5"] = sum5
    now6 = due("N6", came5)
    ready["now6"] = now6

    _, sum6 = share(now6, LAST, "S6")
    ready["sum6_0"] = sum6
    sum5 = home(due("J5", sum5), sums5)
    running = settle(running, sum5, sums5)
    sum6 = inward(due("I6", sum6), sums5)
    sum6 = home(due("J6", sum6), sums5)
    running = settle(running, due("K6", sum6), {0: 0})

    here = locals()
    return final(
        flags,
        running,
        (strip0_left, strip1_left, strip2_left),
        (strip0_right, strip1_right, diag1),
        {name: here[name] for name in FINAL},
    )


def shards(saved_factor, cotangent):
    grid = Grid()
    if grid.row_count == 8 and grid.col_count == 4:
        return placed(grid, saved_factor, cotangent)
    return general(grid, saved_factor, cotangent)


def solution(mesh):
    placed = (P("row", "col"), P("row", "col"))
    return jax.shard_map(
        shards, mesh=mesh, in_specs=placed, out_specs=P("row", "col"), check_vma=False
    )
```

```python
import functools

import jax
import jax.numpy as jnp
from jax import lax
from jax.experimental import pallas as pl
from jax.experimental.pallas import tpu as pltpu
from jax.sharding import PartitionSpec as P

NB = 512
NP = 3
HALF = NB // 2
BASE = 16
TILE = 128

fine = lax.Precision.HIGHEST
good = lax.Precision.HIGH


def mm(left, right, precision=good):
    return jnp.dot(left, right, precision=precision, preferred_element_type=jnp.float32)


def mm_t(left, right, precision=good):
    return lax.dot_general(
        left, right, (((0,), (0,)), ((), ())), precision=precision, preferred_element_type=jnp.float32
    )


def lower_half(matrix):
    return jnp.tril(matrix) - 0.5 * jnp.diag(jnp.diag(matrix))


def fine_dot(left, right):
    return jnp.dot(left, right, precision=fine, preferred_element_type=jnp.float32)


def inverse_kernel(d_ref, x_ref, tiles, base):
    for t in range(NB // TILE):
        span = pl.ds(t * TILE, TILE)
        tiles[span, :] = d_ref[span, span]
    blocks = NB // BASE
    lane = lax.broadcasted_iota(jnp.int32, (blocks, TILE), 1)
    first = lax.rem(lax.broadcasted_iota(jnp.int32, (blocks, TILE), 0), TILE // BASE) * BASE
    place = lane - first
    solved = []
    for i in range(BASE):
        row = tiles[pl.ds(i, blocks, stride=BASE), :]
        acc = jnp.where(place == i, 1.0, 0.0)
        for k in range(i):
            factor = jnp.sum(jnp.where(place == k, row, 0.0), axis=1, keepdims=True)
            acc = acc - factor * solved[k]
        pivot = jnp.sum(jnp.where(place == i, row, 0.0), axis=1, keepdims=True)
        solved.append(acc / pivot)
        base[pl.ds(i, blocks, stride=BASE), :] = solved[i]
    rows = lax.broadcasted_iota(jnp.int32, (HALF, HALF), 0)
    cols = lax.broadcasted_iota(jnp.int32, (HALF, HALF), 1)
    empty = jnp.zeros((TILE, TILE), jnp.float32)
    corners = []
    for t in range(2):
        top = jnp.concatenate([base[pl.ds(t * HALF, TILE), :], empty], axis=1)
        bottom = jnp.concatenate([empty, base[pl.ds(t * HALF + TILE, TILE), :]], axis=1)
        corners.append(jnp.concatenate([top, bottom], axis=0))
    size = BASE
    while size < HALF:
        below = (rows // (2 * size) == cols // (2 * size)) & (rows // size != cols // size) & (rows > cols)
        for t in range(2):
            span = pl.ds(t * HALF, HALF)
            part = jnp.where(below, d_ref[span, span], 0.0)
            corners[t] = corners[t] - fine_dot(fine_dot(corners[t], part), corners[t])
        size *= 2
    top, bottom = pl.ds(0, HALF), pl.ds(HALF, HALF)
    x_ref[top, top] = corners[0]
    x_ref[top, bottom] = jnp.zeros((HALF, HALF), jnp.float32)
    x_ref[bottom, top] = -fine_dot(fine_dot(corners[1], d_ref[bottom, top]), corners[0])
    x_ref[bottom, bottom] = corners[1]


def invert(matrix):
    return pl.pallas_call(
        inverse_kernel,
        out_shape=jax.ShapeDtypeStruct((NB, NB), jnp.float32),
        in_specs=[pl.BlockSpec(memory_space=pltpu.VMEM)],
        out_specs=pl.BlockSpec(memory_space=pltpu.VMEM),
        scratch_shapes=[pltpu.VMEM((NB, TILE), jnp.float32), pltpu.VMEM((NB, TILE), jnp.float32)],
        compiler_params=pltpu.CompilerParams(vmem_limit_bytes=32 * 1024 * 1024),
        cost_estimate=pl.CostEstimate(flops=20 * 2 * HALF**3 * 6, bytes_accessed=2 * 4 * NB * NB, transcendentals=0),
        name="invert",
    )(matrix)


class Grid:
    def __init__(self):
        self.row_count = lax.axis_size("row")
        self.col_count = lax.axis_size("col")
        self.row = lax.axis_index("row")
        self.col = lax.axis_index("col")
        self.odd = self.row % 2 == 1
        self.paired = self.row_count == 8

    def send(self, value, pairs):
        count = self.col_count
        flat = [(a[0] * count + a[1], b[0] * count + b[1]) for a, b in pairs]
        return lax.ppermute(value, ("row", "col"), flat)

    def within(self, value, moves, planes):
        return self.send(value, [((a, c), (b, c)) for c in planes for a, b in moves])

    def down(self, value, rows, planes):
        return self.send(value, [((r, c), (r, c - 1)) for c in planes for r in rows])

    def is_row(self, *rows):
        return functools.reduce(jnp.logical_or, [self.row == r for r in rows])


def spread(grid, carry, root):
    planes = range(grid.col_count)
    if not grid.paired:
        bit = 1
        while bit < grid.row_count:
            carry = carry + grid.within(carry, [(root ^ m, root ^ m ^ bit) for m in range(bit)], planes)
            bit *= 2
        return carry
    base = root & ~1
    for moves in (((0, 4), (1, 3)), ((4, 6), (3, 7), (1, 5), (0, 2))):
        carry = carry + grid.within(carry, [(a ^ base, b ^ base) for a, b in moves], planes)
    other = grid.within(carry, [(r, r ^ 1) for r in range(grid.row_count)], planes)
    upper = jnp.where(grid.odd, other, carry)
    lower = jnp.where(grid.odd, carry, other)
    return jnp.concatenate([upper, lower], axis=0)


def gather_sum(grid, part, roots):
    if not roots:
        return jnp.zeros_like(part)
    chosen = functools.reduce(
        jnp.logical_or, [(grid.col == c) & (grid.row == root) for c, root in roots.items()]
    )

    def pairs(moves):
        return [((a ^ (root & ~1), c), (b ^ (root & ~1), c)) for c, root in roots.items() for a, b in moves]

    if not grid.paired:
        bit = grid.row_count // 2
        while bit:
            part = part + grid.send(
                part,
                [((root ^ m ^ bit, c), (root ^ m, c)) for c, root in roots.items() for m in range(bit)],
            )
            bit //= 2
        return jnp.where(chosen, part, 0.0)
    half = part.shape[0] // 2
    upper, lower = part[:half], part[half:]
    swapped = grid.send(
        jnp.where(grid.odd, upper, lower),
        [((r, c), (r ^ 1, c)) for c in roots for r in range(grid.row_count)],
    )
    carry = jnp.where(grid.odd, lower, upper) + swapped
    carry = carry + grid.send(carry, pairs(((6, 4), (7, 3), (5, 1), (2, 0))))
    carry = carry + grid.send(carry, pairs(((4, 0), (3, 1))))
    other = grid.send(carry, [((root ^ 1, c), (root, c)) for c, root in roots.items()])
    carry = jnp.where(chosen, carry, 0.0)
    return jnp.concatenate(
        [jnp.where(grid.odd, other, carry), jnp.where(grid.odd, carry, other)], axis=0
    )


def adjoint_of(diag_factor, diag_cot, inverse):
    inner = lower_half(mm_t(diag_factor, jnp.tril(diag_cot)))
    return lower_half(mm(mm_t(inverse, inner), inverse))


def general(grid, saved_factor, cotangent):
    row, col = grid.row, grid.col
    last, near = grid.col_count - 1, grid.col_count - 2
    planes = list(range(grid.col_count))
    solved_rows = range(NP, grid.row_count)
    below = row >= NP

    if grid.paired:
        mine = jnp.where(grid.odd, saved_factor[HALF:], saved_factor[:HALF])
        given = jnp.where(grid.odd, saved_factor[:HALF], saved_factor[HALF:])
        mate = grid.within(given, [(r, r ^ 1) for r in range(NP)], planes)
        seeds = [
            jnp.where(row == root, mine, jnp.where(row == root ^ 1, mate, 0.0)) for root in (2, 1, 0)
        ]
    else:
        seeds = [jnp.where(row == root, saved_factor, 0.0) for root in (2, 1, 0)]
    strip0_right = spread(grid, seeds[0][:, NB:], 2)
    strip0_left = spread(grid, seeds[0][:, :NB], 2)
    strip1_left = spread(grid, seeds[1][:, :NB], 1)
    strip1_right = spread(grid, seeds[1][:, NB:], 1)
    strip2 = spread(grid, seeds[2], 0)
    strip2_right = strip2[:, NB:]

    first_inverse = invert(strip0_right)
    second_diag = jnp.where(col == last, strip1_left, strip2_right)
    second_inverse = invert(second_diag)

    solved0 = mm(cotangent[:, NB:], first_inverse)
    solved1 = mm(cotangent[:, :NB] - mm(solved0, strip0_left), second_inverse)
    starts = {1: solved0, 2: solved1}

    steps = last + NP
    held = {}
    running = cotangent
    came = None
    state = {}
    for step in range(1, steps + 1):
        if step in starts:
            now = jnp.where(below & (col == last), starts[step], 0.0)
            if came is not None:
                now = now + came
        elif step == 4:
            solved2 = mm(
                cotangent[:, NB:] - mm(held[2], strip0_right) - mm(held[3], strip1_right),
                second_inverse,
            )
            now = jnp.where(below & (col == near), solved2, 0.0)
            if came is not None:
                now = now + came
        else:
            now = came
        held[step] = now
        which = {c: step - 1 - (last - c) for c in planes}
        roots = {
            c: 2 - k for c, k in which.items() if 0 <= k < NP and not (c == last and k == 2)
        }
        onward = [c for c in roots if c > 0]
        came = grid.down(now, solved_rows, onward) if onward else jnp.zeros_like(now)
        running = running - gather_sum(grid, mm_t(now, saved_factor), roots)
        if step == 1:
            adj0 = adjoint_of(strip0_right, running[:, NB:], first_inverse)
            sym0 = adj0 + adj0.T
            cross = mm(running[:, :NB] - mm(sym0, strip0_left), second_inverse)
            crossed = grid.send(cross, [((2, last), (1, last))])
        if step == 2:
            adj1 = adjoint_of(
                second_diag, running[:, :NB] - mm_t(crossed, strip0_left), second_inverse
            )
            sym1 = adj1 + adj1.T

    blocks = []
    for k in range(NP):
        block = held[k + 1]
        for hop in range(1, grid.col_count):
            if k + 1 + hop in held:
                block = jnp.where(col == last - hop, held[k + 1 + hop], block)
        blocks.append(block)

    hop0 = grid.send(sym0, [((2, last), (2, near))])
    hop1 = grid.send(cross, [((2, last), (2, near))])
    hop2 = grid.send(crossed, [((1, last), (1, near))])
    hop3 = grid.send(sym1, [((1, last), (1, near))])
    left0 = hop0 + hop2.T
    left1 = hop1 + hop3
    cross2 = mm(
        running[:, NB:] - mm(left0, strip0_right) - mm(left1, strip1_right), second_inverse
    )
    from2 = grid.send(cross2, [((2, near), (0, near))])
    from1 = grid.send(cross2, [((1, near), (0, near))])
    adj2 = adjoint_of(
        strip2_right,
        running[:, NB:] - mm_t(from2, strip0_right) - mm_t(from1, strip1_right),
        second_inverse,
    )
    sym2 = adj2 + adj2.T
    if near > 0:
        pair = jnp.stack([hop0 + hop2, hop1 + hop3])
        total = pair
        late = jnp.where(row == 0, from2, cross2)
        late_total = late
        square = sym2
        square_total = sym2
        for c in range(near, 0, -1):
            pair = grid.down(pair, (1, 2), [c])
            total = total + pair
            late = grid.down(late, (0, 1, 2), [c])
            late_total = jnp.where(col == near, late_total, 0.0) + late if c == near else late_total + late
            square = grid.down(square, (0,), [c])
            square_total = (
                jnp.where(col == near, square_total, 0.0) + square if c == near else square_total + square
            )
        mate = grid.within(late_total, [(1, 0)], range(near))
        other = jnp.where(col == near, from1, mate)
    else:
        total = jnp.stack([hop0 + hop2, hop1 + hop3])
        late_total = jnp.where(row == 0, from2, cross2)
        square_total = sym2
        other = from1
    blocks[0] = jnp.where(
        below, blocks[0], jnp.where(row == 2, total[0], jnp.where(row == 1, total[0], late_total).T)
    )
    blocks[1] = jnp.where(below, blocks[1], jnp.where(row == 0, other.T, total[1]))
    blocks[2] = jnp.where(below, blocks[2], jnp.where(row == 0, square_total, late_total))

    result = running
    strips = (
        jnp.concatenate([strip0_left, strip0_right], axis=1),
        jnp.concatenate([strip1_left, strip1_right], axis=1),
        strip2,
    )
    for block, strip in zip(blocks, strips):
        result = result - mm(block, strip)

    right = jnp.where(
        col == last,
        jnp.where(below, held[1], jnp.where(row == 2, adj0, cotangent[:, NB:])),
        jnp.where(
            col == near,
            jnp.where(row == 0, adj2, blocks[2]),
            result[:, NB:],
        ),
    )
    left = jnp.where(
        col == last,
        jnp.where(
            below,
            held[2],
            jnp.where(row == 2, cross, jnp.where(row == 1, adj1, cotangent[:, :NB])),
        ),
        result[:, :NB],
    )
    return jnp.concatenate([left, right], axis=1)


def split(value):
    high = value.astype(jnp.bfloat16)
    return high, (value - high.astype(jnp.float32)).astype(jnp.bfloat16)


def dot3(left, right):
    (lh, ll), (rh, rl) = left, right
    dot = functools.partial(jnp.dot, preferred_element_type=jnp.float32)
    return dot(lh, rh) + (dot(lh, rl) + dot(ll, rh))


def dots(left, right):
    return dot3(split(left), split(right))


SQUARE = (NB, NB)
FLAT = (HALF, NB)


def gated(kernel, bit, clear, ins, outs):
    def body(flags, *refs):
        given, results = refs[:ins], refs[ins : ins + outs]
        here = refs[ins + outs : 2 * ins + outs]
        staged = refs[2 * ins + outs : 2 * ins + 2 * outs] if not clear else results
        extra = refs[2 * ins + (1 if clear else 2) * outs : -1]
        sems = refs[-1]

        @pl.when(flags[bit] == 1)
        def _():
            copies = [pltpu.make_async_copy(a, b, sems.at[k]) for k, (a, b) in enumerate(zip(given, here))]
            for copy in copies:
                copy.start()
            for copy in copies:
                copy.wait()
            kernel(flags, *here, *staged, *extra)
            if not clear:
                copies = [
                    pltpu.make_async_copy(a, b, sems.at[k]) for k, (a, b) in enumerate(zip(staged, results))
                ]
                for copy in copies:
                    copy.start()
                for copy in copies:
                    copy.wait()

        if clear:

            @pl.when(flags[bit] == 0)
            def _():
                for out in results:
                    out[...] = jnp.zeros_like(out)

    return body


def on_chip(kernel, outs, flags, ins, scratch=(), name=None, bit=None, clear=False):
    lazy = bit is not None
    work = [pltpu.VMEM(s, jnp.float32) for s in scratch]
    if lazy:
        kernel = gated(kernel, bit, clear, len(ins), len(outs))
        staged = [] if clear else [pltpu.VMEM(s, jnp.float32) for s in outs]
        work = [pltpu.VMEM(x.shape, jnp.float32) for x in ins] + staged + work
        work += [pltpu.SemaphoreType.DMA((max(len(ins), len(outs)),))]
    inside = pl.ANY if lazy else pltpu.VMEM
    outside = pl.ANY if lazy and not clear else pltpu.VMEM
    result = pl.pallas_call(
        kernel,
        out_shape=[jax.ShapeDtypeStruct(s, jnp.float32) for s in outs],
        in_specs=[pl.BlockSpec(memory_space=pltpu.SMEM)]
        + [pl.BlockSpec(memory_space=inside)] * len(ins),
        out_specs=[pl.BlockSpec(memory_space=outside)] * len(outs),
        scratch_shapes=work,
        compiler_params=pltpu.CompilerParams(vmem_limit_bytes=48 * 1024 * 1024),
        cost_estimate=pl.CostEstimate(flops=0, bytes_accessed=0, transcendentals=0),
        name=name,
    )(flags, *ins)
    return result[0] if len(outs) == 1 else result


ODD, SIDE, TOP, NEXT, ROW, COL, PICK, HEAD, CROSS, FOOT, LOW, LOWEST, MID, LAST, TOP_ALL, NEXT_ALL, UPTO, NEAR, HEAD1, HIGH_ALL = range(20)
UPPER, LOWER = pl.ds(0, HALF), pl.ds(HALF, HALF)
LEFT, RIGHT = pl.ds(0, NB), pl.ds(NB, NB)


def assemble_kernel(flags, own, own_mate, got, got_mate, zero, one):
    here = pl.multiple_of(flags[ODD] * HALF, HALF)
    there = pl.multiple_of((1 - flags[ODD]) * HALF, HALF)

    @pl.when(flags[SIDE] == 1)
    def _():
        zero[pl.ds(here, HALF), :] = own[...]
        zero[pl.ds(there, HALF), :] = own_mate[...]
        one[pl.ds(here, HALF), :] = got[...]
        one[pl.ds(there, HALF), :] = got_mate[...]

    @pl.when(flags[SIDE] == 0)
    def _():
        one[pl.ds(here, HALF), :] = own[...]
        one[pl.ds(there, HALF), :] = own_mate[...]
        zero[pl.ds(here, HALF), :] = got[...]
        zero[pl.ds(there, HALF), :] = got_mate[...]


def pick_kernel(flags, factor, mate, early, later, third, fourth):
    for root, source, span in ((2, factor, UPPER), (3, mate, LOWER)):

        @pl.when(flags[ROW] == root)
        def _(source=source, span=span):
            early[...] = source[span, RIGHT]
            later[...] = source[span, LEFT]

    for root, one, two, span in ((0, mate, factor, UPPER), (1, factor, mate, LOWER)):

        @pl.when(flags[ROW] == root)
        def _(one=one, two=two, span=span):
            later[...] = one[span, RIGHT]
            third[...] = one[span, LEFT]
            fourth[...] = two[span, LEFT]

        @pl.when((flags[ROW] == root) & (flags[COL] == 3))
        def _(one=one, span=span):
            early[...] = one[span, LEFT]

        @pl.when((flags[ROW] == root) & (flags[COL] < 3))
        def _(two=two, span=span):
            early[...] = two[span, RIGHT]


def join_kernel(flags, own, mate, *outs):
    here = pl.multiple_of(flags[ODD] * HALF, HALF)
    there = pl.multiple_of((1 - flags[ODD]) * HALF, HALF)
    for k, out in enumerate(outs):
        span = pl.ds(k * NB, NB)
        out[pl.ds(here, HALF), :] = own[:, span]
        out[pl.ds(there, HALF), :] = mate[:, span]


def first_kernel(flags, cotangent, inverse, out):
    out[...] = dots(cotangent[:, RIGHT], inverse[...])


def second_kernel(flags, cotangent, inverse, block0, strip, out):
    value = cotangent[:, LEFT] - dots(block0[...], strip[...])
    out[...] = dots(value, inverse[...])


def third_kernel(flags, cotangent, inverse, block0, strip0, block1, strip1, out):
    value = cotangent[:, RIGHT] - dots(block0[...], strip0[...])
    value = value - dots(block1[...], strip1[...])
    out[...] = dots(value, inverse[...])


def share_kernel(flags, now, factor, keep, give, turned):
    turned[...] = now[...].T
    here = pl.multiple_of(flags[ODD] * HALF, HALF)
    there = pl.multiple_of((1 - flags[ODD]) * HALF, HALF)
    parts = split(factor[...])
    keep[...] = dot3(split(turned[pl.ds(here, HALF), :]), parts)
    give[...] = dot3(split(turned[pl.ds(there, HALF), :]), parts)


def tri(matrix, scale):
    rows = lax.broadcasted_iota(jnp.int32, matrix.shape, 0)
    cols = lax.broadcasted_iota(jnp.int32, matrix.shape, 1)
    return jnp.where(rows > cols, matrix, jnp.where(rows == cols, scale * matrix, 0.0))


def adjoint_in(diag_factor, diag_cot, inverse, adj, sym, hold):
    hold[...] = tri(dots(diag_factor[...].T, tri(diag_cot, 1.0)), 0.5)
    hold[...] = dots(inverse[...].T, hold[...])
    value = tri(dots(hold[...], inverse[...]), 0.5)
    adj[...] = value
    sym[...] = value + value.T


def adjoint0_kernel(
    flags, total, mate, cotangent, diag_factor, strip, inverse, next_inverse, adj, sym, cross, turned, hold
):
    hold[UPPER, :] = cotangent[UPPER, RIGHT] - total[:, RIGHT]
    hold[LOWER, :] = cotangent[LOWER, RIGHT] - mate[:, RIGHT]
    adjoint_in(diag_factor, hold[...], inverse, adj, sym, hold)
    hold[UPPER, :] = cotangent[UPPER, LEFT] - total[:, LEFT]
    hold[LOWER, :] = cotangent[LOWER, LEFT] - mate[:, LEFT]
    hold[...] = hold[...] - dots(sym[...], strip[...])
    value = dots(hold[...], next_inverse[...])
    cross[...] = value
    turned[...] = value.T


def adjoint1_kernel(flags, total, mate, cotangent, turned, strip, diag_factor, inverse, adj, sym, hold):
    hold[UPPER, :] = cotangent[UPPER, LEFT] - mate[:, LEFT]
    hold[LOWER, :] = cotangent[LOWER, LEFT] - total[:, LEFT]
    hold[...] = hold[...] - dots(turned[...], strip[...])
    adjoint_in(diag_factor, hold[...], inverse, adj, sym, hold)


def adjoint2_kernel(
    flags, upper, lower, total, mate, from2, from1, strip0, strip1, diag_factor, inverse, adj, packed, hold, sym
):
    hold[UPPER, :] = upper[:, RIGHT] - total[:, RIGHT]
    hold[LOWER, :] = lower[:, RIGHT] - mate[:, RIGHT]
    hold[...] = hold[...] - dots(from2[...].T, strip0[...])
    hold[...] = hold[...] - dots(from1[...].T, strip1[...])
    adjoint_in(diag_factor, hold[...], inverse, adj, sym, hold)
    packed[:, pl.ds(0, HALF)] = sym[UPPER, pl.ds(0, HALF)]
    packed[:, pl.ds(HALF, HALF)] = sym[LOWER, pl.ds(0, HALF)]
    packed[:, pl.ds(2 * HALF, HALF)] = sym[LOWER, pl.ds(HALF, HALF)]


def cross_kernel(flags, upper, lower, total, mate, inverse, left0, strip0, left1, strip1, out, hold):
    hold[UPPER, :] = upper[:, RIGHT]
    hold[LOWER, :] = lower[:, RIGHT]

    @pl.when(flags[ROW] == 1)
    def _():
        hold[UPPER, :] = hold[UPPER, :] - mate[:, RIGHT]
        hold[LOWER, :] = hold[LOWER, :] - total[:, RIGHT]

    value = hold[...] - dots(left0[...], strip0[...])
    value = value - dots(left1[...], strip1[...])
    out[...] = dots(value, inverse[...])


EARLY = (
    "now1", "now2", "now3", "now4", "now5", "own0", "own1", "own0_b", "own1_b", "own0_c", "own1_c",
    "from2", "from1", "over2", "over1",
)
LATE = (
    "now1", "now2", "now4", "now5", "now6", "late", "late_b", "late_c", "sym2", "sym_b", "sym_c",
    "adj0", "cross", "adj1", "adj2", "cotangent",
)


def start_kernel(flags, upper, lower, left0, left1, right0, right1, *refs):
    given = dict(zip(EARLY, refs[: len(EARLY)]))
    out, block, high, low, sems = refs[len(EARLY) :]
    step = pl.program_id(0)
    row, col = flags[ROW], flags[COL]
    blocks = {
        "solved": (("now4", "now5"), ("now3", "now4"), ("now2", "now3")),
        "strip": (("own0_c", "own1_c"), ("own0_b", "own1_b"), ("own0", "own1")),
        "foot": (("over2", "over1"), ("over2", "over1"), ("from2", "from1")),
    }
    kinds = {"solved": row >= NP, "strip": (row == 1) | (row == 2), "foot": row == 0}

    def fetch(kind, plane):
        copies = [
            pltpu.make_async_copy(given[name], block.at[k], sems.at[k])
            for k, name in enumerate(blocks[kind][plane])
        ]
        for copy in copies:
            copy.start()
        for copy in copies:
            copy.wait()
        for k in range(2):
            span = pl.ds(k * NB, NB)
            high[:, span], low[:, span] = split(block[k].T if kind == "foot" else block[k])

    @pl.when(step == 0)
    def _():
        for kind, holds in kinds.items():
            for plane in range(3):

                @pl.when(holds & (col == plane))
                def _(kind=kind, plane=plane):
                    fetch(kind, plane)

    def updated(strips):
        parts = [split(strip[...]) for strip in strips]
        for span, base in ((UPPER, upper), (LOWER, lower)):
            value = base[...]
            for k, part in enumerate(parts):
                left = (high[span, pl.ds(k * NB, NB)], low[span, pl.ds(k * NB, NB)])
                value = value - dot3(left, part)
            out[span, :] = value

    @pl.when((step < 2) & (col < 3))
    def _():
        updated((left0, left1))

    @pl.when((step >= 2) & (col < 2))
    def _():
        updated((right0, right1))


def finish_kernel(flags, started, total, mate, left2, right2, *refs):
    given = dict(zip(LATE, refs[: len(LATE)]))
    out, block, packed, high, low, sem, out_sem = refs[len(LATE) :]
    step = pl.program_id(0)
    row, col = flags[ROW], flags[COL]
    blocks = {
        "solved": ("now6", "now5", "now4"),
        "strip": ("late_c", "late_b", "late"),
        "foot": ("sym_c", "sym_b", "sym2"),
    }
    kinds = {"solved": row >= NP, "strip": (row == 1) | (row == 2), "foot": row == 0}

    def fetch(kind, name):
        copy = pltpu.make_async_copy(given[name], packed if kind == "foot" else block, sem)
        copy.start()
        copy.wait()
        if kind == "foot":
            block[UPPER, pl.ds(0, HALF)] = packed[:, pl.ds(0, HALF)]
            block[LOWER, pl.ds(0, HALF)] = packed[:, pl.ds(HALF, HALF)]
            block[UPPER, pl.ds(HALF, HALF)] = packed[:, pl.ds(HALF, HALF)].T
            block[LOWER, pl.ds(HALF, HALF)] = packed[:, pl.ds(2 * HALF, HALF)]
        high[...], low[...] = split(block[...])

    @pl.when(step == 0)
    def _():
        for kind, holds in kinds.items():
            for plane in range(3):

                @pl.when(holds & (col == plane))
                def _(kind=kind, plane=plane):
                    fetch(kind, blocks[kind][plane])

    def updated(strip):
        out[...] = started[...] - dot3((high[...], low[...]), split(strip[...]))

        @pl.when((row == 0) & (col == 0))
        def _():
            out[UPPER, :] = out[UPPER, :] - total[...]
            out[LOWER, :] = out[LOWER, :] - mate[...]

    def moved(name, offset):
        column = pl.multiple_of(lax.rem(step, 2) * HALF + offset, HALF)
        copy = pltpu.make_async_copy(given[name].at[:, pl.ds(column, HALF)], out, out_sem)
        copy.start()
        copy.wait()

    def take(holds, name, offset=0):
        @pl.when(holds)
        def _():
            moved(name, offset)

    @pl.when((step < 2) & (col == 3))
    def _():
        take(row >= NP, "now2")
        take(row == 2, "cross")
        take(row == 1, "adj1")
        take(row == 0, "cotangent")

    @pl.when((step >= 2) & (col == 3))
    def _():
        take(row >= NP, "now1")
        take(row == 2, "adj0")
        take(row < 2, "cotangent", NB)

    @pl.when((step >= 2) & (col == 2))
    def _():
        take(row >= NP, "now4")
        take(row == 0, "adj2")
        take((row == 1) | (row == 2), "late")

    @pl.when((step < 2) & (col < 3))
    def _():
        updated(left2)

    @pl.when((step >= 2) & (col < 2))
    def _():
        updated(right2)


LEFT_SPEC = pl.BlockSpec((NB, HALF), lambda j: (0, jnp.minimum(j, 1)))
RIGHT_SPEC = pl.BlockSpec((NB, HALF), lambda j: (0, jnp.maximum(j - 2, 0)))
WIDE_SPEC = pl.BlockSpec((HALF, HALF), lambda j: (0, j))
TALL_SPEC = pl.BlockSpec((NB, HALF), lambda j: (0, j))


def by_columns(kernel, name, flags, specs, ins, later, scratch):
    return pl.pallas_call(
        kernel,
        grid=(4,),
        out_shape=jax.ShapeDtypeStruct((NB, 2 * NB), jnp.float32),
        in_specs=[pl.BlockSpec(memory_space=pltpu.SMEM)]
        + specs
        + [pl.BlockSpec(memory_space=pl.ANY)] * len(later),
        out_specs=TALL_SPEC,
        scratch_shapes=scratch,
        compiler_params=pltpu.CompilerParams(vmem_limit_bytes=48 * 1024 * 1024),
        cost_estimate=pl.CostEstimate(flops=0, bytes_accessed=0, transcendentals=0),
        name=name,
    )(flags, *ins, *later)


FIRST = ('C1', 'E1', 'S6')
PLAN = {
    "inverse1": "J1",
    "solved1": "J1",
    "now2": "I5",
    "sum2_0": "J1",
    "cross": "",
    "crossed": "",
    "now3": "",
    "own3": "J2",
    "strip1_left": "J2",
    "own4": "I2",
    "strip2_left": "",
    "solved2": "",
    "sum3_0": "",
    "sym1": "J3",
    "now4": "B3",
    "sum4_0": "J3",
    "own0": "J4",
    "own1": "",
    "late": "J4",
    "sum5_0": "H5",
    "now5": "",
    "own0_b": "H5",
    "own0_c": "I4",
    "from2": "",
    "from1": "I1",
    "own1_b": "B3",
    "own1_c": "J4",
    "late_b": "J6",
    "late_c": "J6",
    "running4": "I4",
    "sym2": "I2",
    "sum6_0": "",
    "now6": "B3",
    "over2": "H2",
    "over1": "K6",
    "sym_b": "B4",
    "sym_c": "",
    "started": "K6",
}


def placed(grid, saved_factor, cotangent):
    row, col = grid.row, grid.col
    planes = range(4)
    below = row >= NP
    side = (row // 2) % 2 == 1
    parts = [grid.odd, side, below & (col == 3), below & (col == 2), row, col, col == 1]
    parts += [(row == 2) & (col == 3), ((row == 1) | (row == 2)) & (col == 2), (row == 0) & (col == 2)]
    parts += [below & (col <= 2), below & (col <= 1), below & ((col == 1) | (col == 2)), below & (col == 0)]
    parts += [col == 3, col == 2, below & (col >= 2), row < 4, (row == 1) & (col == 3), col >= 2]
    flags = jnp.stack([jnp.asarray(p).astype(jnp.int32) for p in parts])

    def core(value):
        return grid.within(value, [(r, r ^ 1) for r in range(8)], planes)

    def down(value, *sources, cut=False):
        if not cut:
            return grid.down(value, range(NP, 8), sources)
        upper, lower = value[:HALF], value[HALF:]
        upper = grid.down(upper, range(NP, 8), sources)
        upper, lower = fence(upper, lower)
        lower = grid.down(lower, range(NP, 8), sources)
        return jnp.concatenate([upper, lower], axis=0)

    def own_from(value, source, target):
        return grid.send(value, [((r, source), (r, target)) for r in (1, 2)])

    def moves(roots, pairs):
        return [((a ^ (root & ~1), c), (b ^ (root & ~1), c)) for c, root in roots.items() for a, b in pairs]

    def inward(value, roots):
        pairs = moves(roots, ((6, 4), (7, 3), (5, 1)))
        pairs += [((2, c), (0, c)) for c, root in roots.items() if root < 2]
        return value + grid.send(value, pairs)

    def home(value, roots):
        return value + grid.send(value, moves(roots, ((4, 0), (3, 1))))

    def settle(running, total, mate, roots):
        upper, lower = running
        chosen = functools.reduce(
            jnp.logical_or, [(col == c) & (row == root) for c, root in roots.items()]
        )
        upper = upper - jnp.where(chosen, jnp.where(grid.odd, mate, total), 0.0)
        lower = lower - jnp.where(chosen, jnp.where(grid.odd, total, mate), 0.0)
        return upper, lower

    def share(now, bit, point):
        keep, give = on_chip(
            share_kernel, [(HALF, 2 * NB)] * 2, flags, (now, saved_factor), [SQUARE], "share", bit, True
        )
        if point in FIRST:
            now, keep, give = fence(now, keep, give)
        return now, keep + core(give)

    def inverted(matrix, bit):
        def kernel(flags, *refs):
            inverse_kernel(*refs)

        return on_chip(kernel, [SQUARE], flags, (matrix,), [(NB, TILE)] * 2, "invert", bit)

    def solve(kernel, bit, *ins):
        return on_chip(kernel, [SQUARE], flags, ins, (), "solve", bit, True)

    def fence(*values):
        return lax.optimization_barrier(values)

    factor = saved_factor

    mate = core(factor)
    early, later, third, fourth = on_chip(
        pick_kernel, [FLAT] * 4, flags, (factor, mate), name="pick", bit=NEAR
    )
    near = row < 4

    def away(mine):
        return grid.within(mine, [(r, r ^ 4) for r in range(4)], planes)

    def both(own):
        got = grid.within(own, [(r, r ^ 2) for r in range(8)], planes)
        return on_chip(
            assemble_kernel, [SQUARE] * 2, flags, (own, core(own), got, core(got)), name="assemble"
        )

    got_early = away(early)
    own_early = jnp.where(near, early, got_early)
    later, own_early = fence(later, own_early)
    got_later = away(later)
    strip0_right, diag1 = both(own_early)
    own_later = jnp.where(near, later, got_later)
    strip0_left, strip1_right = both(own_later)

    ready = {}

    def due(point, *values):
        wanted = [ready[name] for name, at in PLAN.items() if at == point and name in ready]
        if not wanted:
            return values if len(values) > 1 else values[0]
        tied = fence(*values, *wanted)[: len(values)]
        return tied if len(values) > 1 else tied[0]

    inverse0 = inverted(strip0_right, TOP_ALL)
    now1 = solve(first_kernel, TOP, cotangent, inverse0)

    def spread_out(last):
        return jnp.where(near, last, grid.within(last, [(0, 4), (1, 5)], range(3)))

    def spread_on(own):
        got = grid.within(own, [(0, 2), (1, 3), (4, 6), (5, 7)], range(3))
        own = jnp.where(side, got, own)
        return on_chip(join_kernel, [SQUARE], flags, (own, core(own)), name="join")

    def others():
        own3 = spread_out(due("A3", third))
        ready["own3"] = own3
        strip1_left = spread_on(due("B3", own3))
        ready["strip1_left"] = strip1_left
        own4 = spread_out(due("A4", fourth))
        ready["own4"] = own4
        strip2_left = spread_on(due("B4", own4))
        ready["strip2_left"] = strip2_left
        return strip1_left, strip2_left

    if "E0" in FIRST:
        strip1_left, strip2_left = others()

    sums1, sums2, sums3 = {3: 2}, {3: 1, 2: 2}, {2: 1, 1: 2}
    sums4, sums5 = {2: 0, 1: 1, 0: 2}, {1: 0, 0: 1}
    to_foot = [((2, c), (0, c)) for c in range(3)]
    to_foot_core = [((1, c), (0, c)) for c in range(3)]
    now1_on, sum1 = share(now1, TOP, "S1")
    came1 = down(due("H1", now1_on), 3, cut="C1" in FIRST)
    inverse1 = inverted(diag1, HIGH_ALL)
    ready["inverse1"] = inverse1
    solved1 = solve(second_kernel, TOP, cotangent, inverse1, now1, strip0_left)
    ready["solved1"] = solved1
    sum1 = inward(due("I1", sum1), sums1)
    ready["sum1"] = sum1
    now2 = due("N2", solved1 + came1)
    ready["now2"] = now2

    if "E1" in FIRST:
        strip1_left, strip2_left = others()

    now2_on, sum2 = share(now2, UPTO, "S2")
    ready["sum2_0"] = sum2
    came2 = down(due("H2", now2_on), 3, 2, cut="C2" in FIRST)
    sum1 = home(due("J1", sum1), sums1)
    mate1 = core(sum1)
    adj0, sym0, cross, turned = on_chip(
        adjoint0_kernel,
        [SQUARE] * 4,
        flags,
        (sum1, mate1, cotangent, strip0_right, strip0_left, inverse0, inverse1),
        [SQUARE],
        "adjoint",
        HEAD,
    )
    ready["cross"] = cross
    crossed = grid.send(turned, [((2, 3), (1, 3))])
    ready["crossed"] = crossed
    block0 = jnp.where(row == 1, crossed, sym0)
    own0 = own_from(block0, 3, 2)
    ready["own0"] = own0
    block0 = due("KA", block0)
    own0_b, own0_c = own_from(block0, 3, 1), own_from(block0, 3, 0)
    sum2 = inward(due("I2", sum2), sums2)
    ready["sum2"] = sum2
    now3 = due("N3", came2)
    ready["now3"] = now3
    solved2 = solve(third_kernel, NEXT, cotangent, inverse1, now2, strip0_right, now3, strip1_right)
    ready["solved2"] = solved2

    if "E2" in FIRST:
        strip1_left, strip2_left = others()

    now3_on, sum3 = share(now3, MID, "S3")
    ready["sum3_0"] = sum3
    came3 = down(due("H3", now3_on), 2, 1, cut="C3" in FIRST)
    sum2 = home(due("J2", sum2), sums2)
    mate2 = core(sum2)
    adj1, sym1 = on_chip(
        adjoint1_kernel,
        [SQUARE] * 2,
        flags,
        (sum2, mate2, cotangent, crossed, strip0_left, diag1, inverse1),
        [SQUARE],
        "adjoint",
        HEAD1,
    )
    ready["sym1"] = sym1
    block1 = jnp.where(row == 1, sym1, cross)
    own1 = own_from(block1, 3, 2)
    ready["own1"] = own1
    block1 = due("KB", block1)
    own1_b, own1_c = own_from(block1, 3, 1), own_from(block1, 3, 0)
    ready.update(own0_b=own0_b, own0_c=own0_c, own1_b=own1_b, own1_c=own1_c)
    chosen = (row == 2) & (col == 2)
    running = (
        cotangent[:HALF] - jnp.where(chosen, sum2, 0.0),
        cotangent[HALF:] - jnp.where(chosen, mate2, 0.0),
    )
    sum3 = inward(due("I3", sum3), sums3)
    ready["sum3"] = sum3
    now4 = due("N4", solved2 + came3)
    ready["now4"] = now4

    if "E3" in FIRST:
        strip1_left, strip2_left = others()

    now4_on, sum4 = share(now4, LOW, "S4")
    ready["sum4_0"] = sum4
    came4 = down(due("H4", now4_on), 2, 1, cut="C4" in FIRST)
    sum3 = home(due("J3", sum3), sums3)
    mate3 = core(sum3)
    late = on_chip(
        cross_kernel,
        [SQUARE],
        flags,
        (*running, sum3, mate3, inverse1, own0, strip0_right, own1, strip1_right),
        [SQUARE],
        "solve",
        CROSS,
        True,
    )
    ready["late"] = late
    running = settle(running, sum3, mate3, sums3)
    from2, from1 = grid.send(late, to_foot), grid.send(late, to_foot_core)
    ready["from2"], ready["from1"] = from2, from1
    late_on = due("KL", late)
    late_b, late_c = own_from(late_on, 2, 1), own_from(late_on, 2, 0)
    ready["late_b"], ready["late_c"] = late_b, late_c
    sum4 = inward(due("I4", sum4), sums4)
    ready["sum4"] = sum4
    now5 = due("N5", came4)
    ready["now5"] = now5

    now5_on, sum5 = share(now5, LOWEST, "S5")
    ready["sum5_0"] = sum5
    came5 = down(due("H5", now5_on), 1, cut="C5" in FIRST)
    sum4 = home(due("J4", sum4), sums4)
    mate4 = core(sum4)
    adj2, sym2 = on_chip(
        adjoint2_kernel,
        [SQUARE, (HALF, 3 * HALF)],
        flags,
        (*running, sum4, mate4, from2, from1, strip0_right, strip1_right, diag1, inverse1),
        [SQUARE] * 2,
        "adjoint",
        FOOT,
    )
    ready["sym2"] = sym2
    running = settle(running, sum4, mate4, sums4)
    ready["running4"] = running[0]
    sym_b = grid.send(sym2, [((0, 2), (0, 1))])
    sym_c = grid.send(sym2, [((0, 2), (0, 0))])
    late_low = due("KO", late_b + late_c)
    over2, over1 = grid.send(late_low, to_foot), grid.send(late_low, to_foot_core)
    ready.update(sym_b=sym_b, sym_c=sym_c, over2=over2, over1=over1)
    sum5 = inward(due("I5", sum5), sums5)
    ready["sum5"] = sum5
    now6 = due("N6", came5)
    ready["now6"] = now6

    _, sum6 = share(now6, LAST, "S6")
    ready["sum6_0"] = sum6
    sum5 = home(due("J5", sum5), sums5)
    running = settle(running, sum5, core(sum5), sums5)
    here = locals()
    started = by_columns(
        start_kernel,
        "start",
        flags,
        [WIDE_SPEC] * 2 + [LEFT_SPEC] * 2 + [RIGHT_SPEC] * 2,
        (*running, strip0_left, strip1_left, strip0_right, strip1_right),
        [here[name] for name in EARLY],
        [
            pltpu.VMEM((2, NB, NB), jnp.float32),
            pltpu.VMEM((NB, 2 * NB), jnp.bfloat16),
            pltpu.VMEM((NB, 2 * NB), jnp.bfloat16),
            pltpu.SemaphoreType.DMA((2,)),
        ],
    )
    ready["started"] = started
    sum6 = inward(due("I6", sum6), sums5)
    sum6 = home(due("J6", sum6), sums5)
    sum6 = due("K6", sum6)
    return by_columns(
        finish_kernel,
        "finish",
        flags,
        [TALL_SPEC, WIDE_SPEC, WIDE_SPEC, LEFT_SPEC, RIGHT_SPEC],
        (started, sum6, core(sum6), strip2_left, diag1),
        [here[name] for name in LATE],
        [
            pltpu.VMEM(SQUARE, jnp.float32),
            pltpu.VMEM((HALF, 3 * HALF), jnp.float32),
            pltpu.VMEM(SQUARE, jnp.bfloat16),
            pltpu.VMEM(SQUARE, jnp.bfloat16),
            pltpu.SemaphoreType.DMA,
            pltpu.SemaphoreType.DMA,
        ],
    )


def shards(saved_factor, cotangent):
    grid = Grid()
    if grid.row_count == 8 and grid.col_count == 4:
        return placed(grid, saved_factor, cotangent)
    return general(grid, saved_factor, cotangent)


def solution(mesh):
    placed = (P("row", "col"), P("row", "col"))
    return jax.shard_map(
        shards, mesh=mesh, in_specs=placed, out_specs=P("row", "col"), check_vma=False
    )
```

```python
import functools

import jax
import jax.numpy as jnp
from jax import lax
from jax.experimental import pallas as pl
from jax.experimental.pallas import tpu as pltpu
from jax.sharding import PartitionSpec as P

NB = 512
NP = 3
HALF = NB // 2
BASE = 16
TILE = 128

fine = lax.Precision.HIGHEST
good = lax.Precision.HIGH


def mm(left, right, precision=good):
    return jnp.dot(left, right, precision=precision, preferred_element_type=jnp.float32)


def mm_t(left, right, precision=good):
    return lax.dot_general(
        left, right, (((0,), (0,)), ((), ())), precision=precision, preferred_element_type=jnp.float32
    )


def lower_half(matrix):
    return jnp.tril(matrix) - 0.5 * jnp.diag(jnp.diag(matrix))


def fine_dot(left, right):
    return jnp.dot(left, right, precision=fine, preferred_element_type=jnp.float32)


def inverse_kernel(d_ref, x_ref, tiles, base):
    for t in range(NB // TILE):
        span = pl.ds(t * TILE, TILE)
        tiles[span, :] = d_ref[span, span]
    blocks = NB // BASE
    lane = lax.broadcasted_iota(jnp.int32, (blocks, TILE), 1)
    first = lax.rem(lax.broadcasted_iota(jnp.int32, (blocks, TILE), 0), TILE // BASE) * BASE
    place = lane - first
    solved = []
    for i in range(BASE):
        row = tiles[pl.ds(i, blocks, stride=BASE), :]
        acc = jnp.where(place == i, 1.0, 0.0)
        for k in range(i):
            factor = jnp.sum(jnp.where(place == k, row, 0.0), axis=1, keepdims=True)
            acc = acc - factor * solved[k]
        pivot = jnp.sum(jnp.where(place == i, row, 0.0), axis=1, keepdims=True)
        solved.append(acc / pivot)
        base[pl.ds(i, blocks, stride=BASE), :] = solved[i]
    rows = lax.broadcasted_iota(jnp.int32, (HALF, HALF), 0)
    cols = lax.broadcasted_iota(jnp.int32, (HALF, HALF), 1)
    empty = jnp.zeros((TILE, TILE), jnp.float32)
    corners = []
    for t in range(2):
        top = jnp.concatenate([base[pl.ds(t * HALF, TILE), :], empty], axis=1)
        bottom = jnp.concatenate([empty, base[pl.ds(t * HALF + TILE, TILE), :]], axis=1)
        corners.append(jnp.concatenate([top, bottom], axis=0))
    size = BASE
    while size < HALF:
        below = (rows // (2 * size) == cols // (2 * size)) & (rows // size != cols // size) & (rows > cols)
        for t in range(2):
            span = pl.ds(t * HALF, HALF)
            part = jnp.where(below, d_ref[span, span], 0.0)
            corners[t] = corners[t] - fine_dot(fine_dot(corners[t], part), corners[t])
        size *= 2
    top, bottom = pl.ds(0, HALF), pl.ds(HALF, HALF)
    x_ref[top, top] = corners[0]
    x_ref[top, bottom] = jnp.zeros((HALF, HALF), jnp.float32)
    x_ref[bottom, top] = -fine_dot(fine_dot(corners[1], d_ref[bottom, top]), corners[0])
    x_ref[bottom, bottom] = corners[1]


def invert(matrix):
    return pl.pallas_call(
        inverse_kernel,
        out_shape=jax.ShapeDtypeStruct((NB, NB), jnp.float32),
        in_specs=[pl.BlockSpec(memory_space=pltpu.VMEM)],
        out_specs=pl.BlockSpec(memory_space=pltpu.VMEM),
        scratch_shapes=[pltpu.VMEM((NB, TILE), jnp.float32), pltpu.VMEM((NB, TILE), jnp.float32)],
        compiler_params=pltpu.CompilerParams(vmem_limit_bytes=32 * 1024 * 1024),
        cost_estimate=pl.CostEstimate(flops=20 * 2 * HALF**3 * 6, bytes_accessed=2 * 4 * NB * NB, transcendentals=0),
        name="invert",
    )(matrix)


class Grid:
    def __init__(self):
        self.row_count = lax.axis_size("row")
        self.col_count = lax.axis_size("col")
        self.row = lax.axis_index("row")
        self.col = lax.axis_index("col")
        self.odd = self.row % 2 == 1
        self.paired = self.row_count == 8

    def send(self, value, pairs):
        count = self.col_count
        flat = [(a[0] * count + a[1], b[0] * count + b[1]) for a, b in pairs]
        return lax.ppermute(value, ("row", "col"), flat)

    def within(self, value, moves, planes):
        return self.send(value, [((a, c), (b, c)) for c in planes for a, b in moves])

    def down(self, value, rows, planes):
        return self.send(value, [((r, c), (r, c - 1)) for c in planes for r in rows])

    def is_row(self, *rows):
        return functools.reduce(jnp.logical_or, [self.row == r for r in rows])


def spread(grid, carry, root):
    planes = range(grid.col_count)
    if not grid.paired:
        bit = 1
        while bit < grid.row_count:
            carry = carry + grid.within(carry, [(root ^ m, root ^ m ^ bit) for m in range(bit)], planes)
            bit *= 2
        return carry
    base = root & ~1
    for moves in (((0, 4), (1, 3)), ((4, 6), (3, 7), (1, 5), (0, 2))):
        carry = carry + grid.within(carry, [(a ^ base, b ^ base) for a, b in moves], planes)
    other = grid.within(carry, [(r, r ^ 1) for r in range(grid.row_count)], planes)
    upper = jnp.where(grid.odd, other, carry)
    lower = jnp.where(grid.odd, carry, other)
    return jnp.concatenate([upper, lower], axis=0)


def gather_sum(grid, part, roots):
    if not roots:
        return jnp.zeros_like(part)
    chosen = functools.reduce(
        jnp.logical_or, [(grid.col == c) & (grid.row == root) for c, root in roots.items()]
    )

    def pairs(moves):
        return [((a ^ (root & ~1), c), (b ^ (root & ~1), c)) for c, root in roots.items() for a, b in moves]

    if not grid.paired:
        bit = grid.row_count // 2
        while bit:
            part = part + grid.send(
                part,
                [((root ^ m ^ bit, c), (root ^ m, c)) for c, root in roots.items() for m in range(bit)],
            )
            bit //= 2
        return jnp.where(chosen, part, 0.0)
    half = part.shape[0] // 2
    upper, lower = part[:half], part[half:]
    swapped = grid.send(
        jnp.where(grid.odd, upper, lower),
        [((r, c), (r ^ 1, c)) for c in roots for r in range(grid.row_count)],
    )
    carry = jnp.where(grid.odd, lower, upper) + swapped
    carry = carry + grid.send(carry, pairs(((6, 4), (7, 3), (5, 1), (2, 0))))
    carry = carry + grid.send(carry, pairs(((4, 0), (3, 1))))
    other = grid.send(carry, [((root ^ 1, c), (root, c)) for c, root in roots.items()])
    carry = jnp.where(chosen, carry, 0.0)
    return jnp.concatenate(
        [jnp.where(grid.odd, other, carry), jnp.where(grid.odd, carry, other)], axis=0
    )


def adjoint_of(diag_factor, diag_cot, inverse):
    inner = lower_half(mm_t(diag_factor, jnp.tril(diag_cot)))
    return lower_half(mm(mm_t(inverse, inner), inverse))


def general(grid, saved_factor, cotangent):
    row, col = grid.row, grid.col
    last, near = grid.col_count - 1, grid.col_count - 2
    planes = list(range(grid.col_count))
    solved_rows = range(NP, grid.row_count)
    below = row >= NP

    if grid.paired:
        mine = jnp.where(grid.odd, saved_factor[HALF:], saved_factor[:HALF])
        given = jnp.where(grid.odd, saved_factor[:HALF], saved_factor[HALF:])
        mate = grid.within(given, [(r, r ^ 1) for r in range(NP)], planes)
        seeds = [
            jnp.where(row == root, mine, jnp.where(row == root ^ 1, mate, 0.0)) for root in (2, 1, 0)
        ]
    else:
        seeds = [jnp.where(row == root, saved_factor, 0.0) for root in (2, 1, 0)]
    strip0_right = spread(grid, seeds[0][:, NB:], 2)
    strip0_left = spread(grid, seeds[0][:, :NB], 2)
    strip1_left = spread(grid, seeds[1][:, :NB], 1)
    strip1_right = spread(grid, seeds[1][:, NB:], 1)
    strip2 = spread(grid, seeds[2], 0)
    strip2_right = strip2[:, NB:]

    first_inverse = invert(strip0_right)
    second_diag = jnp.where(col == last, strip1_left, strip2_right)
    second_inverse = invert(second_diag)

    solved0 = mm(cotangent[:, NB:], first_inverse)
    solved1 = mm(cotangent[:, :NB] - mm(solved0, strip0_left), second_inverse)
    starts = {1: solved0, 2: solved1}

    steps = last + NP
    held = {}
    running = cotangent
    came = None
    state = {}
    for step in range(1, steps + 1):
        if step in starts:
            now = jnp.where(below & (col == last), starts[step], 0.0)
            if came is not None:
                now = now + came
        elif step == 4:
            solved2 = mm(
                cotangent[:, NB:] - mm(held[2], strip0_right) - mm(held[3], strip1_right),
                second_inverse,
            )
            now = jnp.where(below & (col == near), solved2, 0.0)
            if came is not None:
                now = now + came
        else:
            now = came
        held[step] = now
        which = {c: step - 1 - (last - c) for c in planes}
        roots = {
            c: 2 - k for c, k in which.items() if 0 <= k < NP and not (c == last and k == 2)
        }
        onward = [c for c in roots if c > 0]
        came = grid.down(now, solved_rows, onward) if onward else jnp.zeros_like(now)
        running = running - gather_sum(grid, mm_t(now, saved_factor), roots)
        if step == 1:
            adj0 = adjoint_of(strip0_right, running[:, NB:], first_inverse)
            sym0 = adj0 + adj0.T
            cross = mm(running[:, :NB] - mm(sym0, strip0_left), second_inverse)
            crossed = grid.send(cross, [((2, last), (1, last))])
        if step == 2:
            adj1 = adjoint_of(
                second_diag, running[:, :NB] - mm_t(crossed, strip0_left), second_inverse
            )
            sym1 = adj1 + adj1.T

    blocks = []
    for k in range(NP):
        block = held[k + 1]
        for hop in range(1, grid.col_count):
            if k + 1 + hop in held:
                block = jnp.where(col == last - hop, held[k + 1 + hop], block)
        blocks.append(block)

    hop0 = grid.send(sym0, [((2, last), (2, near))])
    hop1 = grid.send(cross, [((2, last), (2, near))])
    hop2 = grid.send(crossed, [((1, last), (1, near))])
    hop3 = grid.send(sym1, [((1, last), (1, near))])
    left0 = hop0 + hop2.T
    left1 = hop1 + hop3
    cross2 = mm(
        running[:, NB:] - mm(left0, strip0_right) - mm(left1, strip1_right), second_inverse
    )
    from2 = grid.send(cross2, [((2, near), (0, near))])
    from1 = grid.send(cross2, [((1, near), (0, near))])
    adj2 = adjoint_of(
        strip2_right,
        running[:, NB:] - mm_t(from2, strip0_right) - mm_t(from1, strip1_right),
        second_inverse,
    )
    sym2 = adj2 + adj2.T
    if near > 0:
        pair = jnp.stack([hop0 + hop2, hop1 + hop3])
        total = pair
        late = jnp.where(row == 0, from2, cross2)
        late_total = late
        square = sym2
        square_total = sym2
        for c in range(near, 0, -1):
            pair = grid.down(pair, (1, 2), [c])
            total = total + pair
            late = grid.down(late, (0, 1, 2), [c])
            late_total = jnp.where(col == near, late_total, 0.0) + late if c == near else late_total + late
            square = grid.down(square, (0,), [c])
            square_total = (
                jnp.where(col == near, square_total, 0.0) + square if c == near else square_total + square
            )
        mate = grid.within(late_total, [(1, 0)], range(near))
        other = jnp.where(col == near, from1, mate)
    else:
        total = jnp.stack([hop0 + hop2, hop1 + hop3])
        late_total = jnp.where(row == 0, from2, cross2)
        square_total = sym2
        other = from1
    blocks[0] = jnp.where(
        below, blocks[0], jnp.where(row == 2, total[0], jnp.where(row == 1, total[0], late_total).T)
    )
    blocks[1] = jnp.where(below, blocks[1], jnp.where(row == 0, other.T, total[1]))
    blocks[2] = jnp.where(below, blocks[2], jnp.where(row == 0, square_total, late_total))

    result = running
    strips = (
        jnp.concatenate([strip0_left, strip0_right], axis=1),
        jnp.concatenate([strip1_left, strip1_right], axis=1),
        strip2,
    )
    for block, strip in zip(blocks, strips):
        result = result - mm(block, strip)

    right = jnp.where(
        col == last,
        jnp.where(below, held[1], jnp.where(row == 2, adj0, cotangent[:, NB:])),
        jnp.where(
            col == near,
            jnp.where(row == 0, adj2, blocks[2]),
            result[:, NB:],
        ),
    )
    left = jnp.where(
        col == last,
        jnp.where(
            below,
            held[2],
            jnp.where(row == 2, cross, jnp.where(row == 1, adj1, cotangent[:, :NB])),
        ),
        result[:, :NB],
    )
    return jnp.concatenate([left, right], axis=1)


def split(value):
    high = value.astype(jnp.bfloat16)
    return high, (value - high.astype(jnp.float32)).astype(jnp.bfloat16)


def dot3(left, right):
    (lh, ll), (rh, rl) = left, right
    dot = functools.partial(jnp.dot, preferred_element_type=jnp.float32)
    return dot(lh, rh) + (dot(lh, rl) + dot(ll, rh))


def dots(left, right):
    return dot3(split(left), split(right))


SQUARE = (NB, NB)
FLAT = (HALF, NB)


def gated(kernel, bit, clear, ins, outs):
    def body(flags, *refs):
        given, results = refs[:ins], refs[ins : ins + outs]
        here = refs[ins + outs : 2 * ins + outs]
        staged = refs[2 * ins + outs : 2 * ins + 2 * outs] if not clear else results
        extra = refs[2 * ins + (1 if clear else 2) * outs : -1]
        sems = refs[-1]

        @pl.when(flags[bit] == 1)
        def _():
            copies = [pltpu.make_async_copy(a, b, sems.at[k]) for k, (a, b) in enumerate(zip(given, here))]
            for copy in copies:
                copy.start()
            for copy in copies:
                copy.wait()
            kernel(flags, *here, *staged, *extra)
            if not clear:
                copies = [
                    pltpu.make_async_copy(a, b, sems.at[k]) for k, (a, b) in enumerate(zip(staged, results))
                ]
                for copy in copies:
                    copy.start()
                for copy in copies:
                    copy.wait()

        if clear:

            @pl.when(flags[bit] == 0)
            def _():
                for out in results:
                    out[...] = jnp.zeros_like(out)

    return body


def on_chip(kernel, outs, flags, ins, scratch=(), name=None, bit=None, clear=False):
    lazy = bit is not None
    work = [pltpu.VMEM(s, jnp.float32) for s in scratch]
    if lazy:
        kernel = gated(kernel, bit, clear, len(ins), len(outs))
        staged = [] if clear else [pltpu.VMEM(s, jnp.float32) for s in outs]
        work = [pltpu.VMEM(x.shape, jnp.float32) for x in ins] + staged + work
        work += [pltpu.SemaphoreType.DMA((max(len(ins), len(outs)),))]
    inside = pl.ANY if lazy else pltpu.VMEM
    outside = pl.ANY if lazy and not clear else pltpu.VMEM
    result = pl.pallas_call(
        kernel,
        out_shape=[jax.ShapeDtypeStruct(s, jnp.float32) for s in outs],
        in_specs=[pl.BlockSpec(memory_space=pltpu.SMEM)]
        + [pl.BlockSpec(memory_space=inside)] * len(ins),
        out_specs=[pl.BlockSpec(memory_space=outside)] * len(outs),
        scratch_shapes=work,
        compiler_params=pltpu.CompilerParams(vmem_limit_bytes=48 * 1024 * 1024),
        cost_estimate=pl.CostEstimate(flops=0, bytes_accessed=0, transcendentals=0),
        name=name,
    )(flags, *ins)
    return result[0] if len(outs) == 1 else result


ODD, SIDE, TOP, NEXT, ROW, COL, PICK, HEAD, CROSS, FOOT, LOW, LOWEST, MID, LAST, TOP_ALL, NEXT_ALL, UPTO, NEAR, HEAD1, HIGH_ALL = range(20)
UPPER, LOWER = pl.ds(0, HALF), pl.ds(HALF, HALF)
LEFT, RIGHT = pl.ds(0, NB), pl.ds(NB, NB)


def assemble_kernel(flags, own, own_mate, got, got_mate, zero, one):
    here = pl.multiple_of(flags[ODD] * HALF, HALF)
    there = pl.multiple_of((1 - flags[ODD]) * HALF, HALF)

    @pl.when(flags[SIDE] == 1)
    def _():
        zero[pl.ds(here, HALF), :] = own[...]
        zero[pl.ds(there, HALF), :] = own_mate[...]
        one[pl.ds(here, HALF), :] = got[...]
        one[pl.ds(there, HALF), :] = got_mate[...]

    @pl.when(flags[SIDE] == 0)
    def _():
        one[pl.ds(here, HALF), :] = own[...]
        one[pl.ds(there, HALF), :] = own_mate[...]
        zero[pl.ds(here, HALF), :] = got[...]
        zero[pl.ds(there, HALF), :] = got_mate[...]


def pick_kernel(flags, factor, mate, early, later, third, fourth):
    for root, source, span in ((2, factor, UPPER), (3, mate, LOWER)):

        @pl.when(flags[ROW] == root)
        def _(source=source, span=span):
            early[...] = source[span, RIGHT]
            later[...] = source[span, LEFT]

    for root, one, two, span in ((0, mate, factor, UPPER), (1, factor, mate, LOWER)):

        @pl.when(flags[ROW] == root)
        def _(one=one, two=two, span=span):
            later[...] = one[span, RIGHT]
            third[...] = one[span, LEFT]
            fourth[...] = two[span, LEFT]

        @pl.when((flags[ROW] == root) & (flags[COL] == 3))
        def _(one=one, span=span):
            early[...] = one[span, LEFT]

        @pl.when((flags[ROW] == root) & (flags[COL] < 3))
        def _(two=two, span=span):
            early[...] = two[span, RIGHT]


def join_kernel(flags, own, mate, *outs):
    here = pl.multiple_of(flags[ODD] * HALF, HALF)
    there = pl.multiple_of((1 - flags[ODD]) * HALF, HALF)
    for k, out in enumerate(outs):
        span = pl.ds(k * NB, NB)
        out[pl.ds(here, HALF), :] = own[:, span]
        out[pl.ds(there, HALF), :] = mate[:, span]


def first_kernel(flags, cotangent, inverse, out):
    out[...] = dots(cotangent[:, RIGHT], inverse[...])


def second_kernel(flags, cotangent, inverse, block0, strip, out):
    value = cotangent[:, LEFT] - dots(block0[...], strip[...])
    out[...] = dots(value, inverse[...])


def third_kernel(flags, cotangent, inverse, block0, strip0, block1, strip1, out):
    value = cotangent[:, RIGHT] - dots(block0[...], strip0[...])
    value = value - dots(block1[...], strip1[...])
    out[...] = dots(value, inverse[...])


def share_kernel(flags, now, factor, keep, give, turned):
    turned[...] = now[...].T
    here = pl.multiple_of(flags[ODD] * HALF, HALF)
    there = pl.multiple_of((1 - flags[ODD]) * HALF, HALF)
    parts = split(factor[...])
    keep[...] = dot3(split(turned[pl.ds(here, HALF), :]), parts)
    give[...] = dot3(split(turned[pl.ds(there, HALF), :]), parts)


def tri(matrix, scale):
    rows = lax.broadcasted_iota(jnp.int32, matrix.shape, 0)
    cols = lax.broadcasted_iota(jnp.int32, matrix.shape, 1)
    return jnp.where(rows > cols, matrix, jnp.where(rows == cols, scale * matrix, 0.0))


def adjoint_in(diag_factor, diag_cot, inverse, adj, sym, hold):
    hold[...] = tri(dots(diag_factor[...].T, tri(diag_cot, 1.0)), 0.5)
    hold[...] = dots(inverse[...].T, hold[...])
    value = tri(dots(hold[...], inverse[...]), 0.5)
    adj[...] = value
    sym[...] = value + value.T


def adjoint0_kernel(
    flags, total, mate, cotangent, diag_factor, strip, inverse, next_inverse, adj, sym, cross, turned, hold
):
    hold[UPPER, :] = cotangent[UPPER, RIGHT] - total[:, RIGHT]
    hold[LOWER, :] = cotangent[LOWER, RIGHT] - mate[:, RIGHT]
    adjoint_in(diag_factor, hold[...], inverse, adj, sym, hold)
    hold[UPPER, :] = cotangent[UPPER, LEFT] - total[:, LEFT]
    hold[LOWER, :] = cotangent[LOWER, LEFT] - mate[:, LEFT]
    hold[...] = hold[...] - dots(sym[...], strip[...])
    value = dots(hold[...], next_inverse[...])
    cross[...] = value
    turned[...] = value.T


def adjoint1_kernel(flags, total, mate, cotangent, turned, strip, diag_factor, inverse, adj, sym, hold):
    hold[UPPER, :] = cotangent[UPPER, LEFT] - mate[:, LEFT]
    hold[LOWER, :] = cotangent[LOWER, LEFT] - total[:, LEFT]
    hold[...] = hold[...] - dots(turned[...], strip[...])
    adjoint_in(diag_factor, hold[...], inverse, adj, sym, hold)


def adjoint2_kernel(
    flags, upper, lower, total, mate, from2, from1, strip0, strip1, diag_factor, inverse, adj, packed, hold, sym
):
    hold[UPPER, :] = upper[:, RIGHT] - total[:, RIGHT]
    hold[LOWER, :] = lower[:, RIGHT] - mate[:, RIGHT]
    hold[...] = hold[...] - dots(from2[...].T, strip0[...])
    hold[...] = hold[...] - dots(from1[...].T, strip1[...])
    adjoint_in(diag_factor, hold[...], inverse, adj, sym, hold)
    packed[:, pl.ds(0, HALF)] = sym[UPPER, pl.ds(0, HALF)]
    packed[:, pl.ds(HALF, HALF)] = sym[LOWER, pl.ds(0, HALF)]
    packed[:, pl.ds(2 * HALF, HALF)] = sym[LOWER, pl.ds(HALF, HALF)]


def cross_kernel(flags, upper, lower, total, mate, inverse, left0, strip0, left1, strip1, out, hold):
    hold[UPPER, :] = upper[:, RIGHT]
    hold[LOWER, :] = lower[:, RIGHT]

    @pl.when(flags[ROW] == 1)
    def _():
        hold[UPPER, :] = hold[UPPER, :] - mate[:, RIGHT]
        hold[LOWER, :] = hold[LOWER, :] - total[:, RIGHT]

    value = hold[...] - dots(left0[...], strip0[...])
    value = value - dots(left1[...], strip1[...])
    out[...] = dots(value, inverse[...])


EARLY = (
    "now1", "now2", "now3", "now4", "now5", "own0", "own1", "own0_b", "own1_b", "own0_c", "own1_c",
    "from2", "from1", "over2", "over1",
)
LATE = (
    "now1", "now2", "now4", "now5", "now6", "late", "late_b", "late_c", "sym2", "sym_b", "sym_c",
    "adj0", "cross", "adj1", "adj2", "cotangent",
)


def start_kernel(flags, upper, lower, left0, left1, right0, right1, *refs):
    given = dict(zip(EARLY, refs[: len(EARLY)]))
    out, block, high, low, sems = refs[len(EARLY) :]
    step = pl.program_id(0)
    row, col = flags[ROW], flags[COL]
    blocks = {
        "solved": (("now4", "now5"), ("now3", "now4"), ("now2", "now3")),
        "strip": (("own0_c", "own1_c"), ("own0_b", "own1_b"), ("own0", "own1")),
        "foot": (("over2", "over1"), ("over2", "over1"), ("from2", "from1")),
    }
    kinds = {"solved": row >= NP, "strip": (row == 1) | (row == 2), "foot": row == 0}

    def fetch(kind, plane):
        copies = [
            pltpu.make_async_copy(given[name], block.at[k], sems.at[k])
            for k, name in enumerate(blocks[kind][plane])
        ]
        for copy in copies:
            copy.start()
        for copy in copies:
            copy.wait()
        for k in range(2):
            span = pl.ds(k * NB, NB)
            high[:, span], low[:, span] = split(block[k].T if kind == "foot" else block[k])

    @pl.when(step == 0)
    def _():
        for kind, holds in kinds.items():
            for plane in range(3):

                @pl.when(holds & (col == plane))
                def _(kind=kind, plane=plane):
                    fetch(kind, plane)

    def updated(strips):
        parts = [split(strip[...]) for strip in strips]
        for span, base in ((UPPER, upper), (LOWER, lower)):
            value = base[...]
            for k, part in enumerate(parts):
                left = (high[span, pl.ds(k * NB, NB)], low[span, pl.ds(k * NB, NB)])
                value = value - dot3(left, part)
            out[span, :] = value

    @pl.when((step < 2) & (col < 3))
    def _():
        updated((left0, left1))

    @pl.when((step >= 2) & (col < 2))
    def _():
        updated((right0, right1))


def finish_kernel(flags, started, total, mate, left2, right2, *refs):
    given = dict(zip(LATE, refs[: len(LATE)]))
    out, block, packed, high, low, sem, out_sem = refs[len(LATE) :]
    step = pl.program_id(0)
    row, col = flags[ROW], flags[COL]
    blocks = {
        "solved": ("now6", "now5", "now4"),
        "strip": ("late_c", "late_b", "late"),
        "foot": ("sym_c", "sym_b", "sym2"),
    }
    kinds = {"solved": row >= NP, "strip": (row == 1) | (row == 2), "foot": row == 0}

    def fetch(kind, name):
        copy = pltpu.make_async_copy(given[name], packed if kind == "foot" else block, sem)
        copy.start()
        copy.wait()
        if kind == "foot":
            block[UPPER, pl.ds(0, HALF)] = packed[:, pl.ds(0, HALF)]
            block[LOWER, pl.ds(0, HALF)] = packed[:, pl.ds(HALF, HALF)]
            block[UPPER, pl.ds(HALF, HALF)] = packed[:, pl.ds(HALF, HALF)].T
            block[LOWER, pl.ds(HALF, HALF)] = packed[:, pl.ds(2 * HALF, HALF)]
        high[...], low[...] = split(block[...])

    @pl.when(step == 0)
    def _():
        for kind, holds in kinds.items():
            for plane in range(3):

                @pl.when(holds & (col == plane))
                def _(kind=kind, plane=plane):
                    fetch(kind, blocks[kind][plane])

    def updated(strip):
        out[...] = started[...] - dot3((high[...], low[...]), split(strip[...]))

        @pl.when((row == 0) & (col == 0))
        def _():
            out[UPPER, :] = out[UPPER, :] - total[...]
            out[LOWER, :] = out[LOWER, :] - mate[...]

    def moved(name, offset):
        column = pl.multiple_of(lax.rem(step, 2) * HALF + offset, HALF)
        copy = pltpu.make_async_copy(given[name].at[:, pl.ds(column, HALF)], out, out_sem)
        copy.start()
        copy.wait()

    def take(holds, name, offset=0):
        @pl.when(holds)
        def _():
            moved(name, offset)

    @pl.when((step < 2) & (col == 3))
    def _():
        take(row >= NP, "now2")
        take(row == 2, "cross")
        take(row == 1, "adj1")
        take(row == 0, "cotangent")

    @pl.when((step >= 2) & (col == 3))
    def _():
        take(row >= NP, "now1")
        take(row == 2, "adj0")
        take(row < 2, "cotangent", NB)

    @pl.when((step >= 2) & (col == 2))
    def _():
        take(row >= NP, "now4")
        take(row == 0, "adj2")
        take((row == 1) | (row == 2), "late")

    @pl.when((step < 2) & (col < 3))
    def _():
        updated(left2)

    @pl.when((step >= 2) & (col < 2))
    def _():
        updated(right2)


LEFT_SPEC = pl.BlockSpec((NB, HALF), lambda j: (0, jnp.minimum(j, 1)))
RIGHT_SPEC = pl.BlockSpec((NB, HALF), lambda j: (0, jnp.maximum(j - 2, 0)))
WIDE_SPEC = pl.BlockSpec((HALF, HALF), lambda j: (0, j))
TALL_SPEC = pl.BlockSpec((NB, HALF), lambda j: (0, j))


def by_columns(kernel, name, flags, specs, ins, later, scratch):
    return pl.pallas_call(
        kernel,
        grid=(4,),
        out_shape=jax.ShapeDtypeStruct((NB, 2 * NB), jnp.float32),
        in_specs=[pl.BlockSpec(memory_space=pltpu.SMEM)]
        + specs
        + [pl.BlockSpec(memory_space=pl.ANY)] * len(later),
        out_specs=TALL_SPEC,
        scratch_shapes=scratch,
        compiler_params=pltpu.CompilerParams(vmem_limit_bytes=48 * 1024 * 1024),
        cost_estimate=pl.CostEstimate(flops=0, bytes_accessed=0, transcendentals=0),
        name=name,
    )(flags, *ins, *later)


def placed(grid, saved_factor, cotangent):
    row, col = grid.row, grid.col
    planes = range(4)
    below = row >= NP
    side = (row // 2) % 2 == 1
    parts = [grid.odd, side, below & (col == 3), below & (col == 2), row, col, col == 1]
    parts += [(row == 2) & (col == 3), ((row == 1) | (row == 2)) & (col == 2), (row == 0) & (col == 2)]
    parts += [below & (col <= 2), below & (col <= 1), below & ((col == 1) | (col == 2)), below & (col == 0)]
    parts += [col == 3, col == 2, below & (col >= 2), row < 4, (row == 1) & (col == 3), col >= 2]
    flags = jnp.stack([jnp.asarray(p).astype(jnp.int32) for p in parts])

    def core(value):
        return grid.within(value, [(r, r ^ 1) for r in range(8)], planes)

    def down(value, *sources, cut=False):
        if not cut:
            return grid.down(value, range(NP, 8), sources)
        upper, lower = value[:HALF], value[HALF:]
        upper = grid.down(upper, range(NP, 8), sources)
        upper, lower = fence(upper, lower)
        lower = grid.down(lower, range(NP, 8), sources)
        return jnp.concatenate([upper, lower], axis=0)

    def own_from(value, source, target):
        return grid.send(value, [((r, source), (r, target)) for r in (1, 2)])

    def moves(roots, pairs):
        return [((a ^ (root & ~1), c), (b ^ (root & ~1), c)) for c, root in roots.items() for a, b in pairs]

    def inward(value, roots):
        pairs = moves(roots, ((6, 4), (7, 3), (5, 1)))
        pairs += [((2, c), (0, c)) for c, root in roots.items() if root < 2]
        return value + grid.send(value, pairs)

    def home(value, roots):
        return value + grid.send(value, moves(roots, ((4, 0), (3, 1))))

    def settle(running, total, mate, roots):
        upper, lower = running
        chosen = functools.reduce(
            jnp.logical_or, [(col == c) & (row == root) for c, root in roots.items()]
        )
        upper = upper - jnp.where(chosen, jnp.where(grid.odd, mate, total), 0.0)
        lower = lower - jnp.where(chosen, jnp.where(grid.odd, total, mate), 0.0)
        return upper, lower

    def share(now, bit, before):
        keep, give = on_chip(
            share_kernel, [(HALF, 2 * NB)] * 2, flags, (now, saved_factor), [SQUARE], "share", bit, True
        )
        if before:
            now, keep, give = fence(now, keep, give)
        return now, keep + core(give)

    def inverted(matrix, bit):
        def kernel(flags, *refs):
            inverse_kernel(*refs)

        return on_chip(kernel, [SQUARE], flags, (matrix,), [(NB, TILE)] * 2, "invert", bit)

    def solve(kernel, bit, *ins):
        return on_chip(kernel, [SQUARE], flags, ins, (), "solve", bit, True)

    def fence(*values):
        return lax.optimization_barrier(values)

    factor = saved_factor

    mate = core(factor)
    early, later, third, fourth = on_chip(
        pick_kernel, [FLAT] * 4, flags, (factor, mate), name="pick", bit=NEAR
    )
    near = row < 4

    def away(mine):
        return grid.within(mine, [(r, r ^ 4) for r in range(4)], planes)

    def both(own):
        got = grid.within(own, [(r, r ^ 2) for r in range(8)], planes)
        return on_chip(
            assemble_kernel, [SQUARE] * 2, flags, (own, core(own), got, core(got)), name="assemble"
        )

    got_early = away(early)
    own_early = jnp.where(near, early, got_early)
    later, own_early = fence(later, own_early)
    got_later = away(later)
    strip0_right, diag1 = both(own_early)
    own_later = jnp.where(near, later, got_later)
    strip0_left, strip1_right = both(own_later)

    def tied(value, *others):
        return fence(value, *others)[0]

    inverse0 = inverted(strip0_right, TOP_ALL)
    now1 = solve(first_kernel, TOP, cotangent, inverse0)

    def spread_out(last):
        return jnp.where(near, last, grid.within(last, [(0, 4), (1, 5)], range(3)))

    def spread_on(own):
        got = grid.within(own, [(0, 2), (1, 3), (4, 6), (5, 7)], range(3))
        own = jnp.where(side, got, own)
        return on_chip(join_kernel, [SQUARE], flags, (own, core(own)), name="join")


    sums1, sums2, sums3 = {3: 2}, {3: 1, 2: 2}, {2: 1, 1: 2}
    sums4, sums5 = {2: 0, 1: 1, 0: 2}, {1: 0, 0: 1}
    to_foot = [((2, c), (0, c)) for c in range(3)]
    to_foot_core = [((1, c), (0, c)) for c in range(3)]
    now1_on, sum1 = share(now1, TOP, False)
    came1 = down(now1_on, 3, cut=False)
    inverse1 = inverted(diag1, HIGH_ALL)
    held_inverse1 = inverse1
    solved1 = solve(second_kernel, TOP, cotangent, inverse1, now1, strip0_left)
    held_solved1 = solved1
    sum1 = inward(sum1, sums1)
    now2 = solved1 + came1
    held_now2 = now2

    own3 = spread_out(third)
    held_own3 = own3
    strip1_left = spread_on(own3)
    held_strip1_left = strip1_left
    own4 = spread_out(fourth)
    held_own4 = own4
    strip2_left = spread_on(own4)

    now2_on, sum2 = share(now2, UPTO, False)
    held_sum2_0 = sum2
    came2 = down(now2_on, 3, 2, cut=False)
    sum1 = home(tied(sum1, held_inverse1, held_solved1, held_sum2_0), sums1)
    mate1 = core(sum1)
    adj0, sym0, cross, turned = on_chip(
        adjoint0_kernel,
        [SQUARE] * 4,
        flags,
        (sum1, mate1, cotangent, strip0_right, strip0_left, inverse0, inverse1),
        [SQUARE],
        "adjoint",
        HEAD,
    )
    crossed = grid.send(turned, [((2, 3), (1, 3))])
    block0 = jnp.where(row == 1, crossed, sym0)
    own0 = own_from(block0, 3, 2)
    held_own0 = own0
    block0 = block0
    own0_b, own0_c = own_from(block0, 3, 1), own_from(block0, 3, 0)
    sum2 = inward(tied(sum2, held_own4), sums2)
    now3 = came2
    solved2 = solve(third_kernel, NEXT, cotangent, inverse1, now2, strip0_right, now3, strip1_right)
    held_solved2 = solved2


    now3_on, sum3 = share(now3, MID, False)
    came3 = down(now3_on, 2, 1, cut=False)
    sum2 = home(tied(sum2, held_own3, held_strip1_left), sums2)
    mate2 = core(sum2)
    adj1, sym1 = on_chip(
        adjoint1_kernel,
        [SQUARE] * 2,
        flags,
        (sum2, mate2, cotangent, crossed, strip0_left, diag1, inverse1),
        [SQUARE],
        "adjoint",
        HEAD1,
    )
    held_sym1 = sym1
    block1 = jnp.where(row == 1, sym1, cross)
    own1 = own_from(block1, 3, 2)
    block1 = block1
    own1_b, own1_c = own_from(block1, 3, 1), own_from(block1, 3, 0)
    held_own0_b = own0_b
    held_own0_c = own0_c
    held_own1_b = own1_b
    held_own1_c = own1_c
    chosen = (row == 2) & (col == 2)
    running = (
        cotangent[:HALF] - jnp.where(chosen, sum2, 0.0),
        cotangent[HALF:] - jnp.where(chosen, mate2, 0.0),
    )
    sum3 = inward(sum3, sums3)
    now4 = solved2 + came3


    now4_on, sum4 = share(now4, LOW, False)
    held_sum4_0 = sum4
    came4 = down(now4_on, 2, 1, cut=False)
    sum3 = home(tied(sum3, held_sym1, held_sum4_0), sums3)
    mate3 = core(sum3)
    late = on_chip(
        cross_kernel,
        [SQUARE],
        flags,
        (*running, sum3, mate3, inverse1, own0, strip0_right, own1, strip1_right),
        [SQUARE],
        "solve",
        CROSS,
        True,
    )
    held_late = late
    running = settle(running, sum3, mate3, sums3)
    from2, from1 = grid.send(late, to_foot), grid.send(late, to_foot_core)
    late_on = tied(late, held_solved2)
    late_b, late_c = own_from(late_on, 2, 1), own_from(late_on, 2, 0)
    held_late_b = late_b
    held_late_c = late_c
    sum4 = inward(tied(sum4, held_own0_c), sums4)
    now5 = came4

    now5_on, sum5 = share(now5, LOWEST, False)
    held_sum5_0 = sum5
    came5 = down(tied(now5_on, held_sum5_0, held_own0_b), 1, cut=False)
    sum4 = home(tied(sum4, held_own0, held_late, held_own1_c), sums4)
    mate4 = core(sum4)
    adj2, sym2 = on_chip(
        adjoint2_kernel,
        [SQUARE, (HALF, 3 * HALF)],
        flags,
        (*running, sum4, mate4, from2, from1, strip0_right, strip1_right, diag1, inverse1),
        [SQUARE] * 2,
        "adjoint",
        FOOT,
    )
    running = settle(running, sum4, mate4, sums4)
    sym_b = grid.send(sym2, [((0, 2), (0, 1))])
    sym_c = grid.send(sym2, [((0, 2), (0, 0))])
    late_low = late_b + late_c
    over2, over1 = grid.send(late_low, to_foot), grid.send(late_low, to_foot_core)
    held_over1 = over1
    sum5 = inward(tied(sum5, held_now2), sums5)
    now6 = came5

    _, sum6 = share(now6, LAST, True)
    sum5 = home(sum5, sums5)
    running = settle(running, sum5, core(sum5), sums5)
    here = locals()
    started = by_columns(
        start_kernel,
        "start",
        flags,
        [WIDE_SPEC] * 2 + [LEFT_SPEC] * 2 + [RIGHT_SPEC] * 2,
        (*running, strip0_left, strip1_left, strip0_right, strip1_right),
        [here[name] for name in EARLY],
        [
            pltpu.VMEM((2, NB, NB), jnp.float32),
            pltpu.VMEM((NB, 2 * NB), jnp.bfloat16),
            pltpu.VMEM((NB, 2 * NB), jnp.bfloat16),
            pltpu.SemaphoreType.DMA((2,)),
        ],
    )
    held_started = started
    sum6 = inward(sum6, sums5)
    sum6 = home(tied(sum6, held_late_b, held_late_c), sums5)
    sum6 = tied(sum6, held_own1_b, held_over1, held_started)
    return by_columns(
        finish_kernel,
        "finish",
        flags,
        [TALL_SPEC, WIDE_SPEC, WIDE_SPEC, LEFT_SPEC, RIGHT_SPEC],
        (started, sum6, core(sum6), strip2_left, diag1),
        [here[name] for name in LATE],
        [
            pltpu.VMEM(SQUARE, jnp.float32),
            pltpu.VMEM((HALF, 3 * HALF), jnp.float32),
            pltpu.VMEM(SQUARE, jnp.bfloat16),
            pltpu.VMEM(SQUARE, jnp.bfloat16),
            pltpu.SemaphoreType.DMA,
            pltpu.SemaphoreType.DMA,
        ],
    )


def shards(saved_factor, cotangent):
    grid = Grid()
    if grid.row_count == 8 and grid.col_count == 4:
        return placed(grid, saved_factor, cotangent)
    return general(grid, saved_factor, cotangent)


def solution(mesh):
    placed = (P("row", "col"), P("row", "col"))
    return jax.shard_map(
        shards, mesh=mesh, in_specs=placed, out_specs=P("row", "col"), check_vma=False
    )
```

```python
import functools

import jax
import jax.numpy as jnp
from jax import lax
from jax.experimental import pallas as pl
from jax.experimental.pallas import tpu as pltpu
from jax.sharding import PartitionSpec as P

NB = 512
NP = 3
HALF = NB // 2
BASE = 16
TILE = 128

fine = lax.Precision.HIGHEST
good = lax.Precision.HIGH


def mm(left, right, precision=good):
    return jnp.dot(left, right, precision=precision, preferred_element_type=jnp.float32)


def mm_t(left, right, precision=good):
    return lax.dot_general(
        left, right, (((0,), (0,)), ((), ())), precision=precision, preferred_element_type=jnp.float32
    )


def lower_half(matrix):
    return jnp.tril(matrix) - 0.5 * jnp.diag(jnp.diag(matrix))


def fine_dot(left, right):
    return jnp.dot(left, right, precision=fine, preferred_element_type=jnp.float32)


def inverse_kernel(d_ref, x_ref, tiles, base):
    for t in range(NB // TILE):
        span = pl.ds(t * TILE, TILE)
        tiles[span, :] = d_ref[span, span]
    blocks = NB // BASE
    lane = lax.broadcasted_iota(jnp.int32, (blocks, TILE), 1)
    first = lax.rem(lax.broadcasted_iota(jnp.int32, (blocks, TILE), 0), TILE // BASE) * BASE
    place = lane - first
    solved = []
    for i in range(BASE):
        row = tiles[pl.ds(i, blocks, stride=BASE), :]
        acc = jnp.where(place == i, 1.0, 0.0)
        for k in range(i):
            factor = jnp.sum(jnp.where(place == k, row, 0.0), axis=1, keepdims=True)
            acc = acc - factor * solved[k]
        pivot = jnp.sum(jnp.where(place == i, row, 0.0), axis=1, keepdims=True)
        solved.append(acc / pivot)
        base[pl.ds(i, blocks, stride=BASE), :] = solved[i]
    rows = lax.broadcasted_iota(jnp.int32, (HALF, HALF), 0)
    cols = lax.broadcasted_iota(jnp.int32, (HALF, HALF), 1)
    empty = jnp.zeros((TILE, TILE), jnp.float32)
    corners = []
    for t in range(2):
        top = jnp.concatenate([base[pl.ds(t * HALF, TILE), :], empty], axis=1)
        bottom = jnp.concatenate([empty, base[pl.ds(t * HALF + TILE, TILE), :]], axis=1)
        corners.append(jnp.concatenate([top, bottom], axis=0))
    size = BASE
    while size < HALF:
        below = (rows // (2 * size) == cols // (2 * size)) & (rows // size != cols // size) & (rows > cols)
        for t in range(2):
            span = pl.ds(t * HALF, HALF)
            part = jnp.where(below, d_ref[span, span], 0.0)
            corners[t] = corners[t] - fine_dot(fine_dot(corners[t], part), corners[t])
        size *= 2
    top, bottom = pl.ds(0, HALF), pl.ds(HALF, HALF)
    x_ref[top, top] = corners[0]
    x_ref[top, bottom] = jnp.zeros((HALF, HALF), jnp.float32)
    x_ref[bottom, top] = -fine_dot(fine_dot(corners[1], d_ref[bottom, top]), corners[0])
    x_ref[bottom, bottom] = corners[1]


def invert(matrix):
    return pl.pallas_call(
        inverse_kernel,
        out_shape=jax.ShapeDtypeStruct((NB, NB), jnp.float32),
        in_specs=[pl.BlockSpec(memory_space=pltpu.VMEM)],
        out_specs=pl.BlockSpec(memory_space=pltpu.VMEM),
        scratch_shapes=[pltpu.VMEM((NB, TILE), jnp.float32), pltpu.VMEM((NB, TILE), jnp.float32)],
        compiler_params=pltpu.CompilerParams(vmem_limit_bytes=32 * 1024 * 1024),
        cost_estimate=pl.CostEstimate(flops=20 * 2 * HALF**3 * 6, bytes_accessed=2 * 4 * NB * NB, transcendentals=0),
        name="invert",
    )(matrix)


class Grid:
    def __init__(self):
        self.row_count = lax.axis_size("row")
        self.col_count = lax.axis_size("col")
        self.row = lax.axis_index("row")
        self.col = lax.axis_index("col")
        self.odd = self.row % 2 == 1
        self.paired = self.row_count == 8

    def send(self, value, pairs):
        count = self.col_count
        flat = [(a[0] * count + a[1], b[0] * count + b[1]) for a, b in pairs]
        return lax.ppermute(value, ("row", "col"), flat)

    def within(self, value, moves, planes):
        return self.send(value, [((a, c), (b, c)) for c in planes for a, b in moves])

    def down(self, value, rows, planes):
        return self.send(value, [((r, c), (r, c - 1)) for c in planes for r in rows])

    def is_row(self, *rows):
        return functools.reduce(jnp.logical_or, [self.row == r for r in rows])


def spread(grid, carry, root):
    planes = range(grid.col_count)
    if not grid.paired:
        bit = 1
        while bit < grid.row_count:
            carry = carry + grid.within(carry, [(root ^ m, root ^ m ^ bit) for m in range(bit)], planes)
            bit *= 2
        return carry
    base = root & ~1
    for moves in (((0, 4), (1, 3)), ((4, 6), (3, 7), (1, 5), (0, 2))):
        carry = carry + grid.within(carry, [(a ^ base, b ^ base) for a, b in moves], planes)
    other = grid.within(carry, [(r, r ^ 1) for r in range(grid.row_count)], planes)
    upper = jnp.where(grid.odd, other, carry)
    lower = jnp.where(grid.odd, carry, other)
    return jnp.concatenate([upper, lower], axis=0)


def gather_sum(grid, part, roots):
    if not roots:
        return jnp.zeros_like(part)
    chosen = functools.reduce(
        jnp.logical_or, [(grid.col == c) & (grid.row == root) for c, root in roots.items()]
    )

    def pairs(moves):
        return [((a ^ (root & ~1), c), (b ^ (root & ~1), c)) for c, root in roots.items() for a, b in moves]

    if not grid.paired:
        bit = grid.row_count // 2
        while bit:
            part = part + grid.send(
                part,
                [((root ^ m ^ bit, c), (root ^ m, c)) for c, root in roots.items() for m in range(bit)],
            )
            bit //= 2
        return jnp.where(chosen, part, 0.0)
    half = part.shape[0] // 2
    upper, lower = part[:half], part[half:]
    swapped = grid.send(
        jnp.where(grid.odd, upper, lower),
        [((r, c), (r ^ 1, c)) for c in roots for r in range(grid.row_count)],
    )
    carry = jnp.where(grid.odd, lower, upper) + swapped
    carry = carry + grid.send(carry, pairs(((6, 4), (7, 3), (5, 1), (2, 0))))
    carry = carry + grid.send(carry, pairs(((4, 0), (3, 1))))
    other = grid.send(carry, [((root ^ 1, c), (root, c)) for c, root in roots.items()])
    carry = jnp.where(chosen, carry, 0.0)
    return jnp.concatenate(
        [jnp.where(grid.odd, other, carry), jnp.where(grid.odd, carry, other)], axis=0
    )


def adjoint_of(diag_factor, diag_cot, inverse):
    inner = lower_half(mm_t(diag_factor, jnp.tril(diag_cot)))
    return lower_half(mm(mm_t(inverse, inner), inverse))


def general(grid, saved_factor, cotangent):
    row, col = grid.row, grid.col
    last, near = grid.col_count - 1, grid.col_count - 2
    planes = list(range(grid.col_count))
    solved_rows = range(NP, grid.row_count)
    below = row >= NP

    if grid.paired:
        mine = jnp.where(grid.odd, saved_factor[HALF:], saved_factor[:HALF])
        given = jnp.where(grid.odd, saved_factor[:HALF], saved_factor[HALF:])
        mate = grid.within(given, [(r, r ^ 1) for r in range(NP)], planes)
        seeds = [
            jnp.where(row == root, mine, jnp.where(row == root ^ 1, mate, 0.0)) for root in (2, 1, 0)
        ]
    else:
        seeds = [jnp.where(row == root, saved_factor, 0.0) for root in (2, 1, 0)]
    strip0_right = spread(grid, seeds[0][:, NB:], 2)
    strip0_left = spread(grid, seeds[0][:, :NB], 2)
    strip1_left = spread(grid, seeds[1][:, :NB], 1)
    strip1_right = spread(grid, seeds[1][:, NB:], 1)
    strip2 = spread(grid, seeds[2], 0)
    strip2_right = strip2[:, NB:]

    first_inverse = invert(strip0_right)
    second_diag = jnp.where(col == last, strip1_left, strip2_right)
    second_inverse = invert(second_diag)

    solved0 = mm(cotangent[:, NB:], first_inverse)
    solved1 = mm(cotangent[:, :NB] - mm(solved0, strip0_left), second_inverse)
    starts = {1: solved0, 2: solved1}

    steps = last + NP
    held = {}
    running = cotangent
    came = None
    state = {}
    for step in range(1, steps + 1):
        if step in starts:
            now = jnp.where(below & (col == last), starts[step], 0.0)
            if came is not None:
                now = now + came
        elif step == 4:
            solved2 = mm(
                cotangent[:, NB:] - mm(held[2], strip0_right) - mm(held[3], strip1_right),
                second_inverse,
            )
            now = jnp.where(below & (col == near), solved2, 0.0)
            if came is not None:
                now = now + came
        else:
            now = came
        held[step] = now
        which = {c: step - 1 - (last - c) for c in planes}
        roots = {
            c: 2 - k for c, k in which.items() if 0 <= k < NP and not (c == last and k == 2)
        }
        onward = [c for c in roots if c > 0]
        came = grid.down(now, solved_rows, onward) if onward else jnp.zeros_like(now)
        running = running - gather_sum(grid, mm_t(now, saved_factor), roots)
        if step == 1:
            adj0 = adjoint_of(strip0_right, running[:, NB:], first_inverse)
            sym0 = adj0 + adj0.T
            cross = mm(running[:, :NB] - mm(sym0, strip0_left), second_inverse)
            crossed = grid.send(cross, [((2, last), (1, last))])
        if step == 2:
            adj1 = adjoint_of(
                second_diag, running[:, :NB] - mm_t(crossed, strip0_left), second_inverse
            )
            sym1 = adj1 + adj1.T

    blocks = []
    for k in range(NP):
        block = held[k + 1]
        for hop in range(1, grid.col_count):
            if k + 1 + hop in held:
                block = jnp.where(col == last - hop, held[k + 1 + hop], block)
        blocks.append(block)

    hop0 = grid.send(sym0, [((2, last), (2, near))])
    hop1 = grid.send(cross, [((2, last), (2, near))])
    hop2 = grid.send(crossed, [((1, last), (1, near))])
    hop3 = grid.send(sym1, [((1, last), (1, near))])
    left0 = hop0 + hop2.T
    left1 = hop1 + hop3
    cross2 = mm(
        running[:, NB:] - mm(left0, strip0_right) - mm(left1, strip1_right), second_inverse
    )
    from2 = grid.send(cross2, [((2, near), (0, near))])
    from1 = grid.send(cross2, [((1, near), (0, near))])
    adj2 = adjoint_of(
        strip2_right,
        running[:, NB:] - mm_t(from2, strip0_right) - mm_t(from1, strip1_right),
        second_inverse,
    )
    sym2 = adj2 + adj2.T
    if near > 0:
        pair = jnp.stack([hop0 + hop2, hop1 + hop3])
        total = pair
        late = jnp.where(row == 0, from2, cross2)
        late_total = late
        square = sym2
        square_total = sym2
        for c in range(near, 0, -1):
            pair = grid.down(pair, (1, 2), [c])
            total = total + pair
            late = grid.down(late, (0, 1, 2), [c])
            late_total = jnp.where(col == near, late_total, 0.0) + late if c == near else late_total + late
            square = grid.down(square, (0,), [c])
            square_total = (
                jnp.where(col == near, square_total, 0.0) + square if c == near else square_total + square
            )
        mate = grid.within(late_total, [(1, 0)], range(near))
        other = jnp.where(col == near, from1, mate)
    else:
        total = jnp.stack([hop0 + hop2, hop1 + hop3])
        late_total = jnp.where(row == 0, from2, cross2)
        square_total = sym2
        other = from1
    blocks[0] = jnp.where(
        below, blocks[0], jnp.where(row == 2, total[0], jnp.where(row == 1, total[0], late_total).T)
    )
    blocks[1] = jnp.where(below, blocks[1], jnp.where(row == 0, other.T, total[1]))
    blocks[2] = jnp.where(below, blocks[2], jnp.where(row == 0, square_total, late_total))

    result = running
    strips = (
        jnp.concatenate([strip0_left, strip0_right], axis=1),
        jnp.concatenate([strip1_left, strip1_right], axis=1),
        strip2,
    )
    for block, strip in zip(blocks, strips):
        result = result - mm(block, strip)

    right = jnp.where(
        col == last,
        jnp.where(below, held[1], jnp.where(row == 2, adj0, cotangent[:, NB:])),
        jnp.where(
            col == near,
            jnp.where(row == 0, adj2, blocks[2]),
            result[:, NB:],
        ),
    )
    left = jnp.where(
        col == last,
        jnp.where(
            below,
            held[2],
            jnp.where(row == 2, cross, jnp.where(row == 1, adj1, cotangent[:, :NB])),
        ),
        result[:, :NB],
    )
    return jnp.concatenate([left, right], axis=1)


def split(value):
    high = value.astype(jnp.bfloat16)
    return high, (value - high.astype(jnp.float32)).astype(jnp.bfloat16)


def dot3(left, right):
    (lh, ll), (rh, rl) = left, right
    dot = functools.partial(jnp.dot, preferred_element_type=jnp.float32)
    return dot(lh, rh) + (dot(lh, rl) + dot(ll, rh))


def dots(left, right):
    return dot3(split(left), split(right))


SQUARE = (NB, NB)
FLAT = (HALF, NB)


def gated(kernel, bit, clear, ins, outs):
    def body(flags, *refs):
        given, results = refs[:ins], refs[ins : ins + outs]
        here = refs[ins + outs : 2 * ins + outs]
        staged = refs[2 * ins + outs : 2 * ins + 2 * outs] if not clear else results
        extra = refs[2 * ins + (1 if clear else 2) * outs : -1]
        sems = refs[-1]

        @pl.when(flags[bit] == 1)
        def _():
            copies = [pltpu.make_async_copy(a, b, sems.at[k]) for k, (a, b) in enumerate(zip(given, here))]
            for copy in copies:
                copy.start()
            for copy in copies:
                copy.wait()
            kernel(flags, *here, *staged, *extra)
            if not clear:
                copies = [
                    pltpu.make_async_copy(a, b, sems.at[k]) for k, (a, b) in enumerate(zip(staged, results))
                ]
                for copy in copies:
                    copy.start()
                for copy in copies:
                    copy.wait()

        if clear:

            @pl.when(flags[bit] == 0)
            def _():
                for out in results:
                    out[...] = jnp.zeros_like(out)

    return body


def on_chip(kernel, outs, flags, ins, scratch=(), name=None, bit=None, clear=False):
    lazy = bit is not None
    work = [pltpu.VMEM(s, jnp.float32) for s in scratch]
    if lazy:
        kernel = gated(kernel, bit, clear, len(ins), len(outs))
        staged = [] if clear else [pltpu.VMEM(s, jnp.float32) for s in outs]
        work = [pltpu.VMEM(x.shape, jnp.float32) for x in ins] + staged + work
        work += [pltpu.SemaphoreType.DMA((max(len(ins), len(outs)),))]
    inside = pl.ANY if lazy else pltpu.VMEM
    outside = pl.ANY if lazy and not clear else pltpu.VMEM
    result = pl.pallas_call(
        kernel,
        out_shape=[jax.ShapeDtypeStruct(s, jnp.float32) for s in outs],
        in_specs=[pl.BlockSpec(memory_space=pltpu.SMEM)]
        + [pl.BlockSpec(memory_space=inside)] * len(ins),
        out_specs=[pl.BlockSpec(memory_space=outside)] * len(outs),
        scratch_shapes=work,
        compiler_params=pltpu.CompilerParams(vmem_limit_bytes=48 * 1024 * 1024),
        cost_estimate=pl.CostEstimate(flops=0, bytes_accessed=0, transcendentals=0),
        name=name,
    )(flags, *ins)
    return result[0] if len(outs) == 1 else result


ODD, SIDE, TOP, NEXT, ROW, COL, PICK, HEAD, CROSS, FOOT, LOW, LOWEST, MID, LAST, TOP_ALL, NEXT_ALL, UPTO, NEAR, HEAD1, HIGH_ALL = range(20)
UPPER, LOWER = pl.ds(0, HALF), pl.ds(HALF, HALF)
LEFT, RIGHT = pl.ds(0, NB), pl.ds(NB, NB)


def assemble_kernel(flags, own, own_mate, got, got_mate, zero, one):
    here = pl.multiple_of(flags[ODD] * HALF, HALF)
    there = pl.multiple_of((1 - flags[ODD]) * HALF, HALF)

    @pl.when(flags[SIDE] == 1)
    def _():
        zero[pl.ds(here, HALF), :] = own[...]
        zero[pl.ds(there, HALF), :] = own_mate[...]
        one[pl.ds(here, HALF), :] = got[...]
        one[pl.ds(there, HALF), :] = got_mate[...]

    @pl.when(flags[SIDE] == 0)
    def _():
        one[pl.ds(here, HALF), :] = own[...]
        one[pl.ds(there, HALF), :] = own_mate[...]
        zero[pl.ds(here, HALF), :] = got[...]
        zero[pl.ds(there, HALF), :] = got_mate[...]


def pick_kernel(flags, factor, mate, early, later, third, fourth):
    for root, source, span in ((2, factor, UPPER), (3, mate, LOWER)):

        @pl.when(flags[ROW] == root)
        def _(source=source, span=span):
            early[...] = source[span, RIGHT]
            later[...] = source[span, LEFT]

    for root, one, two, span in ((0, mate, factor, UPPER), (1, factor, mate, LOWER)):

        @pl.when(flags[ROW] == root)
        def _(one=one, two=two, span=span):
            later[...] = one[span, RIGHT]
            third[...] = one[span, LEFT]
            fourth[...] = two[span, LEFT]

        @pl.when((flags[ROW] == root) & (flags[COL] == 3))
        def _(one=one, span=span):
            early[...] = one[span, LEFT]

        @pl.when((flags[ROW] == root) & (flags[COL] < 3))
        def _(two=two, span=span):
            early[...] = two[span, RIGHT]


def join_kernel(flags, own, mate, *outs):
    here = pl.multiple_of(flags[ODD] * HALF, HALF)
    there = pl.multiple_of((1 - flags[ODD]) * HALF, HALF)
    for k, out in enumerate(outs):
        span = pl.ds(k * NB, NB)
        out[pl.ds(here, HALF), :] = own[:, span]
        out[pl.ds(there, HALF), :] = mate[:, span]


def first_kernel(flags, cotangent, inverse, out):
    out[...] = dots(cotangent[:, RIGHT], inverse[...])


def second_kernel(flags, cotangent, inverse, block0, strip, out):
    value = cotangent[:, LEFT] - dots(block0[...], strip[...])
    out[...] = dots(value, inverse[...])


def third_kernel(flags, cotangent, inverse, block0, strip0, block1, strip1, out):
    value = cotangent[:, RIGHT] - dots(block0[...], strip0[...])
    value = value - dots(block1[...], strip1[...])
    out[...] = dots(value, inverse[...])


def share_kernel(flags, now, factor, keep, give, turned):
    turned[...] = now[...].T
    here = pl.multiple_of(flags[ODD] * HALF, HALF)
    there = pl.multiple_of((1 - flags[ODD]) * HALF, HALF)
    parts = split(factor[...])
    keep[...] = dot3(split(turned[pl.ds(here, HALF), :]), parts)
    give[...] = dot3(split(turned[pl.ds(there, HALF), :]), parts)


def tri(matrix, scale):
    rows = lax.broadcasted_iota(jnp.int32, matrix.shape, 0)
    cols = lax.broadcasted_iota(jnp.int32, matrix.shape, 1)
    return jnp.where(rows > cols, matrix, jnp.where(rows == cols, scale * matrix, 0.0))


def adjoint_in(diag_factor, diag_cot, inverse, adj, sym, hold):
    hold[...] = tri(dots(diag_factor[...].T, tri(diag_cot, 1.0)), 0.5)
    hold[...] = dots(inverse[...].T, hold[...])
    value = tri(dots(hold[...], inverse[...]), 0.5)
    adj[...] = value
    sym[...] = value + value.T


def adjoint0_kernel(
    flags, total, mate, cotangent, diag_factor, strip, inverse, next_inverse, adj, sym, cross, turned, hold
):
    hold[UPPER, :] = cotangent[UPPER, RIGHT] - total[:, RIGHT]
    hold[LOWER, :] = cotangent[LOWER, RIGHT] - mate[:, RIGHT]
    adjoint_in(diag_factor, hold[...], inverse, adj, sym, hold)
    hold[UPPER, :] = cotangent[UPPER, LEFT] - total[:, LEFT]
    hold[LOWER, :] = cotangent[LOWER, LEFT] - mate[:, LEFT]
    hold[...] = hold[...] - dots(sym[...], strip[...])
    value = dots(hold[...], next_inverse[...])
    cross[...] = value
    turned[...] = value.T


def adjoint1_kernel(flags, total, mate, cotangent, turned, strip, diag_factor, inverse, adj, sym, hold):
    hold[UPPER, :] = cotangent[UPPER, LEFT] - mate[:, LEFT]
    hold[LOWER, :] = cotangent[LOWER, LEFT] - total[:, LEFT]
    hold[...] = hold[...] - dots(turned[...], strip[...])
    adjoint_in(diag_factor, hold[...], inverse, adj, sym, hold)


def adjoint2_kernel(
    flags, upper, lower, total, mate, from2, from1, strip0, strip1, diag_factor, inverse, adj, packed, hold, sym
):
    hold[UPPER, :] = upper[:, RIGHT] - total[:, RIGHT]
    hold[LOWER, :] = lower[:, RIGHT] - mate[:, RIGHT]
    hold[...] = hold[...] - dots(from2[...].T, strip0[...])
    hold[...] = hold[...] - dots(from1[...].T, strip1[...])
    adjoint_in(diag_factor, hold[...], inverse, adj, sym, hold)
    packed[:, pl.ds(0, HALF)] = sym[UPPER, pl.ds(0, HALF)]
    packed[:, pl.ds(HALF, HALF)] = sym[LOWER, pl.ds(0, HALF)]
    packed[:, pl.ds(2 * HALF, HALF)] = sym[LOWER, pl.ds(HALF, HALF)]


def cross_kernel(flags, upper, lower, total, mate, inverse, left0, strip0, left1, strip1, out, hold):
    hold[UPPER, :] = upper[:, RIGHT]
    hold[LOWER, :] = lower[:, RIGHT]

    @pl.when(flags[ROW] == 1)
    def _():
        hold[UPPER, :] = hold[UPPER, :] - mate[:, RIGHT]
        hold[LOWER, :] = hold[LOWER, :] - total[:, RIGHT]

    value = hold[...] - dots(left0[...], strip0[...])
    value = value - dots(left1[...], strip1[...])
    out[...] = dots(value, inverse[...])


EARLY = (
    "now1", "now2", "now3", "now4", "now5", "own0", "own1", "own0_b", "own1_b", "own0_c", "own1_c",
    "from2", "from1", "over2", "over1",
)
LATE = (
    "now1", "now2", "now4", "now5", "now6", "late", "late_b", "late_c", "sym2", "sym_b", "sym_c",
    "adj0", "cross", "adj1", "adj2", "cotangent",
)


def start_kernel(flags, upper, lower, left0, left1, right0, right1, *refs):
    given = dict(zip(EARLY, refs[: len(EARLY)]))
    out, block, high, low, sems = refs[len(EARLY) :]
    step = pl.program_id(0)
    row, col = flags[ROW], flags[COL]
    blocks = {
        "solved": (("now4", "now5"), ("now3", "now4"), ("now2", "now3")),
        "strip": (("own0_c", "own1_c"), ("own0_b", "own1_b"), ("own0", "own1")),
        "foot": (("over2", "over1"), ("over2", "over1"), ("from2", "from1")),
    }
    kinds = {"solved": row >= NP, "strip": (row == 1) | (row == 2), "foot": row == 0}

    def fetch(kind, plane):
        copies = [
            pltpu.make_async_copy(given[name], block.at[k], sems.at[k])
            for k, name in enumerate(blocks[kind][plane])
        ]
        for copy in copies:
            copy.start()
        for copy in copies:
            copy.wait()
        for k in range(2):
            span = pl.ds(k * NB, NB)
            high[:, span], low[:, span] = split(block[k].T if kind == "foot" else block[k])

    @pl.when(step == 0)
    def _():
        for kind, holds in kinds.items():
            for plane in range(3):

                @pl.when(holds & (col == plane))
                def _(kind=kind, plane=plane):
                    fetch(kind, plane)

    def updated(strips):
        parts = [split(strip[...]) for strip in strips]
        for span, base in ((UPPER, upper), (LOWER, lower)):
            value = base[...]
            for k, part in enumerate(parts):
                left = (high[span, pl.ds(k * NB, NB)], low[span, pl.ds(k * NB, NB)])
                value = value - dot3(left, part)
            out[span, :] = value

    @pl.when((step < 2) & (col < 3))
    def _():
        updated((left0, left1))

    @pl.when((step >= 2) & (col < 2))
    def _():
        updated((right0, right1))


def finish_kernel(flags, started, total, mate, left2, right2, *refs):
    given = dict(zip(LATE, refs[: len(LATE)]))
    out, block, packed, high, low, sem, out_sem = refs[len(LATE) :]
    step = pl.program_id(0)
    row, col = flags[ROW], flags[COL]
    blocks = {
        "solved": ("now6", "now5", "now4"),
        "strip": ("late_c", "late_b", "late"),
        "foot": ("sym_c", "sym_b", "sym2"),
    }
    kinds = {"solved": row >= NP, "strip": (row == 1) | (row == 2), "foot": row == 0}

    def fetch(kind, name):
        copy = pltpu.make_async_copy(given[name], packed if kind == "foot" else block, sem)
        copy.start()
        copy.wait()
        if kind == "foot":
            block[UPPER, pl.ds(0, HALF)] = packed[:, pl.ds(0, HALF)]
            block[LOWER, pl.ds(0, HALF)] = packed[:, pl.ds(HALF, HALF)]
            block[UPPER, pl.ds(HALF, HALF)] = packed[:, pl.ds(HALF, HALF)].T
            block[LOWER, pl.ds(HALF, HALF)] = packed[:, pl.ds(2 * HALF, HALF)]
        high[...], low[...] = split(block[...])

    @pl.when(step == 0)
    def _():
        for kind, holds in kinds.items():
            for plane in range(3):

                @pl.when(holds & (col == plane))
                def _(kind=kind, plane=plane):
                    fetch(kind, blocks[kind][plane])

    def updated(strip):
        out[...] = started[...] - dot3((high[...], low[...]), split(strip[...]))

        @pl.when((row == 0) & (col == 0))
        def _():
            out[UPPER, :] = out[UPPER, :] - total[...]
            out[LOWER, :] = out[LOWER, :] - mate[...]

    def moved(name, offset):
        column = pl.multiple_of(lax.rem(step, 2) * HALF + offset, HALF)
        copy = pltpu.make_async_copy(given[name].at[:, pl.ds(column, HALF)], out, out_sem)
        copy.start()
        copy.wait()

    def take(holds, name, offset=0):
        @pl.when(holds)
        def _():
            moved(name, offset)

    @pl.when((step < 2) & (col == 3))
    def _():
        take(row >= NP, "now2")
        take(row == 2, "cross")
        take(row == 1, "adj1")
        take(row == 0, "cotangent")

    @pl.when((step >= 2) & (col == 3))
    def _():
        take(row >= NP, "now1")
        take(row == 2, "adj0")
        take(row < 2, "cotangent", NB)

    @pl.when((step >= 2) & (col == 2))
    def _():
        take(row >= NP, "now4")
        take(row == 0, "adj2")
        take((row == 1) | (row == 2), "late")

    @pl.when((step < 2) & (col < 3))
    def _():
        updated(left2)

    @pl.when((step >= 2) & (col < 2))
    def _():
        updated(right2)


LEFT_SPEC = pl.BlockSpec((NB, HALF), lambda j: (0, jnp.minimum(j, 1)))
RIGHT_SPEC = pl.BlockSpec((NB, HALF), lambda j: (0, jnp.maximum(j - 2, 0)))
WIDE_SPEC = pl.BlockSpec((HALF, HALF), lambda j: (0, j))
TALL_SPEC = pl.BlockSpec((NB, HALF), lambda j: (0, j))


def by_columns(kernel, name, flags, specs, ins, later, scratch):
    return pl.pallas_call(
        kernel,
        grid=(4,),
        out_shape=jax.ShapeDtypeStruct((NB, 2 * NB), jnp.float32),
        in_specs=[pl.BlockSpec(memory_space=pltpu.SMEM)]
        + specs
        + [pl.BlockSpec(memory_space=pl.ANY)] * len(later),
        out_specs=TALL_SPEC,
        scratch_shapes=scratch,
        compiler_params=pltpu.CompilerParams(vmem_limit_bytes=48 * 1024 * 1024),
        cost_estimate=pl.CostEstimate(flops=0, bytes_accessed=0, transcendentals=0),
        name=name,
    )(flags, *ins, *later)


def placed(grid, saved_factor, cotangent):
    row, col = grid.row, grid.col
    planes = range(4)
    below = row >= NP
    side = (row // 2) % 2 == 1
    parts = [grid.odd, side, below & (col == 3), below & (col == 2), row, col, col == 1]
    parts += [(row == 2) & (col == 3), ((row == 1) | (row == 2)) & (col == 2), (row == 0) & (col == 2)]
    parts += [below & (col <= 2), below & (col <= 1), below & ((col == 1) | (col == 2)), below & (col == 0)]
    parts += [col == 3, col == 2, below & (col >= 2), row < 4, (row == 1) & (col == 3), col >= 2]
    flags = jnp.stack([jnp.asarray(p).astype(jnp.int32) for p in parts])

    def core(value):
        return grid.within(value, [(r, r ^ 1) for r in range(8)], planes)

    def down(value, *sources, cut=False):
        if not cut:
            return grid.down(value, range(NP, 8), sources)
        upper, lower = value[:HALF], value[HALF:]
        upper = grid.down(upper, range(NP, 8), sources)
        upper, lower = fence(upper, lower)
        lower = grid.down(lower, range(NP, 8), sources)
        return jnp.concatenate([upper, lower], axis=0)

    def own_from(value, source, target):
        return grid.send(value, [((r, source), (r, target)) for r in (1, 2)])

    def moves(roots, pairs):
        return [((a ^ (root & ~1), c), (b ^ (root & ~1), c)) for c, root in roots.items() for a, b in pairs]

    def inward(value, roots):
        pairs = moves(roots, ((6, 4), (7, 3), (5, 1)))
        pairs += [((2, c), (0, c)) for c, root in roots.items() if root < 2]
        return value + grid.send(value, pairs)

    def home(value, roots):
        return value + grid.send(value, moves(roots, ((4, 0), (3, 1))))

    def settle(running, total, mate, roots):
        upper, lower = running
        chosen = functools.reduce(
            jnp.logical_or, [(col == c) & (row == root) for c, root in roots.items()]
        )
        upper = upper - jnp.where(chosen, jnp.where(grid.odd, mate, total), 0.0)
        lower = lower - jnp.where(chosen, jnp.where(grid.odd, total, mate), 0.0)
        return upper, lower

    def share(now, bit, before):
        keep, give = on_chip(
            share_kernel, [(HALF, 2 * NB)] * 2, flags, (now, saved_factor), [SQUARE], "share", bit, True
        )
        if before:
            now, keep, give = fence(now, keep, give)
        return now, keep + core(give)

    def inverted(matrix, bit):
        def kernel(flags, *refs):
            inverse_kernel(*refs)

        return on_chip(kernel, [SQUARE], flags, (matrix,), [(NB, TILE)] * 2, "invert", bit)

    def solve(kernel, bit, *ins):
        return on_chip(kernel, [SQUARE], flags, ins, (), "solve", bit, True)

    def fence(*values):
        return lax.optimization_barrier(values)

    factor = saved_factor

    mate = core(factor)
    early, later, third, fourth = on_chip(
        pick_kernel, [FLAT] * 4, flags, (factor, mate), name="pick", bit=NEAR
    )
    near = row < 4

    def away(mine):
        return grid.within(mine, [(r, r ^ 4) for r in range(4)], planes)

    def both(own):
        got = grid.within(own, [(r, r ^ 2) for r in range(8)], planes)
        return on_chip(
            assemble_kernel, [SQUARE] * 2, flags, (own, core(own), got, core(got)), name="assemble"
        )

    got_early = away(early)
    own_early = jnp.where(near, early, got_early)
    later, own_early = fence(later, own_early)
    got_later = away(later)
    strip0_right, diag1 = both(own_early)
    own_later = jnp.where(near, later, got_later)
    strip0_left, strip1_right = both(own_later)

    def tied(value, *others):
        return fence(value, *others)[0]

    inverse0 = inverted(strip0_right, TOP_ALL)
    now1 = solve(first_kernel, TOP, cotangent, inverse0)

    def spread_out(last):
        return jnp.where(near, last, grid.within(last, [(0, 4), (1, 5)], range(3)))

    def spread_on(own):
        got = grid.within(own, [(0, 2), (1, 3), (4, 6), (5, 7)], range(3))
        own = jnp.where(side, got, own)
        return on_chip(join_kernel, [SQUARE], flags, (own, core(own)), name="join")


    sums1, sums2, sums3 = {3: 2}, {3: 1, 2: 2}, {2: 1, 1: 2}
    sums4, sums5 = {2: 0, 1: 1, 0: 2}, {1: 0, 0: 1}
    to_foot = [((2, c), (0, c)) for c in range(3)]
    to_foot_core = [((1, c), (0, c)) for c in range(3)]
    now1_on, sum1 = share(now1, TOP, False)
    came1 = down(now1_on, 3, cut=False)
    inverse1 = inverted(diag1, HIGH_ALL)
    held_inverse1 = inverse1
    solved1 = solve(second_kernel, TOP, cotangent, inverse1, now1, strip0_left)
    held_solved1 = solved1
    sum1 = inward(tied(sum1, held_solved1), sums1)
    now2 = solved1 + came1
    held_now2 = now2

    own3 = spread_out(third)
    held_own3 = own3
    strip1_left = spread_on(own3)
    held_strip1_left = strip1_left
    own4 = spread_out(fourth)
    held_own4 = own4
    strip2_left = spread_on(own4)

    now2_on, sum2 = share(now2, UPTO, False)
    held_sum2_0 = sum2
    came2 = down(now2_on, 3, 2, cut=False)
    sum1 = home(tied(sum1, held_inverse1, held_sum2_0), sums1)
    mate1 = core(sum1)
    adj0, sym0, cross, turned = on_chip(
        adjoint0_kernel,
        [SQUARE] * 4,
        flags,
        (sum1, mate1, cotangent, strip0_right, strip0_left, inverse0, inverse1),
        [SQUARE],
        "adjoint",
        HEAD,
    )
    crossed = grid.send(turned, [((2, 3), (1, 3))])
    block0 = jnp.where(row == 1, crossed, sym0)
    own0 = own_from(block0, 3, 2)
    held_own0 = own0
    block0 = block0
    own0_b, own0_c = own_from(block0, 3, 1), own_from(block0, 3, 0)
    sum2 = inward(tied(sum2, held_own4), sums2)
    now3 = came2
    solved2 = solve(third_kernel, NEXT, cotangent, inverse1, now2, strip0_right, now3, strip1_right)
    held_solved2 = solved2


    now3_on, sum3 = share(now3, MID, False)
    came3 = down(now3_on, 2, 1, cut=False)
    sum2 = home(tied(sum2, held_own3, held_strip1_left), sums2)
    mate2 = core(sum2)
    adj1, sym1 = on_chip(
        adjoint1_kernel,
        [SQUARE] * 2,
        flags,
        (sum2, mate2, cotangent, crossed, strip0_left, diag1, inverse1),
        [SQUARE],
        "adjoint",
        HEAD1,
    )
    held_sym1 = sym1
    block1 = jnp.where(row == 1, sym1, cross)
    own1 = own_from(block1, 3, 2)
    block1 = block1
    own1_b, own1_c = own_from(block1, 3, 1), own_from(block1, 3, 0)
    held_own0_b = own0_b
    held_own0_c = own0_c
    held_own1_b = own1_b
    held_own1_c = own1_c
    chosen = (row == 2) & (col == 2)
    running = (
        cotangent[:HALF] - jnp.where(chosen, sum2, 0.0),
        cotangent[HALF:] - jnp.where(chosen, mate2, 0.0),
    )
    sum3 = inward(sum3, sums3)
    now4 = solved2 + came3


    now4_on, sum4 = share(now4, LOW, False)
    held_sum4_0 = sum4
    came4 = down(now4_on, 2, 1, cut=False)
    sum3 = home(tied(sum3, held_sym1, held_sum4_0), sums3)
    mate3 = core(sum3)
    late = on_chip(
        cross_kernel,
        [SQUARE],
        flags,
        (*running, sum3, mate3, inverse1, own0, strip0_right, own1, strip1_right),
        [SQUARE],
        "solve",
        CROSS,
        True,
    )
    held_late = late
    running = settle(running, sum3, mate3, sums3)
    from2, from1 = grid.send(late, to_foot), grid.send(late, to_foot_core)
    late_on = tied(late, held_solved2)
    late_b, late_c = own_from(late_on, 2, 1), own_from(late_on, 2, 0)
    held_late_b = late_b
    held_late_c = late_c
    sum4 = inward(tied(sum4, held_own0_c), sums4)
    now5 = came4

    now5_on, sum5 = share(now5, LOWEST, False)
    held_sum5_0 = sum5
    came5 = down(tied(now5_on, held_sum5_0, held_own0_b), 1, cut=False)
    sum4 = home(tied(sum4, held_late, held_own1_c), sums4)
    mate4 = core(sum4)
    adj2, sym2 = on_chip(
        adjoint2_kernel,
        [SQUARE, (HALF, 3 * HALF)],
        flags,
        (*running, sum4, mate4, from2, from1, strip0_right, strip1_right, diag1, inverse1),
        [SQUARE] * 2,
        "adjoint",
        FOOT,
    )
    running = settle(running, sum4, mate4, sums4)
    sym_b = grid.send(sym2, [((0, 2), (0, 1))])
    sym_c = grid.send(sym2, [((0, 2), (0, 0))])
    late_low = late_b + late_c
    over2, over1 = grid.send(late_low, to_foot), grid.send(late_low, to_foot_core)
    held_over1 = over1
    sum5 = inward(tied(sum5, held_now2), sums5)
    now6 = tied(came5, held_own0)

    _, sum6 = share(now6, LAST, True)
    sum5 = home(sum5, sums5)
    running = settle(running, sum5, core(sum5), sums5)
    here = locals()
    started = by_columns(
        start_kernel,
        "start",
        flags,
        [WIDE_SPEC] * 2 + [LEFT_SPEC] * 2 + [RIGHT_SPEC] * 2,
        (*running, strip0_left, strip1_left, strip0_right, strip1_right),
        [here[name] for name in EARLY],
        [
            pltpu.VMEM((2, NB, NB), jnp.float32),
            pltpu.VMEM((NB, 2 * NB), jnp.bfloat16),
            pltpu.VMEM((NB, 2 * NB), jnp.bfloat16),
            pltpu.SemaphoreType.DMA((2,)),
        ],
    )
    held_started = started
    sum6 = inward(sum6, sums5)
    sum6 = home(tied(sum6, held_late_b, held_late_c), sums5)
    sum6 = tied(sum6, held_own1_b, held_over1, held_started)
    return by_columns(
        finish_kernel,
        "finish",
        flags,
        [TALL_SPEC, WIDE_SPEC, WIDE_SPEC, LEFT_SPEC, RIGHT_SPEC],
        (started, sum6, core(sum6), strip2_left, diag1),
        [here[name] for name in LATE],
        [
            pltpu.VMEM(SQUARE, jnp.float32),
            pltpu.VMEM((HALF, 3 * HALF), jnp.float32),
            pltpu.VMEM(SQUARE, jnp.bfloat16),
            pltpu.VMEM(SQUARE, jnp.bfloat16),
            pltpu.SemaphoreType.DMA,
            pltpu.SemaphoreType.DMA,
        ],
    )


def shards(saved_factor, cotangent):
    grid = Grid()
    if grid.row_count == 8 and grid.col_count == 4:
        return placed(grid, saved_factor, cotangent)
    return general(grid, saved_factor, cotangent)


def solution(mesh):
    placed = (P("row", "col"), P("row", "col"))
    return jax.shard_map(
        shards, mesh=mesh, in_specs=placed, out_specs=P("row", "col"), check_vma=False
    )
```

```python
import functools

import jax
import jax.numpy as jnp
from jax import lax
from jax.experimental import pallas as pl
from jax.experimental.pallas import tpu as pltpu
from jax.sharding import PartitionSpec as P

NB = 512
NP = 3
HALF = NB // 2
BASE = 16
TILE = 128

good = lax.Precision.HIGH


def mm(left, right, precision=good):
    return jnp.dot(left, right, precision=precision, preferred_element_type=jnp.float32)


def mm_t(left, right, precision=good):
    return lax.dot_general(
        left, right, (((0,), (0,)), ((), ())), precision=precision, preferred_element_type=jnp.float32
    )


def lower_half(matrix):
    return jnp.tril(matrix) - 0.5 * jnp.diag(jnp.diag(matrix))


def fine_dot(left, right):
    return dots(left, right)


def inverse_kernel(d_ref, x_ref, tiles, base):
    for t in range(NB // TILE):
        span = pl.ds(t * TILE, TILE)
        tiles[span, :] = d_ref[span, span]
    blocks = NB // BASE
    lane = lax.broadcasted_iota(jnp.int32, (blocks, TILE), 1)
    first = lax.rem(lax.broadcasted_iota(jnp.int32, (blocks, TILE), 0), TILE // BASE) * BASE
    place = lane - first
    solved = []
    for i in range(BASE):
        row = tiles[pl.ds(i, blocks, stride=BASE), :]
        acc = jnp.where(place == i, 1.0, 0.0)
        for k in range(i):
            factor = jnp.sum(jnp.where(place == k, row, 0.0), axis=1, keepdims=True)
            acc = acc - factor * solved[k]
        pivot = jnp.sum(jnp.where(place == i, row, 0.0), axis=1, keepdims=True)
        solved.append(acc / pivot)
        base[pl.ds(i, blocks, stride=BASE), :] = solved[i]
    rows = lax.broadcasted_iota(jnp.int32, (HALF, HALF), 0)
    cols = lax.broadcasted_iota(jnp.int32, (HALF, HALF), 1)
    empty = jnp.zeros((TILE, TILE), jnp.float32)
    corners = []
    for t in range(2):
        top = jnp.concatenate([base[pl.ds(t * HALF, TILE), :], empty], axis=1)
        bottom = jnp.concatenate([empty, base[pl.ds(t * HALF + TILE, TILE), :]], axis=1)
        corners.append(jnp.concatenate([top, bottom], axis=0))
    size = BASE
    while size < HALF:
        below = (rows // (2 * size) == cols // (2 * size)) & (rows // size != cols // size) & (rows > cols)
        for t in range(2):
            span = pl.ds(t * HALF, HALF)
            part = jnp.where(below, d_ref[span, span], 0.0)
            corners[t] = corners[t] - fine_dot(fine_dot(corners[t], part), corners[t])
        size *= 2
    top, bottom = pl.ds(0, HALF), pl.ds(HALF, HALF)
    x_ref[top, top] = corners[0]
    x_ref[top, bottom] = jnp.zeros((HALF, HALF), jnp.float32)
    x_ref[bottom, top] = -fine_dot(fine_dot(corners[1], d_ref[bottom, top]), corners[0])
    x_ref[bottom, bottom] = corners[1]


def invert(matrix):
    return pl.pallas_call(
        inverse_kernel,
        out_shape=jax.ShapeDtypeStruct((NB, NB), jnp.float32),
        in_specs=[pl.BlockSpec(memory_space=pltpu.VMEM)],
        out_specs=pl.BlockSpec(memory_space=pltpu.VMEM),
        scratch_shapes=[pltpu.VMEM((NB, TILE), jnp.float32), pltpu.VMEM((NB, TILE), jnp.float32)],
        compiler_params=pltpu.CompilerParams(vmem_limit_bytes=32 * 1024 * 1024),
        cost_estimate=pl.CostEstimate(flops=20 * 2 * HALF**3 * 6, bytes_accessed=2 * 4 * NB * NB, transcendentals=0),
        name="invert",
    )(matrix)


class Grid:
    def __init__(self):
        self.row_count = lax.axis_size("row")
        self.col_count = lax.axis_size("col")
        self.row = lax.axis_index("row")
        self.col = lax.axis_index("col")
        self.odd = self.row % 2 == 1
        self.paired = self.row_count == 8

    def send(self, value, pairs):
        count = self.col_count
        flat = [(a[0] * count + a[1], b[0] * count + b[1]) for a, b in pairs]
        return lax.ppermute(value, ("row", "col"), flat)

    def within(self, value, moves, planes):
        return self.send(value, [((a, c), (b, c)) for c in planes for a, b in moves])

    def down(self, value, rows, planes):
        return self.send(value, [((r, c), (r, c - 1)) for c in planes for r in rows])

    def is_row(self, *rows):
        return functools.reduce(jnp.logical_or, [self.row == r for r in rows])


def spread(grid, carry, root):
    planes = range(grid.col_count)
    if not grid.paired:
        bit = 1
        while bit < grid.row_count:
            carry = carry + grid.within(carry, [(root ^ m, root ^ m ^ bit) for m in range(bit)], planes)
            bit *= 2
        return carry
    base = root & ~1
    for moves in (((0, 4), (1, 3)), ((4, 6), (3, 7), (1, 5), (0, 2))):
        carry = carry + grid.within(carry, [(a ^ base, b ^ base) for a, b in moves], planes)
    other = grid.within(carry, [(r, r ^ 1) for r in range(grid.row_count)], planes)
    upper = jnp.where(grid.odd, other, carry)
    lower = jnp.where(grid.odd, carry, other)
    return jnp.concatenate([upper, lower], axis=0)


def gather_sum(grid, part, roots):
    if not roots:
        return jnp.zeros_like(part)
    chosen = functools.reduce(
        jnp.logical_or, [(grid.col == c) & (grid.row == root) for c, root in roots.items()]
    )

    def pairs(moves):
        return [((a ^ (root & ~1), c), (b ^ (root & ~1), c)) for c, root in roots.items() for a, b in moves]

    if not grid.paired:
        bit = grid.row_count // 2
        while bit:
            part = part + grid.send(
                part,
                [((root ^ m ^ bit, c), (root ^ m, c)) for c, root in roots.items() for m in range(bit)],
            )
            bit //= 2
        return jnp.where(chosen, part, 0.0)
    half = part.shape[0] // 2
    upper, lower = part[:half], part[half:]
    swapped = grid.send(
        jnp.where(grid.odd, upper, lower),
        [((r, c), (r ^ 1, c)) for c in roots for r in range(grid.row_count)],
    )
    carry = jnp.where(grid.odd, lower, upper) + swapped
    carry = carry + grid.send(carry, pairs(((6, 4), (7, 3), (5, 1), (2, 0))))
    carry = carry + grid.send(carry, pairs(((4, 0), (3, 1))))
    other = grid.send(carry, [((root ^ 1, c), (root, c)) for c, root in roots.items()])
    carry = jnp.where(chosen, carry, 0.0)
    return jnp.concatenate(
        [jnp.where(grid.odd, other, carry), jnp.where(grid.odd, carry, other)], axis=0
    )


def adjoint_of(diag_factor, diag_cot, inverse):
    inner = lower_half(mm_t(diag_factor, jnp.tril(diag_cot)))
    return lower_half(mm(mm_t(inverse, inner), inverse))


def general(grid, saved_factor, cotangent):
    row, col = grid.row, grid.col
    last, near = grid.col_count - 1, grid.col_count - 2
    planes = list(range(grid.col_count))
    solved_rows = range(NP, grid.row_count)
    below = row >= NP

    if grid.paired:
        mine = jnp.where(grid.odd, saved_factor[HALF:], saved_factor[:HALF])
        given = jnp.where(grid.odd, saved_factor[:HALF], saved_factor[HALF:])
        mate = grid.within(given, [(r, r ^ 1) for r in range(NP)], planes)
        seeds = [
            jnp.where(row == root, mine, jnp.where(row == root ^ 1, mate, 0.0)) for root in (2, 1, 0)
        ]
    else:
        seeds = [jnp.where(row == root, saved_factor, 0.0) for root in (2, 1, 0)]
    strip0_right = spread(grid, seeds[0][:, NB:], 2)
    strip0_left = spread(grid, seeds[0][:, :NB], 2)
    strip1_left = spread(grid, seeds[1][:, :NB], 1)
    strip1_right = spread(grid, seeds[1][:, NB:], 1)
    strip2 = spread(grid, seeds[2], 0)
    strip2_right = strip2[:, NB:]

    first_inverse = invert(strip0_right)
    second_diag = jnp.where(col == last, strip1_left, strip2_right)
    second_inverse = invert(second_diag)

    solved0 = mm(cotangent[:, NB:], first_inverse)
    solved1 = mm(cotangent[:, :NB] - mm(solved0, strip0_left), second_inverse)
    starts = {1: solved0, 2: solved1}

    steps = last + NP
    held = {}
    running = cotangent
    came = None
    state = {}
    for step in range(1, steps + 1):
        if step in starts:
            now = jnp.where(below & (col == last), starts[step], 0.0)
            if came is not None:
                now = now + came
        elif step == 4:
            solved2 = mm(
                cotangent[:, NB:] - mm(held[2], strip0_right) - mm(held[3], strip1_right),
                second_inverse,
            )
            now = jnp.where(below & (col == near), solved2, 0.0)
            if came is not None:
                now = now + came
        else:
            now = came
        held[step] = now
        which = {c: step - 1 - (last - c) for c in planes}
        roots = {
            c: 2 - k for c, k in which.items() if 0 <= k < NP and not (c == last and k == 2)
        }
        onward = [c for c in roots if c > 0]
        came = grid.down(now, solved_rows, onward) if onward else jnp.zeros_like(now)
        running = running - gather_sum(grid, mm_t(now, saved_factor), roots)
        if step == 1:
            adj0 = adjoint_of(strip0_right, running[:, NB:], first_inverse)
            sym0 = adj0 + adj0.T
            cross = mm(running[:, :NB] - mm(sym0, strip0_left), second_inverse)
            crossed = grid.send(cross, [((2, last), (1, last))])
        if step == 2:
            adj1 = adjoint_of(
                second_diag, running[:, :NB] - mm_t(crossed, strip0_left), second_inverse
            )
            sym1 = adj1 + adj1.T

    blocks = []
    for k in range(NP):
        block = held[k + 1]
        for hop in range(1, grid.col_count):
            if k + 1 + hop in held:
                block = jnp.where(col == last - hop, held[k + 1 + hop], block)
        blocks.append(block)

    hop0 = grid.send(sym0, [((2, last), (2, near))])
    hop1 = grid.send(cross, [((2, last), (2, near))])
    hop2 = grid.send(crossed, [((1, last), (1, near))])
    hop3 = grid.send(sym1, [((1, last), (1, near))])
    left0 = hop0 + hop2.T
    left1 = hop1 + hop3
    cross2 = mm(
        running[:, NB:] - mm(left0, strip0_right) - mm(left1, strip1_right), second_inverse
    )
    from2 = grid.send(cross2, [((2, near), (0, near))])
    from1 = grid.send(cross2, [((1, near), (0, near))])
    adj2 = adjoint_of(
        strip2_right,
        running[:, NB:] - mm_t(from2, strip0_right) - mm_t(from1, strip1_right),
        second_inverse,
    )
    sym2 = adj2 + adj2.T
    if near > 0:
        pair = jnp.stack([hop0 + hop2, hop1 + hop3])
        total = pair
        late = jnp.where(row == 0, from2, cross2)
        late_total = late
        square = sym2
        square_total = sym2
        for c in range(near, 0, -1):
            pair = grid.down(pair, (1, 2), [c])
            total = total + pair
            late = grid.down(late, (0, 1, 2), [c])
            late_total = jnp.where(col == near, late_total, 0.0) + late if c == near else late_total + late
            square = grid.down(square, (0,), [c])
            square_total = (
                jnp.where(col == near, square_total, 0.0) + square if c == near else square_total + square
            )
        mate = grid.within(late_total, [(1, 0)], range(near))
        other = jnp.where(col == near, from1, mate)
    else:
        total = jnp.stack([hop0 + hop2, hop1 + hop3])
        late_total = jnp.where(row == 0, from2, cross2)
        square_total = sym2
        other = from1
    blocks[0] = jnp.where(
        below, blocks[0], jnp.where(row == 2, total[0], jnp.where(row == 1, total[0], late_total).T)
    )
    blocks[1] = jnp.where(below, blocks[1], jnp.where(row == 0, other.T, total[1]))
    blocks[2] = jnp.where(below, blocks[2], jnp.where(row == 0, square_total, late_total))

    result = running
    strips = (
        jnp.concatenate([strip0_left, strip0_right], axis=1),
        jnp.concatenate([strip1_left, strip1_right], axis=1),
        strip2,
    )
    for block, strip in zip(blocks, strips):
        result = result - mm(block, strip)

    right = jnp.where(
        col == last,
        jnp.where(below, held[1], jnp.where(row == 2, adj0, cotangent[:, NB:])),
        jnp.where(
            col == near,
            jnp.where(row == 0, adj2, blocks[2]),
            result[:, NB:],
        ),
    )
    left = jnp.where(
        col == last,
        jnp.where(
            below,
            held[2],
            jnp.where(row == 2, cross, jnp.where(row == 1, adj1, cotangent[:, :NB])),
        ),
        result[:, :NB],
    )
    return jnp.concatenate([left, right], axis=1)


def split(value):
    high = value.astype(jnp.bfloat16)
    return high, (value - high.astype(jnp.float32)).astype(jnp.bfloat16)


def dot3(left, right):
    (lh, ll), (rh, rl) = left, right
    dot = functools.partial(jnp.dot, preferred_element_type=jnp.float32)
    return dot(lh, rh) + (dot(lh, rl) + dot(ll, rh))


def dots(left, right):
    return dot3(split(left), split(right))


SQUARE = (NB, NB)
FLAT = (HALF, NB)


def gated(kernel, bit, clear, ins, outs):
    def body(flags, *refs):
        given, results = refs[:ins], refs[ins : ins + outs]
        here = refs[ins + outs : 2 * ins + outs]
        staged = refs[2 * ins + outs : 2 * ins + 2 * outs] if not clear else results
        extra = refs[2 * ins + (1 if clear else 2) * outs : -1]
        sems = refs[-1]

        @pl.when(flags[bit] == 1)
        def _():
            copies = [pltpu.make_async_copy(a, b, sems.at[k]) for k, (a, b) in enumerate(zip(given, here))]
            for copy in copies:
                copy.start()
            for copy in copies:
                copy.wait()
            kernel(flags, *here, *staged, *extra)
            if not clear:
                copies = [
                    pltpu.make_async_copy(a, b, sems.at[k]) for k, (a, b) in enumerate(zip(staged, results))
                ]
                for copy in copies:
                    copy.start()
                for copy in copies:
                    copy.wait()

        if clear:

            @pl.when(flags[bit] == 0)
            def _():
                for out in results:
                    out[...] = jnp.zeros_like(out)

    return body


def on_chip(kernel, outs, flags, ins, scratch=(), name=None, bit=None, clear=False):
    lazy = bit is not None
    work = [pltpu.VMEM(s, jnp.float32) for s in scratch]
    if lazy:
        kernel = gated(kernel, bit, clear, len(ins), len(outs))
        staged = [] if clear else [pltpu.VMEM(s, jnp.float32) for s in outs]
        work = [pltpu.VMEM(x.shape, jnp.float32) for x in ins] + staged + work
        work += [pltpu.SemaphoreType.DMA((max(len(ins), len(outs)),))]
    inside = pl.ANY if lazy else pltpu.VMEM
    outside = pl.ANY if lazy and not clear else pltpu.VMEM
    result = pl.pallas_call(
        kernel,
        out_shape=[jax.ShapeDtypeStruct(s, jnp.float32) for s in outs],
        in_specs=[pl.BlockSpec(memory_space=pltpu.SMEM)]
        + [pl.BlockSpec(memory_space=inside)] * len(ins),
        out_specs=[pl.BlockSpec(memory_space=outside)] * len(outs),
        scratch_shapes=work,
        compiler_params=pltpu.CompilerParams(vmem_limit_bytes=48 * 1024 * 1024),
        cost_estimate=pl.CostEstimate(flops=0, bytes_accessed=0, transcendentals=0),
        name=name,
    )(flags, *ins)
    return result[0] if len(outs) == 1 else result


ODD, SIDE, TOP, NEXT, ROW, COL, PICK, HEAD, CROSS, FOOT, LOW, LOWEST, MID, LAST, TOP_ALL, NEXT_ALL, UPTO, NEAR, HEAD1, HIGH_ALL = range(20)
UPPER, LOWER = pl.ds(0, HALF), pl.ds(HALF, HALF)
LEFT, RIGHT = pl.ds(0, NB), pl.ds(NB, NB)


def assemble_kernel(flags, own, own_mate, got, got_mate, zero, one):
    here = pl.multiple_of(flags[ODD] * HALF, HALF)
    there = pl.multiple_of((1 - flags[ODD]) * HALF, HALF)

    @pl.when(flags[SIDE] == 1)
    def _():
        zero[pl.ds(here, HALF), :] = own[...]
        zero[pl.ds(there, HALF), :] = own_mate[...]
        one[pl.ds(here, HALF), :] = got[...]
        one[pl.ds(there, HALF), :] = got_mate[...]

    @pl.when(flags[SIDE] == 0)
    def _():
        one[pl.ds(here, HALF), :] = own[...]
        one[pl.ds(there, HALF), :] = own_mate[...]
        zero[pl.ds(here, HALF), :] = got[...]
        zero[pl.ds(there, HALF), :] = got_mate[...]


def pick_kernel(flags, factor, mate, early, later, third, fourth):
    for root, source, span in ((2, factor, UPPER), (3, mate, LOWER)):

        @pl.when(flags[ROW] == root)
        def _(source=source, span=span):
            early[...] = source[span, RIGHT]
            later[...] = source[span, LEFT]

    for root, one, two, span in ((0, mate, factor, UPPER), (1, factor, mate, LOWER)):

        @pl.when(flags[ROW] == root)
        def _(one=one, two=two, span=span):
            later[...] = one[span, RIGHT]
            third[...] = one[span, LEFT]
            fourth[...] = two[span, LEFT]

        @pl.when((flags[ROW] == root) & (flags[COL] == 3))
        def _(one=one, span=span):
            early[...] = one[span, LEFT]

        @pl.when((flags[ROW] == root) & (flags[COL] < 3))
        def _(two=two, span=span):
            early[...] = two[span, RIGHT]


def join_kernel(flags, own, mate, *outs):
    here = pl.multiple_of(flags[ODD] * HALF, HALF)
    there = pl.multiple_of((1 - flags[ODD]) * HALF, HALF)
    for k, out in enumerate(outs):
        span = pl.ds(k * NB, NB)
        out[pl.ds(here, HALF), :] = own[:, span]
        out[pl.ds(there, HALF), :] = mate[:, span]


def first_kernel(flags, cotangent, inverse, out):
    out[...] = dots(cotangent[:, RIGHT], inverse[...])


def second_kernel(flags, cotangent, inverse, block0, strip, out):
    value = cotangent[:, LEFT] - dots(block0[...], strip[...])
    out[...] = dots(value, inverse[...])


def third_kernel(flags, cotangent, inverse, block0, strip0, block1, strip1, out):
    value = cotangent[:, RIGHT] - dots(block0[...], strip0[...])
    value = value - dots(block1[...], strip1[...])
    out[...] = dots(value, inverse[...])


def share_kernel(flags, now, factor, keep, give, turned):
    turned[...] = now[...].T
    here = pl.multiple_of(flags[ODD] * HALF, HALF)
    there = pl.multiple_of((1 - flags[ODD]) * HALF, HALF)
    parts = split(factor[...])
    keep[...] = dot3(split(turned[pl.ds(here, HALF), :]), parts)
    give[...] = dot3(split(turned[pl.ds(there, HALF), :]), parts)


def tri(matrix, scale):
    rows = lax.broadcasted_iota(jnp.int32, matrix.shape, 0)
    cols = lax.broadcasted_iota(jnp.int32, matrix.shape, 1)
    return jnp.where(rows > cols, matrix, jnp.where(rows == cols, scale * matrix, 0.0))


def adjoint_in(diag_factor, diag_cot, inverse, adj, sym, hold):
    hold[...] = tri(dots(diag_factor[...].T, tri(diag_cot, 1.0)), 0.5)
    hold[...] = dots(inverse[...].T, hold[...])
    value = tri(dots(hold[...], inverse[...]), 0.5)
    adj[...] = value
    sym[...] = value + value.T


def adjoint0_kernel(
    flags, total, mate, cotangent, diag_factor, strip, inverse, next_inverse, adj, sym, cross, turned, hold
):
    hold[UPPER, :] = cotangent[UPPER, RIGHT] - total[:, RIGHT]
    hold[LOWER, :] = cotangent[LOWER, RIGHT] - mate[:, RIGHT]
    adjoint_in(diag_factor, hold[...], inverse, adj, sym, hold)
    hold[UPPER, :] = cotangent[UPPER, LEFT] - total[:, LEFT]
    hold[LOWER, :] = cotangent[LOWER, LEFT] - mate[:, LEFT]
    hold[...] = hold[...] - dots(sym[...], strip[...])
    value = dots(hold[...], next_inverse[...])
    cross[...] = value
    turned[...] = value.T


def adjoint1_kernel(flags, total, mate, cotangent, turned, strip, diag_factor, inverse, adj, sym, hold):
    hold[UPPER, :] = cotangent[UPPER, LEFT] - mate[:, LEFT]
    hold[LOWER, :] = cotangent[LOWER, LEFT] - total[:, LEFT]
    hold[...] = hold[...] - dots(turned[...], strip[...])
    adjoint_in(diag_factor, hold[...], inverse, adj, sym, hold)


def adjoint2_kernel(
    flags, upper, lower, total, mate, from2, from1, strip0, strip1, diag_factor, inverse, adj, packed, hold, sym
):
    hold[UPPER, :] = upper[:, RIGHT] - total[:, RIGHT]
    hold[LOWER, :] = lower[:, RIGHT] - mate[:, RIGHT]
    hold[...] = hold[...] - dots(from2[...].T, strip0[...])
    hold[...] = hold[...] - dots(from1[...].T, strip1[...])
    adjoint_in(diag_factor, hold[...], inverse, adj, sym, hold)
    packed[:, pl.ds(0, HALF)] = sym[UPPER, pl.ds(0, HALF)]
    packed[:, pl.ds(HALF, HALF)] = sym[LOWER, pl.ds(0, HALF)]
    packed[:, pl.ds(2 * HALF, HALF)] = sym[LOWER, pl.ds(HALF, HALF)]


def cross_kernel(flags, upper, lower, total, mate, inverse, left0, strip0, left1, strip1, out, hold):
    hold[UPPER, :] = upper[:, RIGHT]
    hold[LOWER, :] = lower[:, RIGHT]

    @pl.when(flags[ROW] == 1)
    def _():
        hold[UPPER, :] = hold[UPPER, :] - mate[:, RIGHT]
        hold[LOWER, :] = hold[LOWER, :] - total[:, RIGHT]

    value = hold[...] - dots(left0[...], strip0[...])
    value = value - dots(left1[...], strip1[...])
    out[...] = dots(value, inverse[...])


EARLY = (
    "now1", "now2", "now3", "now4", "now5", "own0", "own1", "own0_b", "own1_b", "own0_c", "own1_c",
    "from2", "from1", "over2", "over1",
)
LATE = (
    "now1", "now2", "now4", "now5", "now6", "late", "late_b", "late_c", "sym2", "sym_b", "sym_c",
    "adj0", "cross", "adj1", "adj2", "cotangent",
)


def start_kernel(flags, upper, lower, left0, left1, right0, right1, *refs):
    given = dict(zip(EARLY, refs[: len(EARLY)]))
    out, block, high, low, sems = refs[len(EARLY) :]
    step = pl.program_id(0)
    row, col = flags[ROW], flags[COL]
    blocks = {
        "solved": (("now4", "now5"), ("now3", "now4"), ("now2", "now3")),
        "strip": (("own0_c", "own1_c"), ("own0_b", "own1_b"), ("own0", "own1")),
        "foot": (("over2", "over1"), ("over2", "over1"), ("from2", "from1")),
    }
    kinds = {"solved": row >= NP, "strip": (row == 1) | (row == 2), "foot": row == 0}

    def fetch(kind, plane):
        copies = [
            pltpu.make_async_copy(given[name], block.at[k], sems.at[k])
            for k, name in enumerate(blocks[kind][plane])
        ]
        for copy in copies:
            copy.start()
        for copy in copies:
            copy.wait()
        for k in range(2):
            span = pl.ds(k * NB, NB)
            high[:, span], low[:, span] = split(block[k].T if kind == "foot" else block[k])

    @pl.when(step == 0)
    def _():
        for kind, holds in kinds.items():
            for plane in range(3):

                @pl.when(holds & (col == plane))
                def _(kind=kind, plane=plane):
                    fetch(kind, plane)

    def updated(strips):
        parts = [split(strip[...]) for strip in strips]
        for span, base in ((UPPER, upper), (LOWER, lower)):
            value = base[...]
            for k, part in enumerate(parts):
                left = (high[span, pl.ds(k * NB, NB)], low[span, pl.ds(k * NB, NB)])
                value = value - dot3(left, part)
            out[span, :] = value

    @pl.when((step < 2) & (col < 3))
    def _():
        updated((left0, left1))

    @pl.when((step >= 2) & (col < 2))
    def _():
        updated((right0, right1))


def finish_kernel(flags, started, total, mate, left2, right2, *refs):
    given = dict(zip(LATE, refs[: len(LATE)]))
    out, block, packed, high, low, sem, out_sem = refs[len(LATE) :]
    step = pl.program_id(0)
    row, col = flags[ROW], flags[COL]
    blocks = {
        "solved": ("now6", "now5", "now4"),
        "strip": ("late_c", "late_b", "late"),
        "foot": ("sym_c", "sym_b", "sym2"),
    }
    kinds = {"solved": row >= NP, "strip": (row == 1) | (row == 2), "foot": row == 0}

    def fetch(kind, name):
        copy = pltpu.make_async_copy(given[name], packed if kind == "foot" else block, sem)
        copy.start()
        copy.wait()
        if kind == "foot":
            block[UPPER, pl.ds(0, HALF)] = packed[:, pl.ds(0, HALF)]
            block[LOWER, pl.ds(0, HALF)] = packed[:, pl.ds(HALF, HALF)]
            block[UPPER, pl.ds(HALF, HALF)] = packed[:, pl.ds(HALF, HALF)].T
            block[LOWER, pl.ds(HALF, HALF)] = packed[:, pl.ds(2 * HALF, HALF)]
        high[...], low[...] = split(block[...])

    @pl.when(step == 0)
    def _():
        for kind, holds in kinds.items():
            for plane in range(3):

                @pl.when(holds & (col == plane))
                def _(kind=kind, plane=plane):
                    fetch(kind, blocks[kind][plane])

    def updated(strip):
        out[...] = started[...] - dot3((high[...], low[...]), split(strip[...]))

        @pl.when((row == 0) & (col == 0))
        def _():
            out[UPPER, :] = out[UPPER, :] - total[...]
            out[LOWER, :] = out[LOWER, :] - mate[...]

    def moved(name, offset):
        column = pl.multiple_of(lax.rem(step, 2) * HALF + offset, HALF)
        copy = pltpu.make_async_copy(given[name].at[:, pl.ds(column, HALF)], out, out_sem)
        copy.start()
        copy.wait()

    def take(holds, name, offset=0):
        @pl.when(holds)
        def _():
            moved(name, offset)

    @pl.when((step < 2) & (col == 3))
    def _():
        take(row >= NP, "now2")
        take(row == 2, "cross")
        take(row == 1, "adj1")
        take(row == 0, "cotangent")

    @pl.when((step >= 2) & (col == 3))
    def _():
        take(row >= NP, "now1")
        take(row == 2, "adj0")
        take(row < 2, "cotangent", NB)

    @pl.when((step >= 2) & (col == 2))
    def _():
        take(row >= NP, "now4")
        take(row == 0, "adj2")
        take((row == 1) | (row == 2), "late")

    @pl.when((step < 2) & (col < 3))
    def _():
        updated(left2)

    @pl.when((step >= 2) & (col < 2))
    def _():
        updated(right2)


LEFT_SPEC = pl.BlockSpec((NB, HALF), lambda j: (0, jnp.minimum(j, 1)))
RIGHT_SPEC = pl.BlockSpec((NB, HALF), lambda j: (0, jnp.maximum(j - 2, 0)))
WIDE_SPEC = pl.BlockSpec((HALF, HALF), lambda j: (0, j))
TALL_SPEC = pl.BlockSpec((NB, HALF), lambda j: (0, j))


def by_columns(kernel, name, flags, specs, ins, later, scratch):
    return pl.pallas_call(
        kernel,
        grid=(4,),
        out_shape=jax.ShapeDtypeStruct((NB, 2 * NB), jnp.float32),
        in_specs=[pl.BlockSpec(memory_space=pltpu.SMEM)]
        + specs
        + [pl.BlockSpec(memory_space=pl.ANY)] * len(later),
        out_specs=TALL_SPEC,
        scratch_shapes=scratch,
        compiler_params=pltpu.CompilerParams(vmem_limit_bytes=48 * 1024 * 1024),
        cost_estimate=pl.CostEstimate(flops=0, bytes_accessed=0, transcendentals=0),
        name=name,
    )(flags, *ins, *later)


def placed(grid, saved_factor, cotangent):
    row, col = grid.row, grid.col
    planes = range(4)
    below = row >= NP
    side = (row // 2) % 2 == 1
    parts = [grid.odd, side, below & (col == 3), below & (col == 2), row, col, col == 1]
    parts += [(row == 2) & (col == 3), ((row == 1) | (row == 2)) & (col == 2), (row == 0) & (col == 2)]
    parts += [below & (col <= 2), below & (col <= 1), below & ((col == 1) | (col == 2)), below & (col == 0)]
    parts += [col == 3, col == 2, below & (col >= 2), row < 4, (row == 1) & (col == 3), col >= 2]
    flags = jnp.stack([jnp.asarray(p).astype(jnp.int32) for p in parts])

    def core(value):
        return grid.within(value, [(r, r ^ 1) for r in range(8)], planes)

    def down(value, *sources, cut=False):
        if not cut:
            return grid.down(value, range(NP, 8), sources)
        upper, lower = value[:HALF], value[HALF:]
        upper = grid.down(upper, range(NP, 8), sources)
        upper, lower = fence(upper, lower)
        lower = grid.down(lower, range(NP, 8), sources)
        return jnp.concatenate([upper, lower], axis=0)

    def own_from(value, source, target):
        return grid.send(value, [((r, source), (r, target)) for r in (1, 2)])

    def moves(roots, pairs):
        return [((a ^ (root & ~1), c), (b ^ (root & ~1), c)) for c, root in roots.items() for a, b in pairs]

    def inward(value, roots):
        pairs = moves(roots, ((6, 4), (7, 3), (5, 1)))
        pairs += [((2, c), (0, c)) for c, root in roots.items() if root < 2]
        return value + grid.send(value, pairs)

    def home(value, roots):
        return value + grid.send(value, moves(roots, ((4, 0), (3, 1))))

    def settle(running, total, mate, roots):
        upper, lower = running
        chosen = functools.reduce(
            jnp.logical_or, [(col == c) & (row == root) for c, root in roots.items()]
        )
        upper = upper - jnp.where(chosen, jnp.where(grid.odd, mate, total), 0.0)
        lower = lower - jnp.where(chosen, jnp.where(grid.odd, total, mate), 0.0)
        return upper, lower

    def share(now, bit, before):
        keep, give = on_chip(
            share_kernel, [(HALF, 2 * NB)] * 2, flags, (now, saved_factor), [SQUARE], "share", bit, True
        )
        if before:
            now, keep, give = fence(now, keep, give)
        return now, keep + core(give)

    def inverted(matrix, bit):
        def kernel(flags, *refs):
            inverse_kernel(*refs)

        return on_chip(kernel, [SQUARE], flags, (matrix,), [(NB, TILE)] * 2, "invert", bit)

    def solve(kernel, bit, *ins):
        return on_chip(kernel, [SQUARE], flags, ins, (), "solve", bit, True)

    def fence(*values):
        return lax.optimization_barrier(values)

    factor = saved_factor

    mate = core(factor)
    early, later, third, fourth = on_chip(
        pick_kernel, [FLAT] * 4, flags, (factor, mate), name="pick", bit=NEAR
    )
    near = row < 4

    def away(mine):
        return grid.within(mine, [(r, r ^ 4) for r in range(4)], planes)

    def both(own):
        got = grid.within(own, [(r, r ^ 2) for r in range(8)], planes)
        return on_chip(
            assemble_kernel, [SQUARE] * 2, flags, (own, core(own), got, core(got)), name="assemble"
        )

    got_early = away(early)
    own_early = jnp.where(near, early, got_early)
    later, own_early = fence(later, own_early)
    got_later = away(later)
    strip0_right, diag1 = both(own_early)
    own_later = jnp.where(near, later, got_later)
    strip0_left, strip1_right = both(own_later)

    def tied(value, *others):
        return fence(value, *others)[0]

    inverse0 = inverted(strip0_right, TOP_ALL)
    now1 = solve(first_kernel, TOP, cotangent, inverse0)

    def spread_out(last):
        return jnp.where(near, last, grid.within(last, [(0, 4), (1, 5)], range(3)))

    def spread_on(own):
        got = grid.within(own, [(0, 2), (1, 3), (4, 6), (5, 7)], range(3))
        own = jnp.where(side, got, own)
        return on_chip(join_kernel, [SQUARE], flags, (own, core(own)), name="join")


    sums1, sums2, sums3 = {3: 2}, {3: 1, 2: 2}, {2: 1, 1: 2}
    sums4, sums5 = {2: 0, 1: 1, 0: 2}, {1: 0, 0: 1}
    to_foot = [((2, c), (0, c)) for c in range(3)]
    to_foot_core = [((1, c), (0, c)) for c in range(3)]
    now1_on, sum1 = share(now1, TOP, False)
    came1 = down(now1_on, 3, cut=False)
    inverse1 = inverted(diag1, HIGH_ALL)
    held_inverse1 = inverse1
    solved1 = solve(second_kernel, TOP, cotangent, inverse1, now1, strip0_left)
    held_solved1 = solved1
    sum1 = inward(tied(sum1, held_solved1), sums1)
    now2 = solved1 + came1
    held_now2 = now2

    own3 = spread_out(third)
    held_own3 = own3
    strip1_left = spread_on(own3)
    held_strip1_left = strip1_left
    own4 = spread_out(fourth)
    held_own4 = own4
    strip2_left = spread_on(own4)

    now2_on, sum2 = share(now2, UPTO, False)
    held_sum2_0 = sum2
    came2 = down(now2_on, 3, 2, cut=False)
    sum1 = home(tied(sum1, held_inverse1, held_sum2_0), sums1)
    mate1 = core(sum1)
    adj0, sym0, cross, turned = on_chip(
        adjoint0_kernel,
        [SQUARE] * 4,
        flags,
        (sum1, mate1, cotangent, strip0_right, strip0_left, inverse0, inverse1),
        [SQUARE],
        "adjoint",
        HEAD,
    )
    crossed = grid.send(turned, [((2, 3), (1, 3))])
    block0 = jnp.where(row == 1, crossed, sym0)
    own0 = own_from(block0, 3, 2)
    held_own0 = own0
    block0 = block0
    own0_b, own0_c = own_from(block0, 3, 1), own_from(block0, 3, 0)
    sum2 = inward(tied(sum2, held_own4), sums2)
    now3 = came2
    solved2 = solve(third_kernel, NEXT, cotangent, inverse1, now2, strip0_right, now3, strip1_right)
    held_solved2 = solved2


    now3_on, sum3 = share(now3, MID, False)
    came3 = down(now3_on, 2, 1, cut=False)
    sum2 = home(tied(sum2, held_own3, held_strip1_left), sums2)
    mate2 = core(sum2)
    adj1, sym1 = on_chip(
        adjoint1_kernel,
        [SQUARE] * 2,
        flags,
        (sum2, mate2, cotangent, crossed, strip0_left, diag1, inverse1),
        [SQUARE],
        "adjoint",
        HEAD1,
    )
    held_sym1 = sym1
    block1 = jnp.where(row == 1, sym1, cross)
    own1 = own_from(block1, 3, 2)
    block1 = block1
    own1_b, own1_c = own_from(block1, 3, 1), own_from(block1, 3, 0)
    held_own0_b = own0_b
    held_own0_c = own0_c
    held_own1_b = own1_b
    held_own1_c = own1_c
    chosen = (row == 2) & (col == 2)
    running = (
        cotangent[:HALF] - jnp.where(chosen, sum2, 0.0),
        cotangent[HALF:] - jnp.where(chosen, mate2, 0.0),
    )
    sum3 = inward(sum3, sums3)
    now4 = solved2 + came3


    now4_on, sum4 = share(now4, LOW, False)
    held_sum4_0 = sum4
    came4 = down(now4_on, 2, 1, cut=False)
    sum3 = home(tied(sum3, held_sym1, held_sum4_0), sums3)
    mate3 = core(sum3)
    late = on_chip(
        cross_kernel,
        [SQUARE],
        flags,
        (*running, sum3, mate3, inverse1, own0, strip0_right, own1, strip1_right),
        [SQUARE],
        "solve",
        CROSS,
        True,
    )
    held_late = late
    running = settle(running, sum3, mate3, sums3)
    from2, from1 = grid.send(late, to_foot), grid.send(late, to_foot_core)
    late_on = tied(late, held_solved2)
    late_b, late_c = own_from(late_on, 2, 1), own_from(late_on, 2, 0)
    held_late_b = late_b
    held_late_c = late_c
    sum4 = inward(tied(sum4, held_own0_c), sums4)
    now5 = came4

    now5_on, sum5 = share(now5, LOWEST, False)
    held_sum5_0 = sum5
    came5 = down(tied(now5_on, held_sum5_0, held_own0_b), 1, cut=False)
    sum4 = home(tied(sum4, held_late, held_own1_c), sums4)
    mate4 = core(sum4)
    adj2, sym2 = on_chip(
        adjoint2_kernel,
        [SQUARE, (HALF, 3 * HALF)],
        flags,
        (*running, sum4, mate4, from2, from1, strip0_right, strip1_right, diag1, inverse1),
        [SQUARE] * 2,
        "adjoint",
        FOOT,
    )
    running = settle(running, sum4, mate4, sums4)
    sym_b = grid.send(sym2, [((0, 2), (0, 1))])
    sym_c = grid.send(sym2, [((0, 2), (0, 0))])
    late_low = late_b + late_c
    over2, over1 = grid.send(late_low, to_foot), grid.send(late_low, to_foot_core)
    held_over1 = over1
    sum5 = inward(tied(sum5, held_now2), sums5)
    now6 = tied(came5, held_own0)

    _, sum6 = share(now6, LAST, True)
    sum5 = home(sum5, sums5)
    running = settle(running, sum5, core(sum5), sums5)
    here = locals()
    started = by_columns(
        start_kernel,
        "start",
        flags,
        [WIDE_SPEC] * 2 + [LEFT_SPEC] * 2 + [RIGHT_SPEC] * 2,
        (*running, strip0_left, strip1_left, strip0_right, strip1_right),
        [here[name] for name in EARLY],
        [
            pltpu.VMEM((2, NB, NB), jnp.float32),
            pltpu.VMEM((NB, 2 * NB), jnp.bfloat16),
            pltpu.VMEM((NB, 2 * NB), jnp.bfloat16),
            pltpu.SemaphoreType.DMA((2,)),
        ],
    )
    held_started = started
    sum6 = inward(sum6, sums5)
    sum6 = home(tied(sum6, held_late_b, held_late_c), sums5)
    sum6 = tied(sum6, held_own1_b, held_over1, held_started)
    return by_columns(
        finish_kernel,
        "finish",
        flags,
        [TALL_SPEC, WIDE_SPEC, WIDE_SPEC, LEFT_SPEC, RIGHT_SPEC],
        (started, sum6, core(sum6), strip2_left, diag1),
        [here[name] for name in LATE],
        [
            pltpu.VMEM(SQUARE, jnp.float32),
            pltpu.VMEM((HALF, 3 * HALF), jnp.float32),
            pltpu.VMEM(SQUARE, jnp.bfloat16),
            pltpu.VMEM(SQUARE, jnp.bfloat16),
            pltpu.SemaphoreType.DMA,
            pltpu.SemaphoreType.DMA,
        ],
    )


def shards(saved_factor, cotangent):
    grid = Grid()
    if grid.row_count == 8 and grid.col_count == 4:
        return placed(grid, saved_factor, cotangent)
    return general(grid, saved_factor, cotangent)


def solution(mesh):
    placed = (P("row", "col"), P("row", "col"))
    return jax.shard_map(
        shards, mesh=mesh, in_specs=placed, out_specs=P("row", "col"), check_vma=False
    )
```
